32 devices in a mesh: rep: 4 (over y, core), fsdp: 8 (over z, x).
Axes of the slice: x: 2, y: 2, z: 4, core: 2. Of those that a mesh axis runs over, the one named last changes fastest.
Arguments:
- patches: bfloat16 [384, 80, 768], P(('rep', 'fsdp')), may hold values from -6 to 6
- visible_count: int32 [384], P(('rep', 'fsdp')), may hold values from 20 to 78, as said below
- patch_index: int32 [384, 80], P(('rep', 'fsdp')), may hold values from 0 to 195, as said below
- prenorm_gain: bfloat16 [768], P('fsdp'), may hold values from 0.5 to 1.5
- prenorm_bias: bfloat16 [768], P('fsdp'), may hold values from -4 to 4
- heads_weight: bfloat16 [768, 2304], P('fsdp'), may hold values from -0.21875 to 0.21875
- heads_bias: bfloat16 [1536], P('fsdp'), may hold values from -4 to 4
- output_weight: bfloat16 [768, 768], P('fsdp'), may hold values from -0.625 to 0.625
- output_bias: bfloat16 [768], P('fsdp'), may hold values from -4 to 4
- midnorm_gain: bfloat16 [768], P('fsdp'), may hold values from 0.5 to 1.5
- midnorm_bias: bfloat16 [768], P('fsdp'), may hold values from -4 to 4
- expand_weight: bfloat16 [768, 3072], P('fsdp'), may hold values from -0.21875 to 0.21875
- expand_bias: bfloat16 [3072], P('fsdp'), may hold values from -4 to 4
- reduce_weight: bfloat16 [3072, 768], P('fsdp'), may hold values from -0.109375 to 0.109375
- reduce_bias: bfloat16 [768], P('fsdp'), may hold values from -4 to 4
- upstream: bfloat16 [384, 80, 768], P(('rep', 'fsdp')), may hold values from -6 to 6
Outputs:
- block_result_output: bfloat16 [384, 80, 768], P(('rep', 'fsdp'))
- patches_grad: bfloat16 [384, 80, 768], P(('rep', 'fsdp'))
- prenorm_gain_grad: float32 [768], P('fsdp')
- prenorm_bias_grad: float32 [768], P('fsdp')
- heads_weight_grad: float32 [768, 2304], P('fsdp')
- head_bias_gradient: float32 [1536], P('fsdp')
- output_weight_grad: float32 [768, 768], P('fsdp')
- output_bias_grad: float32 [768], P('fsdp')
- midnorm_gain_grad: float32 [768], P('fsdp')
- midnorm_bias_grad: float32 [768], P('fsdp')
- expand_weight_grad: float32 [768, 3072], P('fsdp')
- expand_bias_grad: float32 [3072], P('fsdp')
- reduce_weight_grad: float32 [3072, 768], P('fsdp')
- reduce_bias_grad: float32 [768], P('fsdp')
The draws below stay inside these ranges and needn't reach their ends.
Inputs may be any that keep to these rules, and one draw needn't show every extreme that they name: `visible_count`: visible patches of each image; slots from this count on are padding. `patch_index`: the slots of one image hold distinct patches.
All inputs are finite; a program needn't handle non-finite values.
Results may differ from the reference program's by a relative error of at most 0.013.
Values may be sent and summed in bfloat16 or wider, within the bound.
No kernel may reach another device: no remote copies, remote signals or barrier semaphores. Data moves between devices by JAX's collectives and lax.ppermute only.
A program may use at most 192 MiB of HBM per device.

```python
import jax
import jax.numpy as jnp
from jax import lax

D = 768
FF = 3072
HEADS = 12
HEAD_DIM = 64
SLOTS = 80
GRID = 14
MIN_VIS = 20
MAX_VIS = 78
PATCHES = 196
IMAGES = 384


def draw_visible_count(key, part):
    key = jax.random.fold_in(key, 11)
    counts = jax.random.randint(key, (IMAGES,), MIN_VIS, MAX_VIS + 1)
    places = jnp.arange(IMAGES, dtype=jnp.int32)
    counts = jnp.where(places == 0, MAX_VIS, counts)
    counts = jnp.where(places == 1, MIN_VIS, counts)
    return counts.astype(jnp.int32)


def draw_patch_index(key, part):
    key = jax.random.fold_in(key, 23)
    image_keys = jax.random.split(key, IMAGES)
    orders = jax.vmap(lambda single: jax.random.permutation(single, PATCHES))(image_keys)
    return orders[:, :SLOTS].astype(jnp.int32)


def strengthened(entries, own_key, source, target, parts, factor):
    def block_of(dim):
        return (jnp.arange(entries.shape[dim]) // (entries.shape[dim] // parts)).reshape((-1,) + (1,) * (entries.ndim - 1 - dim))

    first = jax.random.permutation(own_key, parts)[block_of(target)]
    second = (block_of(target) + parts // 2) % parts
    return jnp.where((block_of(source) == first) | (block_of(source) == second), factor * entries, entries)


def level_of(rng, dims, shards, smallest, high):
    def one(dim, blocks):
        heights = jax.random.uniform(jax.random.fold_in(jax.random.fold_in(rng, 6), dim), (blocks,), jnp.float32, smallest / len(shards), high / len(shards))
        return jnp.repeat(jnp.exp(heights), dims[dim] // blocks).reshape((-1,) + (1,) * (len(dims) - dim - 1))

    level = one(*shards[0])
    for cut in shards[1:]:
        level = level * one(*cut)
    return level


def noise(rng, extent, deviation, most, shards=(), held_as=jnp.bfloat16):
    level = level_of(rng, extent, shards, -0.22, 0.18) if shards else 1.0
    array = jax.random.normal(rng, extent, jnp.float32) * deviation * level
    return jnp.minimum(jnp.maximum(array, -most), most).astype(held_as)


def heavy_noise(own_key, dims, deviation, most, shards, heavy, kind=jnp.bfloat16):
    array = deviation * jax.random.normal(own_key, dims, jnp.float32)
    if shards:
        array = array * level_of(own_key, dims, shards, -0.22, 0.18)
    return jnp.clip(strengthened(array, jax.random.fold_in(own_key, 3), *heavy), -most, most).astype(kind)


def setup_inputs(seed: int = 0) -> dict:
    key_of = jax.random.split(jax.random.key(seed), 17)
    patches = heavy_noise(key_of[0], (IMAGES, SLOTS, D), 1.0, 6.0, ((0, 32),), (0, 2, 32, 2.75))
    visible_count = draw_visible_count(jax.random.fold_in(key_of[16], 71), 0)
    patch_index = draw_patch_index(jax.random.fold_in(key_of[16], 71), 0)
    prenorm_gain = jnp.clip(1.0 + 0.1 * jax.random.normal(key_of[3], (D,), jnp.float32), 0.5, 1.5).astype(jnp.bfloat16)
    prenorm_bias = noise(key_of[4], (D,), 0.3, 4.0, ((0, 8),))
    heads_weight = noise(key_of[5], (D, 3 * D), D ** -0.5, 0.21875, ((0, 8),))
    heads_bias = noise(key_of[6], (2 * D,), 0.3, 4.0, ((0, 8),))
    output_weight = noise(key_of[7], (D, D), (D // 8) ** -0.5, 0.625, ((0, 8),))
    output_bias = noise(key_of[8], (D,), 0.3, 4.0, ((0, 8),))
    midnorm_gain = jnp.clip(1.0 + 0.1 * jax.random.normal(key_of[9], (D,), jnp.float32), 0.5, 1.5).astype(jnp.bfloat16)
    midnorm_bias = noise(key_of[10], (D,), 0.3, 4.0, ((0, 8),))
    expand_weight = noise(key_of[11], (D, FF), D ** -0.5, 0.21875, ((0, 8),))
    expand_bias = noise(key_of[12], (FF,), 0.3, 4.0, ((0, 8),))
    reduce_weight = noise(key_of[13], (FF, D), FF ** -0.5, 0.109375, ((0, 8),))
    reduce_bias = noise(key_of[14], (D,), 0.3, 4.0, ((0, 8),))
    upstream = noise(key_of[15], (IMAGES, SLOTS, D), 1.0, 6.0, ((0, 32),))
    return {"patches": patches, "visible_count": visible_count, "patch_index": patch_index, "prenorm_gain": prenorm_gain, "prenorm_bias": prenorm_bias, "heads_weight": heads_weight, "heads_bias": heads_bias, "output_weight": output_weight, "output_bias": output_bias, "midnorm_gain": midnorm_gain, "midnorm_bias": midnorm_bias, "expand_weight": expand_weight, "expand_bias": expand_bias, "reduce_weight": reduce_weight, "reduce_bias": reduce_bias, "upstream": upstream}


@jax.custom_vjp
def low(v):
    return lax.optimization_barrier(v.astype(jnp.bfloat16)).astype(jnp.float32)

@jax.custom_vjp
def low_back(v):
    return v

def low_keep(v):
    return (low(v), None)

def low_pass(kept, grad):
    return (grad,)

def back_keep(v):
    return (v, None)

def back_low(kept, grad):
    return (low(grad),)
low.defvjp(low_keep, low_pass)
low_back.defvjp(back_keep, back_low)
epsilon = 1e-06
masked_score = -1e+30
precise = lax.Precision.HIGHEST

def position_table(patch_ids):
    quarter = D // 4
    frequency = 1.0 / 10000.0 ** (jnp.arange(quarter, dtype=jnp.float32) / quarter)
    row_place = (patch_ids // GRID).astype(jnp.float32)[..., None] * frequency
    col_place = (patch_ids % GRID).astype(jnp.float32)[..., None] * frequency
    return jnp.concatenate([jnp.sin(row_place), jnp.cos(row_place), jnp.sin(col_place), jnp.cos(col_place)], axis=-1)

def layer_norm(values, norm_gain, norm_shift):
    center = values - lax.optimization_barrier(jnp.mean(values, axis=-1, keepdims=True))
    spread = lax.optimization_barrier(jnp.mean(center * center, axis=-1, keepdims=True))
    return center * lax.rsqrt(spread + epsilon) * norm_gain + norm_shift

def forward(inputs, key_padding_mask, position, prenorm_gain, prenorm_bias, heads_weight, heads_bias, output_weight, output_bias, midnorm_gain, midnorm_bias, expand_weight, expand_bias, reduce_weight, reduce_bias):
    count_img = inputs.shape[0]
    start = (inputs + position).reshape(-1, D)
    first = low(layer_norm(start, prenorm_gain, prenorm_bias))
    bias_full = jnp.concatenate([heads_bias[:D], jnp.zeros((D,), jnp.float32), heads_bias[D:]])
    projected = jnp.dot(first, heads_weight, precision=precise) + bias_full
    projected = low_back(low(projected)).reshape(count_img, SLOTS, 3, HEADS, HEAD_DIM)
    queries = projected[:, :, 0]
    keys_all = projected[:, :, 1]
    values_all = projected[:, :, 2]
    scores = jnp.einsum('bqhd,bkhd->bhqk', queries, keys_all, precision=precise) * HEAD_DIM ** (-0.5)
    scores = low_back(scores)
    scores = jnp.where(key_padding_mask[:, None, None, :], scores, masked_score)
    attend = low(jax.nn.softmax(scores, axis=-1))
    mixed = jnp.einsum('bhqk,bkhd->bqhd', attend, values_all, precision=precise)
    mixed = low_back(low(mixed)).reshape(-1, D)
    branch = low_back(jnp.dot(mixed, output_weight, precision=precise) + output_bias)
    middle = start + branch
    second = low(layer_norm(middle, midnorm_gain, midnorm_bias))
    hidden = low_back(jnp.dot(second, expand_weight, precision=precise) + expand_bias)
    active = low(jax.nn.gelu(hidden, approximate=False))
    result = middle + jnp.dot(active, reduce_weight, precision=precise) + reduce_bias
    return result.reshape(count_img, SLOTS, D)

def reference(patches, visible_count, patch_index, prenorm_gain, prenorm_bias, heads_weight, heads_bias, output_weight, output_bias, midnorm_gain, midnorm_bias, expand_weight, expand_bias, reduce_weight, reduce_bias, upstream):
    params = tuple((weight.astype(jnp.float32) for weight in (prenorm_gain, prenorm_bias, heads_weight, heads_bias, output_weight, output_bias, midnorm_gain, midnorm_bias, expand_weight, expand_bias, reduce_weight, reduce_bias)))
    per_group = max((divisor for divisor in range(1, 52) if IMAGES % divisor == 0))
    groups = IMAGES // per_group

    def one_group(totals, pieces):
        inputs, counts, patch_ids, arriving = pieces
        slot_index_list = jnp.arange(SLOTS, dtype=jnp.int32)
        key_padding_mask = slot_index_list[None, :] < counts[:, None]
        position = position_table(patch_ids)

        def apply(inputs_f32, *weights):
            return forward(inputs_f32, key_padding_mask, position, *weights)
        result, pullback = jax.vjp(apply, inputs.astype(jnp.float32), *params)
        cotangent = arriving.astype(jnp.float32) * key_padding_mask[:, :, None].astype(jnp.float32)
        grads = pullback(cotangent)
        totals = tuple((total + grad for total, grad in zip(totals, grads[1:])))
        return (totals, (result.astype(jnp.bfloat16), grads[0].astype(jnp.bfloat16)))
    initial = tuple((jnp.zeros(weight.shape, jnp.float32) for weight in params))
    stacked = (patches.reshape(groups, per_group, SLOTS, D), visible_count.reshape(groups, per_group), patch_index.reshape(groups, per_group, SLOTS), upstream.reshape(groups, per_group, SLOTS, D))
    totals, (outputs, input_grads) = lax.scan(one_group, initial, stacked)
    block_result_output = outputs.reshape(IMAGES, SLOTS, D)
    patches_grad = input_grads.reshape(IMAGES, SLOTS, D)
    return (block_result_output, patches_grad, totals[0], totals[1], totals[2], totals[3], totals[4], totals[5], totals[6], totals[7], totals[8], totals[9], totals[10], totals[11])
```

```python
import functools

import numpy as np
import jax
import jax.numpy as jnp
from jax import lax
from jax.experimental import pallas as pl
from jax.experimental.pallas import tpu as pltpu
from jax.sharding import PartitionSpec as P

D = 768
FF = 3072
HEADS = 12
HEAD_DIM = 64
SLOTS = 80
GRID = 14
NF = 8
RB = D // NF
FB = FF // NF
CH = 3
CW = FF // CH
LANE = 128
HB = 3 * D // LANE
OB = D // LANE
EB = CW // LANE
QH = HB * RB // 4
QO = OB * RB // 4
QM = (EB * RB + OB * LANE) // 4
SM = 16

EPS = 1e-06
NEG = -1e30
bf16 = jnp.bfloat16
f32 = jnp.float32
NN = (((1,), (0,)), ((), ()))
NT = (((1,), (1,)), ((), ()))
TN = (((0,), (0,)), ((), ()))
VMEM_LIMIT = 60 << 20


def mm(a, b, dims):
    return lax.dot_general(a, b, dims, preferred_element_type=f32)


def params(limit=VMEM_LIMIT):
    return pltpu.CompilerParams(vmem_limit_bytes=limit)


def whole(shape):
    return pl.BlockSpec(shape, lambda *_: (0,) * len(shape))


ANY = pl.BlockSpec(memory_space=pl.ANY)
SMEM = pl.BlockSpec(memory_space=pltpu.SMEM)


def block_of(w, base, quarter, start, n):
    q, off = divmod(start, quarter)
    if off + n <= quarter:
        return w[q, :, base + off : base + off + n, :].reshape(NF * n, LANE)
    head = quarter - off
    return jnp.concatenate(
        [w[q, :, base + off : base + quarter, :], w[q + 1, :, base : base + n - head, :]], axis=1
    ).reshape(NF * n, LANE)


def put_block(w, base, quarter, start, n, value):
    value = value.reshape(NF, n, LANE)
    q, off = divmod(start, quarter)
    if off + n <= quarter:
        w[q, :, base + off : base + off + n, :] = value
    else:
        head = quarter - off
        w[q, :, base + off : base + quarter, :] = value[:, :head]
        w[q + 1, :, base : base + n - head, :] = value[:, head:]


def columns(w, base, quarter, rows, blocks):
    return jnp.concatenate([block_of(w, base, quarter, b * rows, rows) for b in blocks], axis=1)


def put_columns(w, base, quarter, rows, blocks, value):
    for i, b in enumerate(blocks):
        put_block(w, base, quarter, b * rows, rows, value[:, i * LANE : (i + 1) * LANE])


def piece_copies(bufs, layout, idx, w, sems):
    rows = w.shape[2]
    return [
        pltpu.make_async_copy(bufs[b].at[:, pl.ds(off, rows)], w.at[idx[n]], sems.at[n])
        for n, (b, off) in enumerate(layout)
    ]


def frequency_table():
    quarter = D // 4
    frequency = 1.0 / 10000.0 ** (jnp.arange(quarter, dtype=f32) / quarter)
    angle = jnp.arange(16, dtype=f32)[:, None] * frequency
    table = jnp.concatenate([jnp.sin(angle), jnp.cos(angle)], axis=-1)
    high = table.astype(bf16)
    rest = table - high.astype(f32)
    middle = rest.astype(bf16)
    low = (rest - middle.astype(f32)).astype(bf16)
    return jnp.concatenate([high, middle, low], axis=0)


def normalised(v):
    c = v - jnp.mean(v, axis=-1, keepdims=True)
    r = lax.rsqrt(jnp.mean(c * c, axis=-1, keepdims=True) + EPS)
    return c * r, r


def norm_back(xhat, r, gain, d):
    e = gain * d
    return r * (
        e - jnp.mean(e, axis=-1, keepdims=True) - xhat * jnp.mean(e * xhat, axis=-1, keepdims=True)
    )


def start_kernel(G, cnt, table, ids, patches, upstream, start, xhat, seed, seed_sum):
    step = pl.program_id(0)

    @pl.when(step == 0)
    def _():
        seed_sum[...] = jnp.zeros_like(seed_sum)

    tab = table[...]
    place = lax.broadcasted_iota(jnp.int32, (48, SLOTS), 0) % 16
    row = lax.broadcasted_iota(jnp.int32, (SLOTS, D), 0)
    total = jnp.zeros((SLOTS, D), f32)
    for g in range(G):
        pid = ids[g]
        by_row = jnp.where(place == pid // GRID, 1.0, 0.0).astype(bf16)
        by_col = jnp.where(place == pid % GRID, 1.0, 0.0).astype(bf16)
        position = jnp.concatenate([mm(by_row, tab, TN), mm(by_col, tab, TN)], axis=1)
        v = patches[g].astype(f32) + position
        here = pl.ds(g * SLOTS, SLOTS)
        start[here, :] = v
        xhat[here, :] = normalised(v)[0]
        s = jnp.where(row < cnt[step * G + g], upstream[g].astype(f32), 0.0)
        seed[here, :] = s.astype(bf16)
        total += s
    seed_sum[...] += jnp.sum(total, axis=0, keepdims=True)


def start_call(counts, table, ids, patches, upstream):
    n = patches.shape[0]
    G = 4 if n % 4 == 0 else 1
    rows = n * SLOTS
    blk = pl.BlockSpec((G * SLOTS, D), lambda i: (i, 0))
    img = pl.BlockSpec((G, SLOTS, D), lambda i: (i, 0, 0))
    return pl.pallas_call(
        functools.partial(start_kernel, G),
        grid=(n // G,),
        in_specs=[SMEM, whole(table.shape), pl.BlockSpec((G, 1, SLOTS), lambda i: (i, 0, 0)), img, img],
        out_specs=[blk, blk, blk, whole((1, D))],
        out_shape=[
            jax.ShapeDtypeStruct((rows, D), f32),
            jax.ShapeDtypeStruct((rows, D), f32),
            jax.ShapeDtypeStruct((rows, D), bf16),
            jax.ShapeDtypeStruct((1, D), f32),
        ],
        compiler_params=params(),
        cost_estimate=pl.CostEstimate(flops=1 << 26, bytes_accessed=rows * D * 14, transcendentals=rows),
        name="start",
    )(counts, table, ids, patches, upstream)


def head_masks():
    lane = lax.broadcasted_iota(jnp.int32, (SLOTS, LANE), 1)
    return lane < HEAD_DIM


def both_heads(x, left):
    zero = jnp.zeros_like(x)
    return jnp.concatenate([jnp.where(left, x, zero), jnp.where(left, zero, x)], axis=0)


def attend_kernel(G, layout, nbuf, cnt, idx, xhat, par, *rest):
    bufs = rest[:nbuf]
    first, qkv, probs, mixed, w, sems = rest[nbuf:]
    step = pl.program_id(0)

    @pl.when(step == 0)
    def _():
        copies = piece_copies(bufs, layout, idx, w, sems)
        for c in copies:
            c.start()
        for c in copies:
            c.wait()

    x = (xhat[...] * par[0:1, :D] + par[1:2, :D]).astype(bf16)
    first[...] = x
    for part in range(3):
        cols = slice(part * D, (part + 1) * D)
        wp = columns(w, 0, QH, RB, range(part * OB, (part + 1) * OB))
        qkv[:, cols] = (mm(x, wp, NN) + par[2:3, cols]).astype(bf16)
    left = head_masks()
    key = lax.broadcasted_iota(jnp.int32, (SLOTS, SLOTS), 0)

    @pl.loop(0, G)
    def _(g):
        live = key < cnt[step * G + g]
        rows = pl.ds(pl.multiple_of(g * SLOTS, SLOTS), SLOTS)
        for p in range(HEADS // 2):
            c = p * LANE
            q = qkv[rows, c : c + LANE]
            k = qkv[rows, D + c : D + c + LANE]
            v = qkv[rows, 2 * D + c : 2 * D + c + LANE]
            s = mm(both_heads(k, left), q, NT) * HEAD_DIM**-0.5
            halves = []
            for h in range(2):
                sh = jnp.where(live, s[h * SLOTS : (h + 1) * SLOTS], NEG)
                e = jnp.exp(sh - jnp.max(sh, axis=0, keepdims=True))
                halves.append(e / jnp.sum(e, axis=0, keepdims=True))
            pt = jnp.concatenate(halves, axis=0).astype(bf16)
            probs[g, p] = pt
            mixed[rows, c : c + LANE] = mm(pt, both_heads(v, left), TN).astype(bf16)


def attend_call(counts, w, xhat, par, G=4):
    idx, bufs, layout = w
    rows = xhat.shape[0]
    n = rows // SLOTS
    G = G if n % G == 0 else 1

    def blk(width):
        return pl.BlockSpec((G * SLOTS, width), lambda i: (i, 0))

    return pl.pallas_call(
        functools.partial(attend_kernel, G, layout, len(bufs)),
        grid=(n // G,),
        in_specs=[SMEM, SMEM, blk(D), whole(par.shape)] + [ANY] * len(bufs),
        out_specs=[
            blk(D),
            blk(3 * D),
            pl.BlockSpec((G, HEADS // 2, 2 * SLOTS, SLOTS), lambda i: (i, 0, 0, 0)),
            blk(D),
        ],
        out_shape=[
            jax.ShapeDtypeStruct((rows, D), bf16),
            jax.ShapeDtypeStruct((rows, 3 * D), bf16),
            jax.ShapeDtypeStruct((n, HEADS // 2, 2 * SLOTS, SLOTS), bf16),
            jax.ShapeDtypeStruct((rows, D), bf16),
        ],
        scratch_shapes=[
            pltpu.VMEM((4, NF, QH, LANE), bf16),
            pltpu.SemaphoreType.DMA((len(layout),)),
        ],
        compiler_params=params(),
        cost_estimate=pl.CostEstimate(
            flops=2 * rows * D * 3 * D * 4, bytes_accessed=20 << 20, transcendentals=n * HEADS * 6400
        ),
        name="attend",
    )(counts, idx, xhat, par, *bufs)


def middle_kernel(layout, nbuf, idx, mixed, start, par, *rest):
    bufs = rest[:nbuf]
    middle, second, w, sems = rest[nbuf:]

    @pl.when(pl.program_id(0) == 0)
    def _():
        copies = piece_copies(bufs, layout, idx, w, sems)
        for c in copies:
            c.start()
        for c in copies:
            c.wait()

    m = start[...] + mm(mixed[...], columns(w, 0, QO, RB, range(OB)), NN) + par[3:4, :D]
    middle[...] = m
    second[...] = (normalised(m)[0] * par[4:5, :D] + par[5:6, :D]).astype(bf16)


def row_block(rows):
    return 240 if rows % 240 == 0 else SLOTS


def middle_call(w, mixed, start, par):
    idx, bufs, layout = w
    rows = mixed.shape[0]
    B = row_block(rows)
    blk = pl.BlockSpec((B, D), lambda i: (i, 0))
    return pl.pallas_call(
        functools.partial(middle_kernel, layout, len(bufs)),
        grid=(rows // B,),
        in_specs=[SMEM, blk, blk, whole(par.shape)] + [ANY] * len(bufs),
        out_specs=[blk, blk],
        out_shape=[jax.ShapeDtypeStruct((rows, D), f32), jax.ShapeDtypeStruct((rows, D), bf16)],
        scratch_shapes=[
            pltpu.VMEM((4, NF, QO, LANE), bf16),
            pltpu.SemaphoreType.DMA((len(layout),)),
        ],
        compiler_params=params(),
        cost_estimate=pl.CostEstimate(flops=2 * rows * D * D, bytes_accessed=rows * D * 12, transcendentals=rows),
        name="middle",
    )(idx, mixed, start, par, *bufs)


def gelu_and_slope(h):
    a = jnp.abs(h)
    e = jnp.exp(-0.5 * (h * h))
    t = 1.0 / (1.0 + 0.23164189 * a)
    poly = t * (
        0.127414796
        + t * (-0.142248368 + t * (0.7107068705 + t * (-0.7265760135 + t * 0.5307027145)))
    )
    tail = poly * e
    phi = jnp.where(h >= 0, 1.0 - tail, tail)
    return h * phi, phi + h * e * 0.3989422804014327


def mlp_kernel(chunk, layout, nbuf, fresh, last, widx, oidx, second, seed, res_in, dsec_in, par, *rest):
    bufs = rest[:nbuf]
    res, dsec, hsum = rest[nbuf : nbuf + 3]
    outs = rest[nbuf + 3 : nbuf + 7]
    w, ge, gr, stage, sems, osems = rest[nbuf + 7 :]
    step = pl.program_id(0)
    steps = pl.num_programs(0)

    @pl.when(step == 0)
    def _():
        copies = piece_copies(bufs, layout, widx, w, sems)
        for c in copies:
            c.start()
        ge[...] = jnp.zeros_like(ge)
        gr[...] = jnp.zeros_like(gr)
        hsum[...] = jnp.zeros_like(hsum)
        for c in copies:
            c.wait()

    x = second[...]
    s = seed[...]
    half = EB // 2
    acc = res_in[...]
    dacc = None if fresh else dsec_in[...]
    if fresh:
        acc = acc + par[7:8, :D]
    for t in range(2):
        blocks = range(t * half, (t + 1) * half)
        we = columns(w, 0, QM, RB, blocks)
        fs = slice(t * half, (t + 1) * half)
        wr = jnp.concatenate(
            [w[2 + b // 3, fs, (b % 3) * LANE : (b % 3 + 1) * LANE, :].reshape(half * LANE, LANE) for b in range(OB)],
            axis=1,
        )
        cols = slice(t * half * LANE, (t + 1) * half * LANE)
        h = mm(x, we, NN) + par[8 + chunk : 9 + chunk, cols]
        active, slope = gelu_and_slope(h)
        a = active.astype(bf16)
        dh = (mm(s, wr, NT) * slope)
        d = dh.astype(bf16)
        hsum[0:1, cols] += jnp.sum(d.astype(f32), axis=0, keepdims=True)
        acc = acc + mm(a, wr, NN)
        g = mm(d, we, NT)
        dacc = g if dacc is None else dacc + g
        ge[:, cols] += mm(x, d, TN)
        gr[cols, :] += mm(a, s, TN)
    res[...] = acc.astype(res.dtype)
    dsec[...] = dacc

    @pl.when(step == steps - 1)
    def _():
        for b in range(EB):
            stage[b // 4, :, (b % 4) * RB : (b % 4 + 1) * RB, :] = (
                ge[:, b * LANE : (b + 1) * LANE].astype(bf16).reshape(NF, RB, LANE)
            )
        for b in range(OB):
            stage[2 + b // 3, :, (b % 3) * LANE : (b % 3 + 1) * LANE, :] = (
                gr[:, b * LANE : (b + 1) * LANE].astype(bf16).reshape(NF, LANE, LANE)
            )
        copies = [
            pltpu.make_async_copy(stage.at[oidx[n]], o, osems.at[n]) for n, o in enumerate(outs)
        ]
        for c in copies:
            c.start()
        for c in copies:
            c.wait()


def mlp_call(chunk, w, oidx, second, seed, res_in, dsec_in, par):
    widx, bufs, layout = w
    rows = second.shape[0]
    B = row_block(rows)
    fresh, last = chunk == 0, chunk == CH - 1
    blk = pl.BlockSpec((B, D), lambda i: (i, 0))
    dspec = blk if not fresh else ANY
    piece = jax.ShapeDtypeStruct((NF, QM, LANE), bf16)
    return pl.pallas_call(
        functools.partial(mlp_kernel, chunk, layout, len(bufs), fresh, last),
        grid=(rows // B,),
        in_specs=[SMEM, SMEM, blk, blk, blk, dspec, whole(par.shape)] + [ANY] * len(bufs),
        out_specs=[blk, blk, whole((1, CW))] + [ANY] * 4,
        out_shape=[
            jax.ShapeDtypeStruct((rows, D), bf16 if last else f32),
            jax.ShapeDtypeStruct((rows, D), f32),
            jax.ShapeDtypeStruct((1, CW), f32),
        ]
        + [piece] * 4,
        scratch_shapes=[
            pltpu.VMEM((4, NF, QM, LANE), bf16),
            pltpu.VMEM((D, CW), f32),
            pltpu.VMEM((CW, D), f32),
            pltpu.VMEM((4, NF, QM, LANE), bf16),
            pltpu.SemaphoreType.DMA((len(layout),)),
            pltpu.SemaphoreType.DMA((4,)),
        ],
        compiler_params=params(),
        cost_estimate=pl.CostEstimate(
            flops=12 * rows * D * CW, bytes_accessed=rows * D * 20, transcendentals=rows * CW
        ),
        name="mlp",
    )(widx, oidx, second, seed, res_in, dsec_in, par, *bufs)


def branch_kernel(layout, nbuf, idx, oidx, middle, dsec, seed, mixed, par, *rest):
    bufs = rest[:nbuf]
    dmid, dmixed, sums = rest[nbuf : nbuf + 3]
    outs = rest[nbuf + 3 : nbuf + 7]
    w, acc, stage, sems, osems = rest[nbuf + 7 :]
    step = pl.program_id(0)

    @pl.when(step == 0)
    def _():
        copies = piece_copies(bufs, layout, idx, w, sems)
        for c in copies:
            c.start()
        acc[...] = jnp.zeros_like(acc)
        sums[...] = jnp.zeros_like(sums)
        for c in copies:
            c.wait()

    d = dsec[...]
    xhat, r = normalised(middle[...])
    dm = seed[...].astype(f32) + norm_back(xhat, r, par[4:5, :D], d)
    dmid[...] = dm
    db = dm.astype(bf16)
    sums[0:1, :] += jnp.sum(d * xhat, axis=0, keepdims=True)
    sums[1:2, :] += jnp.sum(d, axis=0, keepdims=True)
    sums[2:3, :] += jnp.sum(db.astype(f32), axis=0, keepdims=True)
    acc[...] += mm(mixed[...], db, TN)
    dmixed[...] = mm(db, columns(w, 0, QO, RB, range(OB)), NT).astype(bf16)

    @pl.when(step == pl.num_programs(0) - 1)
    def _():
        put_columns(stage, 0, QO, RB, range(OB), acc[...].astype(bf16))
        copies = [
            pltpu.make_async_copy(stage.at[oidx[n]], o, osems.at[n]) for n, o in enumerate(outs)
        ]
        for c in copies:
            c.start()
        for c in copies:
            c.wait()


def branch_call(w, oidx, middle, dsec, seed, mixed, par):
    idx, bufs, layout = w
    rows = mixed.shape[0]
    B = row_block(rows)
    blk = pl.BlockSpec((B, D), lambda i: (i, 0))
    return pl.pallas_call(
        functools.partial(branch_kernel, layout, len(bufs)),
        grid=(rows // B,),
        in_specs=[SMEM, SMEM, blk, blk, blk, blk, whole(par.shape)] + [ANY] * len(bufs),
        out_specs=[blk, blk, whole((8, D))] + [ANY] * 4,
        out_shape=[
            jax.ShapeDtypeStruct((rows, D), f32),
            jax.ShapeDtypeStruct((rows, D), bf16),
            jax.ShapeDtypeStruct((8, D), f32),
        ]
        + [jax.ShapeDtypeStruct((NF, QO, LANE), bf16)] * 4,
        scratch_shapes=[
            pltpu.VMEM((4, NF, QO, LANE), bf16),
            pltpu.VMEM((D, D), f32),
            pltpu.VMEM((4, NF, QO, LANE), bf16),
            pltpu.SemaphoreType.DMA((len(layout),)),
            pltpu.SemaphoreType.DMA((4,)),
        ],
        compiler_params=params(),
        cost_estimate=pl.CostEstimate(flops=4 * rows * D * D, bytes_accessed=rows * D * 20, transcendentals=rows),
        name="branch",
    )(idx, oidx, middle, dsec, seed, mixed, par, *bufs)


def attend_back_kernel(G, oidx, qkv, probs, dmixed, first, *rest):
    dproj, sums = rest[:2]
    outs = rest[2:6]
    acc, stage, osems = rest[6:]
    step = pl.program_id(0)

    @pl.when(step == 0)
    def _():
        acc[...] = jnp.zeros_like(acc)
        sums[...] = jnp.zeros_like(sums)

    left = head_masks()
    scale = HEAD_DIM**-0.5

    @pl.loop(0, G)
    def _(g):
        rows = pl.ds(pl.multiple_of(g * SLOTS, SLOTS), SLOTS)
        for p in range(HEADS // 2):
            c = p * LANE
            q = qkv[rows, c : c + LANE]
            k = qkv[rows, D + c : D + c + LANE]
            v = qkv[rows, 2 * D + c : 2 * D + c + LANE]
            do = dmixed[rows, c : c + LANE]
            pt = probs[g, p]
            dv2 = mm(pt, do, NN)
            dv = jnp.where(left, dv2[:SLOTS], dv2[SLOTS:])
            dp = mm(both_heads(v, left), do, NT)
            prob = pt.astype(f32)
            parts = []
            for h in range(2):
                ph = prob[h * SLOTS : (h + 1) * SLOTS]
                dh = dp[h * SLOTS : (h + 1) * SLOTS]
                parts.append(ph * (dh - jnp.sum(ph * dh, axis=0, keepdims=True)))
            ds = jnp.concatenate(parts, axis=0).astype(bf16)
            dk2 = mm(ds, q, NN)
            dk = jnp.where(left, dk2[:SLOTS], dk2[SLOTS:]) * scale
            dq = mm(ds, both_heads(k, left), TN) * scale
            dproj[rows, c : c + LANE] = dq.astype(bf16)
            dproj[rows, D + c : D + c + LANE] = dk.astype(bf16)
            dproj[rows, 2 * D + c : 2 * D + c + LANE] = dv.astype(bf16)

    dall = dproj[...]
    sums[0:1, :] += jnp.sum(dall.astype(f32), axis=0, keepdims=True)
    x = first[...]
    for part in range(3):
        cols = slice(part * D, (part + 1) * D)
        acc[:, cols] += mm(x, dall[:, cols], TN)

    @pl.when(step == pl.num_programs(0) - 1)
    def _():
        put_columns(stage, 0, QH, RB, range(HB), acc[...].astype(bf16))
        copies = [
            pltpu.make_async_copy(stage.at[oidx[n]], o, osems.at[n]) for n, o in enumerate(outs)
        ]
        for c in copies:
            c.start()
        for c in copies:
            c.wait()


def attend_back_call(oidx, qkv, probs, dmixed, first, G=4):
    rows = first.shape[0]
    n = rows // SLOTS
    G = G if n % G == 0 else 1
    piece = jax.ShapeDtypeStruct((NF, QH, LANE), bf16)

    def blk(width):
        return pl.BlockSpec((G * SLOTS, width), lambda i: (i, 0))

    return pl.pallas_call(
        functools.partial(attend_back_kernel, G),
        grid=(n // G,),
        in_specs=[
            SMEM,
            blk(3 * D),
            pl.BlockSpec((G, HEADS // 2, 2 * SLOTS, SLOTS), lambda i: (i, 0, 0, 0)),
            blk(D),
            blk(D),
        ],
        out_specs=[blk(3 * D), whole((8, 3 * D))] + [ANY] * 4,
        out_shape=[jax.ShapeDtypeStruct((rows, 3 * D), bf16), jax.ShapeDtypeStruct((8, 3 * D), f32)]
        + [piece] * 4,
        scratch_shapes=[
            pltpu.VMEM((D, 3 * D), f32),
            pltpu.VMEM((4, NF, QH, LANE), bf16),
            pltpu.SemaphoreType.DMA((4,)),
        ],
        compiler_params=params(),
        cost_estimate=pl.CostEstimate(
            flops=2 * rows * D * 3 * D * 5, bytes_accessed=20 << 20, transcendentals=0
        ),
        name="attend_back",
    )(oidx, qkv, probs, dmixed, first)


def input_kernel(layout, nbuf, idx, dproj, start, dmid, par, *rest):
    bufs = rest[:nbuf]
    out, sums, w, sems = rest[nbuf:]

    @pl.when(pl.program_id(0) == 0)
    def _():
        copies = piece_copies(bufs, layout, idx, w, sems)
        for c in copies:
            c.start()
        sums[...] = jnp.zeros_like(sums)
        for c in copies:
            c.wait()

    d = None
    for part in range(3):
        wp = columns(w, 0, QH, RB, range(part * OB, (part + 1) * OB))
        t = mm(dproj[:, part * D : (part + 1) * D], wp, NT)
        d = t if d is None else d + t
    xhat, r = normalised(start[...])
    sums[0:1, :] += jnp.sum(d * xhat, axis=0, keepdims=True)
    sums[1:2, :] += jnp.sum(d, axis=0, keepdims=True)
    out[...] = (dmid[...] + norm_back(xhat, r, par[0:1, :D], d)).astype(bf16)


def input_call(w, dproj, start, dmid, par):
    idx, bufs, layout = w
    rows = start.shape[0]
    B = row_block(rows)
    blk = pl.BlockSpec((B, D), lambda i: (i, 0))
    return pl.pallas_call(
        functools.partial(input_kernel, layout, len(bufs)),
        grid=(rows // B,),
        in_specs=[SMEM, pl.BlockSpec((B, 3 * D), lambda i: (i, 0)), blk, blk, whole(par.shape)]
        + [ANY] * len(bufs),
        out_specs=[blk, whole((8, D))],
        out_shape=[jax.ShapeDtypeStruct((rows, D), bf16), jax.ShapeDtypeStruct((8, D), f32)],
        scratch_shapes=[
            pltpu.VMEM((4, NF, QH, LANE), bf16),
            pltpu.SemaphoreType.DMA((len(layout),)),
        ],
        compiler_params=params(),
        cost_estimate=pl.CostEstimate(
            flops=2 * rows * D * 3 * D, bytes_accessed=rows * D * 16, transcendentals=rows
        ),
        name="input_back",
    )(idx, dproj, start, dmid, par, *bufs)


def block_major(a):
    return a.reshape(a.shape[0], -1, LANE).transpose(1, 0, 2).reshape(-1, LANE)


def from_block_major(a, rows):
    return a.reshape(-1, rows, LANE).transpose(1, 0, 2).reshape(rows, -1)


def small_rows(g1, b1, hb, ob, g2, b2, eb, rb):
    return jnp.concatenate([v.reshape(NF, -1) for v in (g1, b1, hb, ob, g2, b2, eb, rb)], axis=1)


SMALL = (("g1", RB), ("b1", RB), ("hb", 2 * RB), ("ob", RB), ("g2", RB), ("b2", RB), ("eb", FB), ("rb", RB))


def split_small(sm):
    out, at = {}, 0
    for name, width in SMALL:
        out[name] = sm[:, at : at + width]
        at += width
    return out


def par_of(sm):
    s = {k: v.astype(f32) for k, v in split_small(sm).items()}
    hb = s["hb"].reshape(2 * D)
    zero = jnp.zeros((D,), f32)
    eb = s["eb"].reshape(NF, CH, LANE).transpose(1, 0, 2).reshape(CH, CW)

    def wide(v):
        return jnp.pad(v, (0, FF - v.shape[0]))

    rows = [
        s["g1"].reshape(D),
        s["b1"].reshape(D),
        jnp.concatenate([hb[:D], zero, hb[D:]]),
        s["ob"].reshape(D),
        s["g2"].reshape(D),
        s["b2"].reshape(D),
        zero,
        s["rb"].reshape(D),
        eb[0],
        eb[1],
        eb[2],
    ]
    rows += [zero] * 5
    return jnp.stack([wide(r) for r in rows])


def small_grads(seed_sum, hsums, bsums, hbsum, isums):
    eb = jnp.stack([h[0] for h in hsums]).reshape(CH, NF, LANE).transpose(1, 0, 2).reshape(FF)
    hb = jnp.concatenate([hbsum[0, :D], hbsum[0, 2 * D :]])
    return small_rows(isums[0], isums[1], hb, bsums[2], bsums[0], bsums[1], eb, seed_sum[0])


def chain(counts, ids, patches, upstream, table, hooks):
    n = patches.shape[0]
    start, xhat, seed, seed_sum = start_call(counts, table, ids.reshape(n, 1, SLOTS), patches, upstream)
    hw, par = hooks.heads()
    first, qkv, probs, mixed = attend_call(counts, hw, xhat, par)
    ow = hooks.out()
    middle, second = middle_call(ow, mixed, start, par)
    res, dsec = middle, jnp.zeros((8, LANE), f32)
    hsums = []
    for j in range(CH):
        res, dsec, hs, *pieces = mlp_call(j, hooks.mlp(j), hooks.order, second, seed, res, dsec, par)
        hsums.append(hs)
        hooks.grads("m%d" % j, pieces)
    dmid, dmixed, bsums, *pieces = branch_call(ow, hooks.order, middle, dsec, seed, mixed, par)
    hooks.grads("o", pieces)
    dproj, hbsum, *pieces = attend_back_call(hooks.order, qkv, probs, dmixed, first)
    hooks.grads("h", pieces)
    pgrad, isums = input_call(hw, dproj, start, dmid, par)
    smalls = small_grads(seed_sum, hsums, bsums, hbsum, isums)
    return res.reshape(n, SLOTS, D), pgrad.reshape(n, SLOTS, D), hooks.finish(smalls)


FOUR = tuple((b, 0) for b in range(4))


class Plain:
    def __init__(self, args):
        self.full = {k: lax.all_gather(v, "fsdp", axis=0, tiled=True) for k, v in args.items()}
        self.order = jnp.arange(4, dtype=jnp.int32)
        self.got = {}

    def pieces(self, a, quarter):
        return self.order, [a[:, q * quarter : (q + 1) * quarter] for q in range(4)], FOUR

    def heads(self):
        f = self.full
        sm = small_rows(*(f[k] for k, _ in SMALL))
        w = jax.vmap(block_major)(f["hw"].reshape(NF, RB, 3 * D))
        return self.pieces(w, QH), par_of(sm)

    def out(self):
        return self.pieces(jax.vmap(block_major)(self.full["ow"].reshape(NF, RB, D)), QO)

    def mlp(self, j):
        e = self.full["ew"].reshape(NF, RB, NF, CH, LANE)[:, :, :, j].transpose(0, 2, 1, 3)
        r = self.full["rw"].reshape(NF, CH, LANE, OB, LANE)[:, j].transpose(0, 2, 1, 3)
        w = jnp.concatenate([e.reshape(NF, -1, LANE), r.reshape(NF, -1, LANE)], axis=1)
        return self.pieces(w, QM)

    def grads(self, name, pieces):
        self.got[name] = jnp.concatenate(pieces, axis=1)

    def finish(self, smalls):
        g = self.got
        hw = jax.vmap(lambda a: from_block_major(a, RB))(g["h"]).reshape(D, 3 * D)
        ow = jax.vmap(lambda a: from_block_major(a, RB))(g["o"]).reshape(D, D)
        e = jnp.stack([g["m%d" % j][:, : EB * RB].reshape(NF, NF, RB, LANE) for j in range(CH)])
        ew = e.transpose(1, 3, 2, 0, 4).reshape(D, FF)
        r = jnp.stack([g["m%d" % j][:, EB * RB :].reshape(NF, OB, LANE, LANE) for j in range(CH)])
        rw = r.transpose(1, 0, 3, 2, 4).reshape(FF, D)
        s = {k: v.reshape(-1) for k, v in split_small(smalls).items()}
        s.update(hw=hw, ow=ow, ew=ew, rw=rw)

        def total(v):
            part = lax.psum_scatter(v.astype(bf16), "fsdp", scatter_dimension=0, tiled=True)
            return lax.psum(part, "rep").astype(f32)

        return {k: total(v) for k, v in s.items()}


CORE = ((0, 1), (1, 0), (2, 3), (3, 2))
ACROSS = ((0, 2), (2, 0), (1, 3), (3, 1))


def to_core(a):
    return lax.ppermute(a, "rep", CORE)


def to_across(a):
    return lax.ppermute(a, "rep", ACROSS)


def gathered(a):
    return lax.all_gather(a[None], "fsdp", axis=0, tiled=True)


class Fast:
    def __init__(self, args):
        rep = lax.axis_index("rep")
        y, c = rep // 2, rep % 2
        self.y, self.c = y, c
        q = 2 * c + y
        self.order = jnp.stack([q, q ^ 1, q ^ 2, q ^ 3]).astype(jnp.int32)
        self.got = {}
        sm = jnp.concatenate([args[k] for k, _ in SMALL]).reshape(9, LANE)
        hw = lax.dynamic_slice_in_dim(block_major(args["hw"]), c * 2 * QH, 2 * QH, 0)
        hw = jnp.concatenate([hw, sm, jnp.zeros((SM - 9, LANE), bf16)], axis=0)
        ow = lax.dynamic_slice_in_dim(block_major(args["ow"]), q * QO, QO, 0)
        e = args["ew"].reshape(RB, NF, CH, LANE).transpose(2, 1, 0, 3).reshape(CH, -1, LANE)
        r = args["rw"].reshape(CH, LANE, OB, LANE).transpose(0, 2, 1, 3).reshape(CH, -1, LANE)
        m = jnp.concatenate([e, r], axis=1)
        m = lax.dynamic_slice_in_dim(m, q * QM, QM, 1)
        self.h = gathered(hw)
        self.h2 = to_core(self.h)
        self.a = self.spread(gathered(jnp.concatenate([ow, m[0]], axis=0)))
        self.b = self.spread(gathered(jnp.concatenate([m[1], m[2]], axis=0)))

    def spread(self, a):
        b = to_across(a)
        return [a, b, to_core(a), to_core(b)]

    def heads(self):
        c = self.c
        idx = jnp.stack([2 * c, 2 * c + 1, 2 - 2 * c, 3 - 2 * c]).astype(jnp.int32)
        par = par_of(self.h[:, 2 * QH : 2 * QH + 9].reshape(NF, 9 * LANE))
        return (idx, [self.h, self.h2], ((0, 0), (0, QH), (1, 0), (1, QH))), par

    def out(self):
        return self.order, self.a, FOUR

    def mlp(self, j):
        if j == 0:
            return self.order, self.a, tuple((b, QO) for b in range(4))
        return self.order, self.b, tuple((b, (j - 1) * QM) for b in range(4))

    def grads(self, name, pieces):
        self.got[name] = pieces

    def to_quarter(self, pieces):
        a0 = pieces[0] + to_core(pieces[2])
        a1 = pieces[1] + to_core(pieces[3])
        return a0 + to_across(a1)

    def reduced(self, b):
        return lax.psum_scatter(b, "fsdp", scatter_dimension=0, tiled=True)[0]

    def whole_shard(self, own):
        across = to_across(own)
        half = jnp.where(self.y == 0, jnp.concatenate([own, across], 1), jnp.concatenate([across, own], 1))
        other = to_core(half)
        return jnp.where(self.c == 0, jnp.concatenate([half, other], 1), jnp.concatenate([other, half], 1))

    def finish(self, smalls):
        m = [self.reduced(self.to_quarter(self.got["m%d" % j])) for j in range(CH)]
        m = self.whole_shard(jnp.stack(m))
        e = m[:, : EB * RB].reshape(CH, NF, RB, LANE)
        r = m[:, EB * RB :].reshape(CH, OB, LANE, LANE)
        out = {
            "ew": e.transpose(2, 1, 0, 3).reshape(RB, FF).astype(f32),
            "rw": r.transpose(0, 2, 1, 3).reshape(FB, D).astype(f32),
        }
        s = smalls.astype(bf16).reshape(NF, 9, LANE)
        s = s + to_core(s)
        s = s + to_across(s)
        h = self.to_quarter(self.got["h"])
        o = self.to_quarter(self.got["o"])
        h = self.reduced(jnp.concatenate([h, o, s], axis=1))
        sm = split_small(h[QH + QO :].reshape(1, 9 * LANE).astype(f32))
        out.update({k: v[0] for k, v in sm.items()})
        hw = self.whole_shard(h[None, :QH])[0]
        ow = self.whole_shard(h[None, QH : QH + QO])[0]
        out["hw"] = from_block_major(hw, RB).astype(f32)
        out["ow"] = from_block_major(ow, RB).astype(f32)
        return out


NAMES = ("g1", "b1", "hw", "hb", "ow", "ob", "g2", "b2", "ew", "eb", "rw", "rb")


def body(fast, patches, visible_count, patch_index, *rest):
    args = dict(zip(NAMES, rest[:12]))
    upstream = rest[12]
    hooks = (Fast if fast else Plain)(args)
    out, pgrad, g = chain(visible_count, patch_index, patches, upstream, frequency_table(), hooks)
    return (out, pgrad) + tuple(g[k] for k in NAMES)


def solution(mesh):
    rows = P(("rep", "fsdp"), None, None)
    mat, vec = P("fsdp", None), P("fsdp")
    weights = tuple(mat if k[1] == "w" else vec for k in NAMES)
    fast = mesh.shape["fsdp"] == NF and mesh.shape["rep"] == 4
    return jax.shard_map(
        functools.partial(body, fast),
        mesh=mesh,
        in_specs=(rows, P(("rep", "fsdp")), P(("rep", "fsdp"), None)) + weights + (rows,),
        out_specs=(rows, rows) + weights,
        check_vma=False,
    )
```

```python
import functools

import numpy as np
import jax
import jax.numpy as jnp
from jax import lax
from jax.experimental import pallas as pl
from jax.experimental.pallas import tpu as pltpu
from jax.sharding import PartitionSpec as P

D = 768
FF = 3072
HEADS = 12
HEAD_DIM = 64
SLOTS = 80
GRID = 14
NF = 8
RB = D // NF
FB = FF // NF
CH = 3
CW = FF // CH
LANE = 128
HB = 3 * D // LANE
OB = D // LANE
EB = CW // LANE
QH = HB * RB // 4
QO = OB * RB // 4
QM = (EB * RB + OB * LANE) // 4
SM = 16

EPS = 1e-06
NEG = -1e30
bf16 = jnp.bfloat16
f32 = jnp.float32
NN = (((1,), (0,)), ((), ()))
NT = (((1,), (1,)), ((), ()))
TN = (((0,), (0,)), ((), ()))
VMEM_LIMIT = 60 << 20
PER = 4
COST = pl.CostEstimate(flops=1000, bytes_accessed=1000, transcendentals=0)


def mm(a, b, dims):
    return lax.dot_general(a, b, dims, preferred_element_type=f32)


def params(limit=VMEM_LIMIT):
    return pltpu.CompilerParams(vmem_limit_bytes=limit)


def whole(shape):
    return pl.BlockSpec(shape, lambda *_: (0,) * len(shape))


ANY = pl.BlockSpec(memory_space=pl.ANY)
SMEM = pl.BlockSpec(memory_space=pltpu.SMEM)


def block_of(w, base, quarter, start, n):
    q, off = divmod(start, quarter)
    if off + n <= quarter:
        return w[q, :, base + off : base + off + n, :].reshape(NF * n, LANE)
    head = quarter - off
    return jnp.concatenate(
        [w[q, :, base + off : base + quarter, :], w[q + 1, :, base : base + n - head, :]], axis=1
    ).reshape(NF * n, LANE)


def put_block(w, base, quarter, start, n, value):
    value = value.reshape(NF, n, LANE)
    q, off = divmod(start, quarter)
    if off + n <= quarter:
        w[q, :, base + off : base + off + n, :] = value
    else:
        head = quarter - off
        w[q, :, base + off : base + quarter, :] = value[:, :head]
        w[q + 1, :, base : base + n - head, :] = value[:, head:]


def columns(w, base, quarter, rows, blocks):
    return jnp.concatenate([block_of(w, base, quarter, b * rows, rows) for b in blocks], axis=1)


def put_columns(w, base, quarter, rows, blocks, value):
    for i, b in enumerate(blocks):
        put_block(w, base, quarter, b * rows, rows, value[:, i * LANE : (i + 1) * LANE])


def piece_copies(bufs, plan, idx, w, sems):
    copies = []
    for buf, source, target, rows in plan:
        for k in range(bufs[buf].shape[0]):
            n = len(copies)
            copies.append(
                pltpu.make_async_copy(
                    bufs[buf].at[k, pl.ds(source, rows)],
                    w.at[idx[n] // NF, idx[n] % NF, pl.ds(target, rows)],
                    sems.at[n],
                )
            )
    return copies


def n_copies(bufs, plan):
    return sum(bufs[entry[0]].shape[0] for entry in plan)


def send_copies(stage, idx, outs, sems):
    copies = []
    for out in outs:
        for k in range(out.shape[0]):
            n = len(copies)
            copies.append(
                pltpu.make_async_copy(stage.at[idx[n] // NF, idx[n] % NF], out.at[k], sems.at[n])
            )
    return copies


def frequency_table():
    quarter = D // 4
    frequency = 1.0 / 10000.0 ** (jnp.arange(quarter, dtype=f32) / quarter)
    angle = jnp.arange(16, dtype=f32)[:, None] * frequency
    table = jnp.concatenate([jnp.sin(angle), jnp.cos(angle)], axis=-1)
    high = table.astype(bf16)
    rest = table - high.astype(f32)
    middle = rest.astype(bf16)
    low = (rest - middle.astype(f32)).astype(bf16)
    return jnp.concatenate([high, middle, low], axis=0)


def normalised(v):
    c = v - jnp.mean(v, axis=-1, keepdims=True)
    r = lax.rsqrt(jnp.mean(c * c, axis=-1, keepdims=True) + EPS)
    return c * r, r


def norm_back(xhat, r, gain, d):
    e = gain * d
    return r * (
        e - jnp.mean(e, axis=-1, keepdims=True) - xhat * jnp.mean(e * xhat, axis=-1, keepdims=True)
    )


def start_kernel(G, cnt, table, ids, patches, upstream, start, xhat, seed, seed_sum):
    step = pl.program_id(0)

    @pl.when(step == 0)
    def _():
        seed_sum[...] = jnp.zeros_like(seed_sum)

    tab = table[...]
    place = lax.broadcasted_iota(jnp.int32, (48, SLOTS), 0) % 16
    row = lax.broadcasted_iota(jnp.int32, (SLOTS, D), 0)
    total = jnp.zeros((SLOTS, D), f32)
    for g in range(G):
        pid = ids[g]
        by_row = jnp.where(place == pid // GRID, 1.0, 0.0).astype(bf16)
        by_col = jnp.where(place == pid % GRID, 1.0, 0.0).astype(bf16)
        position = jnp.concatenate([mm(by_row, tab, TN), mm(by_col, tab, TN)], axis=1)
        v = patches[g].astype(f32) + position
        here = pl.ds(g * SLOTS, SLOTS)
        start[here, :] = v
        xhat[here, :] = normalised(v)[0]
        s = jnp.where(row < cnt[step * G + g], upstream[g].astype(f32), 0.0)
        seed[here, :] = s.astype(bf16)
        total += s
    seed_sum[...] += jnp.sum(total, axis=0, keepdims=True)


def start_call(counts, table, ids, patches, upstream):
    n = patches.shape[0]
    G = 4 if n % 4 == 0 else 1
    rows = n * SLOTS
    blk = pl.BlockSpec((G * SLOTS, D), lambda i: (i, 0))
    img = pl.BlockSpec((G, SLOTS, D), lambda i: (i, 0, 0))
    return pl.pallas_call(
        functools.partial(start_kernel, G),
        grid=(n // G,),
        in_specs=[SMEM, whole(table.shape), pl.BlockSpec((G, 1, SLOTS), lambda i: (i, 0, 0)), img, img],
        out_specs=[blk, blk, blk, whole((1, D))],
        out_shape=[
            jax.ShapeDtypeStruct((rows, D), f32),
            jax.ShapeDtypeStruct((rows, D), f32),
            jax.ShapeDtypeStruct((rows, D), bf16),
            jax.ShapeDtypeStruct((1, D), f32),
        ],
        compiler_params=params(),
        cost_estimate=COST,
        name="start",
    )(counts, table, ids, patches, upstream)


def head_masks():
    lane = lax.broadcasted_iota(jnp.int32, (SLOTS, LANE), 1)
    return lane < HEAD_DIM


def both_heads(x, left):
    zero = jnp.zeros_like(x)
    return jnp.concatenate([jnp.where(left, x, zero), jnp.where(left, zero, x)], axis=0)


def attend_kernel(G, base, plan, nbuf, cnt, idx, xhat, par, *rest):
    bufs = rest[:nbuf]
    first, qkv, probs, mixed, w, sems = rest[nbuf:]
    step = pl.program_id(0)

    @pl.when(step == 0)
    def _():
        copies = piece_copies(bufs, plan, idx, w, sems)
        for c in copies:
            c.start()
        for c in copies:
            c.wait()

    x = (xhat[...] * par[0:1, :D] + par[1:2, :D]).astype(bf16)
    first[...] = x
    for part in range(3):
        cols = slice(part * D, (part + 1) * D)
        wp = columns(w, 0, QH, RB, range(part * OB, (part + 1) * OB))
        qkv[:, cols] = (mm(x, wp, NN) + par[2:3, cols]).astype(bf16)
    left = head_masks()
    key = lax.broadcasted_iota(jnp.int32, (SLOTS, SLOTS), 0)

    @pl.loop(0, G)
    def _(g):
        live = key < cnt[base + step * G + g]
        rows = pl.ds(pl.multiple_of(g * SLOTS, SLOTS), SLOTS)
        for p in range(HEADS // 2):
            c = p * LANE
            q = qkv[rows, c : c + LANE]
            k = qkv[rows, D + c : D + c + LANE]
            v = qkv[rows, 2 * D + c : 2 * D + c + LANE]
            s = mm(both_heads(k, left), q, NT) * HEAD_DIM**-0.5
            halves = []
            for h in range(2):
                sh = jnp.where(live, s[h * SLOTS : (h + 1) * SLOTS], NEG)
                e = jnp.exp(sh - jnp.max(sh, axis=0, keepdims=True))
                halves.append(e / jnp.sum(e, axis=0, keepdims=True))
            pt = jnp.concatenate(halves, axis=0).astype(bf16)
            probs[g, p] = pt
            mixed[rows, c : c + LANE] = mm(pt, both_heads(v, left), TN).astype(bf16)


def attend_call(counts, w, xhat, par, base, n, G):
    idx, bufs, plan = w
    rows = n * SLOTS
    skip = base // G

    def blk(width):
        return pl.BlockSpec((G * SLOTS, width), lambda i: (i, 0))

    return pl.pallas_call(
        functools.partial(attend_kernel, G, base, plan, len(bufs)),
        grid=(n // G,),
        in_specs=[SMEM, SMEM, pl.BlockSpec((G * SLOTS, D), lambda i: (i + skip, 0)), whole(par.shape)] + [ANY] * len(bufs),
        out_specs=[
            blk(D),
            blk(3 * D),
            pl.BlockSpec((G, HEADS // 2, 2 * SLOTS, SLOTS), lambda i: (i, 0, 0, 0)),
            blk(D),
        ],
        out_shape=[
            jax.ShapeDtypeStruct((rows, D), bf16),
            jax.ShapeDtypeStruct((rows, 3 * D), bf16),
            jax.ShapeDtypeStruct((n, HEADS // 2, 2 * SLOTS, SLOTS), bf16),
            jax.ShapeDtypeStruct((rows, D), bf16),
        ],
        scratch_shapes=[
            pltpu.VMEM((4, NF, QH, LANE), bf16),
            pltpu.SemaphoreType.DMA((n_copies(bufs, plan),)),
        ],
        compiler_params=params(),
        cost_estimate=COST,
        name="attend",
    )(counts, idx, xhat, par, *bufs)


def middle_kernel(plan, nbuf, idx, mixed, start, par, *rest):
    bufs = rest[:nbuf]
    middle, second, w, sems = rest[nbuf:]

    @pl.when(pl.program_id(0) == 0)
    def _():
        copies = piece_copies(bufs, plan, idx, w, sems)
        for c in copies:
            c.start()
        for c in copies:
            c.wait()

    m = start[...] + mm(mixed[...], columns(w, 0, QO, RB, range(OB)), NN) + par[3:4, :D]
    middle[...] = m
    second[...] = (normalised(m)[0] * par[4:5, :D] + par[5:6, :D]).astype(bf16)


def row_block(rows):
    return 240 if rows % 240 == 0 else SLOTS


def middle_call(w, mixed, start, par):
    idx, bufs, plan = w
    rows = mixed.shape[0]
    B = row_block(rows)
    blk = pl.BlockSpec((B, D), lambda i: (i, 0))
    return pl.pallas_call(
        functools.partial(middle_kernel, plan, len(bufs)),
        grid=(rows // B,),
        in_specs=[SMEM, blk, blk, whole(par.shape)] + [ANY] * len(bufs),
        out_specs=[blk, blk],
        out_shape=[jax.ShapeDtypeStruct((rows, D), f32), jax.ShapeDtypeStruct((rows, D), bf16)],
        scratch_shapes=[
            pltpu.VMEM((4, NF, QO, LANE), bf16),
            pltpu.SemaphoreType.DMA((4 * NF,)),
        ],
        compiler_params=params(),
        cost_estimate=COST,
        name="middle",
    )(idx, mixed, start, par, *bufs)


def gelu_and_slope(h):
    a = jnp.abs(h)
    e = jnp.exp(-0.5 * (h * h))
    t = 1.0 / (1.0 + 0.23164189 * a)
    poly = t * (
        0.127414796
        + t * (-0.142248368 + t * (0.7107068705 + t * (-0.7265760135 + t * 0.5307027145)))
    )
    tail = poly * e
    phi = jnp.where(h >= 0, 1.0 - tail, tail)
    return h * phi, phi + h * e * 0.3989422804014327


def mlp_kernel(chunk, plan, nbuf, fresh, last, widx, oidx, second, seed, res_in, dsec_in, par, *rest):
    bufs = rest[:nbuf]
    res, dsec, hsum = rest[nbuf : nbuf + 3]
    outs = rest[nbuf + 3 : -6]
    w, ge, gr, stage, sems, osems = rest[-6:]
    step = pl.program_id(0)
    steps = pl.num_programs(0)

    @pl.when(step == 0)
    def _():
        copies = piece_copies(bufs, plan, widx, w, sems)
        for c in copies:
            c.start()
        ge[...] = jnp.zeros_like(ge)
        gr[...] = jnp.zeros_like(gr)
        hsum[...] = jnp.zeros_like(hsum)
        for c in copies:
            c.wait()

    x = second[...]
    s = seed[...]
    half = EB // 2
    acc = res_in[...]
    dacc = None if fresh else dsec_in[...]
    if fresh:
        acc = acc + par[7:8, :D]
    for t in range(2):
        blocks = range(t * half, (t + 1) * half)
        we = columns(w, 0, QM, RB, blocks)
        fs = slice(t * half, (t + 1) * half)
        wr = jnp.concatenate(
            [w[2 + b // 3, fs, (b % 3) * LANE : (b % 3 + 1) * LANE, :].reshape(half * LANE, LANE) for b in range(OB)],
            axis=1,
        )
        cols = slice(t * half * LANE, (t + 1) * half * LANE)
        h = mm(x, we, NN) + par[8 + chunk : 9 + chunk, cols]
        active, slope = gelu_and_slope(h)
        a = active.astype(bf16)
        dh = (mm(s, wr, NT) * slope)
        d = dh.astype(bf16)
        hsum[0:1, cols] += jnp.sum(d.astype(f32), axis=0, keepdims=True)
        acc = acc + mm(a, wr, NN)
        g = mm(d, we, NT)
        dacc = g if dacc is None else dacc + g
        ge[:, cols] += mm(x, d, TN)
        gr[cols, :] += mm(a, s, TN)
    res[...] = acc.astype(res.dtype)
    dsec[...] = dacc

    @pl.when(step == steps - 1)
    def _():
        for b in range(EB):
            stage[b // 4, :, (b % 4) * RB : (b % 4 + 1) * RB, :] = (
                ge[:, b * LANE : (b + 1) * LANE].astype(bf16).reshape(NF, RB, LANE)
            )
        for b in range(OB):
            stage[2 + b // 3, :, (b % 3) * LANE : (b % 3 + 1) * LANE, :] = (
                gr[:, b * LANE : (b + 1) * LANE].astype(bf16).reshape(NF, LANE, LANE)
            )
        copies = send_copies(stage, oidx, outs, osems)
        for c in copies:
            c.start()
        for c in copies:
            c.wait()


def mlp_call(chunk, w, order, second, seed, res_in, dsec_in, par):
    widx, bufs, plan = w
    oidx, per = order
    rows = second.shape[0]
    B = row_block(rows)
    fresh, last = chunk == 0, chunk == CH - 1
    blk = pl.BlockSpec((B, D), lambda i: (i, 0))
    dspec = blk if not fresh else ANY
    pieces = [jax.ShapeDtypeStruct((per, QM, LANE), bf16)] * (4 * NF // per)
    return pl.pallas_call(
        functools.partial(mlp_kernel, chunk, plan, len(bufs), fresh, last),
        grid=(rows // B,),
        in_specs=[SMEM, SMEM, blk, blk, blk, dspec, whole(par.shape)] + [ANY] * len(bufs),
        out_specs=[blk, blk, whole((1, CW))] + [ANY] * len(pieces),
        out_shape=[
            jax.ShapeDtypeStruct((rows, D), bf16 if last else f32),
            jax.ShapeDtypeStruct((rows, D), f32),
            jax.ShapeDtypeStruct((1, CW), f32),
        ]
        + pieces,
        scratch_shapes=[
            pltpu.VMEM((4, NF, QM, LANE), bf16),
            pltpu.VMEM((D, CW), f32),
            pltpu.VMEM((CW, D), f32),
            pltpu.VMEM((4, NF, QM, LANE), bf16),
            pltpu.SemaphoreType.DMA((n_copies(bufs, plan),)),
            pltpu.SemaphoreType.DMA((4 * NF,)),
        ],
        compiler_params=params(),
        cost_estimate=COST,
        name="mlp",
    )(widx, oidx, second, seed, res_in, dsec_in, par, *bufs)


def branch_kernel(plan, nbuf, idx, oidx, middle, dsec, seed, mixed, par, *rest):
    bufs = rest[:nbuf]
    dmid, dmixed, sums = rest[nbuf : nbuf + 3]
    outs = rest[nbuf + 3 : -5]
    w, acc, stage, sems, osems = rest[-5:]
    step = pl.program_id(0)

    @pl.when(step == 0)
    def _():
        copies = piece_copies(bufs, plan, idx, w, sems)
        for c in copies:
            c.start()
        acc[...] = jnp.zeros_like(acc)
        sums[...] = jnp.zeros_like(sums)
        for c in copies:
            c.wait()

    d = dsec[...]
    xhat, r = normalised(middle[...])
    dm = seed[...].astype(f32) + norm_back(xhat, r, par[4:5, :D], d)
    dmid[...] = dm
    db = dm.astype(bf16)
    sums[0:1, :] += jnp.sum(d * xhat, axis=0, keepdims=True)
    sums[1:2, :] += jnp.sum(d, axis=0, keepdims=True)
    sums[2:3, :] += jnp.sum(db.astype(f32), axis=0, keepdims=True)
    acc[...] += mm(mixed[...], db, TN)
    dmixed[...] = mm(db, columns(w, 0, QO, RB, range(OB)), NT).astype(bf16)

    @pl.when(step == pl.num_programs(0) - 1)
    def _():
        put_columns(stage, 0, QO, RB, range(OB), acc[...].astype(bf16))
        copies = send_copies(stage, oidx, outs, osems)
        for c in copies:
            c.start()
        for c in copies:
            c.wait()


def branch_call(w, order, middle, dsec, seed, mixed, par):
    idx, bufs, plan = w
    oidx, per = order
    pieces = [jax.ShapeDtypeStruct((per, QO, LANE), bf16)] * (4 * NF // per)
    rows = mixed.shape[0]
    B = row_block(rows)
    blk = pl.BlockSpec((B, D), lambda i: (i, 0))
    return pl.pallas_call(
        functools.partial(branch_kernel, plan, len(bufs)),
        grid=(rows // B,),
        in_specs=[SMEM, SMEM, blk, blk, blk, blk, whole(par.shape)] + [ANY] * len(bufs),
        out_specs=[blk, blk, whole((8, D))] + [ANY] * len(pieces),
        out_shape=[
            jax.ShapeDtypeStruct((rows, D), f32),
            jax.ShapeDtypeStruct((rows, D), bf16),
            jax.ShapeDtypeStruct((8, D), f32),
        ]
        + pieces,
        scratch_shapes=[
            pltpu.VMEM((4, NF, QO, LANE), bf16),
            pltpu.VMEM((D, D), f32),
            pltpu.VMEM((4, NF, QO, LANE), bf16),
            pltpu.SemaphoreType.DMA((4 * NF,)),
            pltpu.SemaphoreType.DMA((4 * NF,)),
        ],
        compiler_params=params(),
        cost_estimate=COST,
        name="branch",
    )(idx, oidx, middle, dsec, seed, mixed, par, *bufs)


THIRDS = 3
PT = HEADS // 2 // THIRDS
WT = PT * LANE


def attend_back_kernel(G, oidx, q_ref, k_ref, v_ref, probs, dmixed, first, *rest):
    dproj, sums = rest[:2]
    outs = rest[2:-3]
    acc, stage, osems = rest[-3:]
    step = pl.program_id(0)

    @pl.when(step == 0)
    def _():
        acc[...] = jnp.zeros_like(acc)
        sums[...] = jnp.zeros_like(sums)

    left = head_masks()
    scale = HEAD_DIM**-0.5

    @pl.loop(0, G // 2)
    def _(g):
        todo = []
        for h in range(2):
            rows = pl.ds(pl.multiple_of((2 * g + h) * SLOTS, SLOTS), SLOTS)
            for p in range(PT):
                todo.append((2 * g + h, p, rows, slice(p * LANE, (p + 1) * LANE)))
        dos = [dmixed[rows, c] for _, _, rows, c in todo]
        pts = [probs[i, p] for i, p, _, _ in todo]
        dps = [
            mm(both_heads(v_ref[rows, c], left), do, NT) for (_, _, rows, c), do in zip(todo, dos)
        ]
        dvs = [mm(pt, do, NN) for pt, do in zip(pts, dos)]
        dss = []
        for pt, dp in zip(pts, dps):
            prob = pt.astype(f32)
            parts = []
            for h in range(2):
                ph = prob[h * SLOTS : (h + 1) * SLOTS]
                dh = dp[h * SLOTS : (h + 1) * SLOTS]
                parts.append(ph * (dh - jnp.sum(ph * dh, axis=0, keepdims=True)))
            dss.append(jnp.concatenate(parts, axis=0).astype(bf16))
        dks = [mm(ds, q_ref[rows, c], NN) for ds, (_, _, rows, c) in zip(dss, todo)]
        dqs = [mm(ds, both_heads(k_ref[rows, c], left), TN) for ds, (_, _, rows, c) in zip(dss, todo)]
        for (_, p, rows, c), dq, dk2, dv2 in zip(todo, dqs, dks, dvs):
            dk = jnp.where(left, dk2[:SLOTS], dk2[SLOTS:]) * scale
            dv = jnp.where(left, dv2[:SLOTS], dv2[SLOTS:])
            dproj[rows, p * LANE : (p + 1) * LANE] = (dq * scale).astype(bf16)
            dproj[rows, WT + p * LANE : WT + (p + 1) * LANE] = dk.astype(bf16)
            dproj[rows, 2 * WT + p * LANE : 2 * WT + (p + 1) * LANE] = dv.astype(bf16)

    dall = dproj[...]
    sums[0:1, :] += jnp.sum(dall.astype(f32), axis=0, keepdims=True)
    acc[...] += mm(first[...], dall, TN)

    @pl.when(step == pl.num_programs(0) - 1)
    def _():
        put_columns(stage, 0, QO, RB, range(OB), acc[...].astype(bf16))
        copies = send_copies(stage, oidx, outs, osems)
        for c in copies:
            c.start()
        for c in copies:
            c.wait()


def attend_back_call(t, order, qkv, probs, dmixed, first, G=4):
    oidx, per = order
    rows = first.shape[0]
    n = rows // SLOTS
    G = G if n % G == 0 else 2
    pieces = [jax.ShapeDtypeStruct((per, QO, LANE), bf16)] * (4 * NF // per)

    def blk(width, col):
        return pl.BlockSpec((G * SLOTS, width), lambda i: (i, col))

    return pl.pallas_call(
        functools.partial(attend_back_kernel, G),
        grid=(n // G,),
        in_specs=[
            SMEM,
            blk(WT, t),
            blk(WT, THIRDS + t),
            blk(WT, 2 * THIRDS + t),
            pl.BlockSpec((G, PT, 2 * SLOTS, SLOTS), lambda i: (i, t, 0, 0)),
            blk(WT, t),
            blk(D, 0),
        ],
        out_specs=[blk(3 * WT, 0), whole((8, 3 * WT))] + [ANY] * len(pieces),
        out_shape=[jax.ShapeDtypeStruct((rows, 3 * WT), bf16), jax.ShapeDtypeStruct((8, 3 * WT), f32)]
        + pieces,
        scratch_shapes=[
            pltpu.VMEM((D, 3 * WT), f32),
            pltpu.VMEM((4, NF, QO, LANE), bf16),
            pltpu.SemaphoreType.DMA((4 * NF,)),
        ],
        compiler_params=params(),
        cost_estimate=COST,
        name="attend_back",
    )(oidx, qkv, qkv, qkv, probs, dmixed, first)


def third_blocks(t):
    return [part * OB + t * PT + p for part in range(3) for p in range(PT)]


def input_kernel(plan, nbuf, idx, d0, d1, d2, start, dmid, par, *rest):
    bufs = rest[:nbuf]
    out, sums, w, sems = rest[nbuf:]

    @pl.when(pl.program_id(0) == 0)
    def _():
        copies = piece_copies(bufs, plan, idx, w, sems)
        for c in copies:
            c.start()
        sums[...] = jnp.zeros_like(sums)
        for c in copies:
            c.wait()

    d = None
    for n, dproj in enumerate((d0, d1, d2)):
        t = mm(dproj[...], columns(w, 0, QH, RB, third_blocks(n)), NT)
        d = t if d is None else d + t
    xhat, r = normalised(start[...])
    sums[0:1, :] += jnp.sum(d * xhat, axis=0, keepdims=True)
    sums[1:2, :] += jnp.sum(d, axis=0, keepdims=True)
    out[...] = (dmid[...] + norm_back(xhat, r, par[0:1, :D], d)).astype(bf16)


def input_call(w, dprojs, start, dmid, par):
    idx, bufs, plan = w
    rows = start.shape[0]
    B = row_block(rows)
    blk = pl.BlockSpec((B, D), lambda i: (i, 0))
    return pl.pallas_call(
        functools.partial(input_kernel, plan, len(bufs)),
        grid=(rows // B,),
        in_specs=[SMEM, blk, blk, blk, blk, blk, whole(par.shape)]
        + [ANY] * len(bufs),
        out_specs=[blk, whole((8, D))],
        out_shape=[jax.ShapeDtypeStruct((rows, D), bf16), jax.ShapeDtypeStruct((8, D), f32)],
        scratch_shapes=[
            pltpu.VMEM((4, NF, QH, LANE), bf16),
            pltpu.SemaphoreType.DMA((n_copies(bufs, plan),)),
        ],
        compiler_params=params(),
        cost_estimate=COST,
        name="input_back",
    )(idx, *dprojs, start, dmid, par, *bufs)


SEGMENTS = ("g1", "b1", "ob", "g2", "b2", "rb")
BASE = (0, 6, 30, 36, 42, 48)
BASE_Q, BASE_V, BASE_E, VROWS = 12, 24, 56, 80
TURNS = ((0, 0), (1, 0), (1, 1), (2, 0), (2, 1), (3, 0))


def small_shard(args):
    rows = [args[k] for k in SEGMENTS] + [args["hb"][:RB], args["hb"][RB:]]
    rows = jnp.pad(jnp.stack(rows), ((0, 0), (0, LANE - RB)))
    return jnp.concatenate([rows, args["eb"].reshape(CH, LANE), jnp.zeros((SM - 11, LANE), bf16)], axis=0)


def small_maps(f_of):
    col = lax.broadcasted_iota(jnp.int32, (VROWS, NF * SM), 1)
    row = lax.broadcasted_iota(jnp.int32, (VROWS, NF * SM), 0)
    slot, i = col // SM, col % SM
    f = jnp.zeros_like(col)
    for n in range(NF):
        f = jnp.where(slot == n, f_of[n], f)
    seg = f
    base = jnp.full_like(col, -VROWS)
    for n, b in enumerate(BASE):
        base = jnp.where(i == n, b, base)
    for n in (6, 7):
        s = 2 * f + (n - 6)
        late = s >= NF
        base = jnp.where(i == n, jnp.where(late, BASE_V, BASE_Q), base)
        seg = jnp.where(i == n, jnp.where(late, s - NF, s), seg)
    at = base + 3 * seg // 4
    lane_in = lax.broadcasted_iota(jnp.int32, (LANE, LANE), 0)
    lane_out = lax.broadcasted_iota(jnp.int32, (LANE, LANE), 1)
    maps = []
    for m, second in TURNS:
        pick = jnp.where((row == at + second) & (seg % 4 == m), 1.0, 0.0).astype(bf16)
        shift = 96 * m % LANE - LANE * second
        lanes = jnp.where((lane_in < RB) & (lane_out == lane_in + shift), 1.0, 0.0).astype(bf16)
        maps.append((pick, lanes))
    whole_row = BASE_E + (i - 8) * NF + f
    pick = jnp.where((row == whole_row) & (i >= 8) & (i < 8 + CH), 1.0, 0.0).astype(bf16)
    maps.append((pick, jnp.where(lane_in == lane_out, 1.0, 0.0).astype(bf16)))
    return maps


PAR_ROWS = ((0, 0, 6), (1, 6, 6), (2, 12, 18), (3, 30, 6), (4, 36, 6), (5, 42, 6), (7, 48, 6), (8, 56, 8), (9, 64, 8), (10, 72, 8))


def par_kernel(row, idx, one, two, par, small, sems):
    copies = [
        pltpu.make_async_copy(v.at[pl.ds(0, 4), pl.ds(row, SM)], small.at[pl.ds(4 * n, 4)], sems.at[n])
        for n, v in enumerate((one, two))
    ]
    for c in copies:
        c.start()
    for c in copies:
        c.wait()
    source = small[...].reshape(NF * SM, LANE)
    flat = jnp.zeros((VROWS, LANE), f32)
    for pick, lanes in small_maps([idx[n] for n in range(NF)]):
        flat += mm(mm(pick, source, NN).astype(bf16), lanes, NN)
    par[...] = jnp.zeros_like(par)
    for r, start, n in PAR_ROWS:
        for i in range(n):
            par[r : r + 1, i * LANE : (i + 1) * LANE] = flat[start + i : start + i + 1, :]


def par_call(idx, one, two, row):
    return pl.pallas_call(
        functools.partial(par_kernel, row),
        in_specs=[SMEM, ANY, ANY],
        out_shape=jax.ShapeDtypeStruct((16, FF), f32),
        scratch_shapes=[pltpu.VMEM((NF, SM, LANE), bf16), pltpu.SemaphoreType.DMA((2,))],
        compiler_params=params(),
        cost_estimate=COST,
        name="small_params",
    )(idx, one, two)


def small_grad_kernel(idx, seed_sum, h0, h1, h2, bsums, t0, t1, t2, isums, out, flat):
    flat[...] = jnp.zeros_like(flat)

    def place(start, value):
        for i in range(value.shape[1] // LANE):
            flat[start + i : start + i + 1, :] = value[:, i * LANE : (i + 1) * LANE]

    place(0, isums[0:1, :])
    place(6, isums[1:2, :])
    for t, v in enumerate((t0, t1, t2)):
        place(BASE_Q + PT * t, v[0:1, :WT])
        place(BASE_V + PT * t, v[0:1, 2 * WT :])
    place(30, bsums[2:3, :])
    place(36, bsums[0:1, :])
    place(42, bsums[1:2, :])
    place(48, seed_sum[...])
    for j, h in enumerate((h0, h1, h2)):
        place(BASE_E + j * NF, h[...])
    source = flat[...].astype(bf16)
    total = jnp.zeros((NF * SM, LANE), f32)
    for pick, lanes in small_maps([idx[n] for n in range(NF)]):
        total += mm(mm(pick, source, TN).astype(bf16), lanes, NT)
    out[...] = total.astype(bf16).reshape(NF, SM, LANE)


def small_grad_call(idx, *sums):
    return pl.pallas_call(
        small_grad_kernel,
        in_specs=[SMEM] + [whole(v.shape) for v in sums],
        out_shape=jax.ShapeDtypeStruct((NF, SM, LANE), bf16),
        scratch_shapes=[pltpu.VMEM((VROWS, LANE), f32)],
        compiler_params=params(),
        cost_estimate=COST,
        name="small_grads",
    )(idx, *sums)


def finish_mlp_kernel(idx, *rest):
    bufs = rest[:4]
    ew, rw, w, sems = rest[4:]
    copies = [pltpu.make_async_copy(b, w.at[idx[n]], sems.at[n]) for n, b in enumerate(bufs)]
    for c in copies:
        c.start()
    for c in copies:
        c.wait()

    def rows(j, q, r, n):
        if j < CH - 1:
            return w[q, j * QM + r : j * QM + r + n, :].astype(f32)
        r += (j + q % 2) * QM
        return w[q - q % 2, r : r + n, :].astype(f32) + w[q - q % 2 + 1, r : r + n, :].astype(f32)

    for j in range(CH):
        for b in range(EB):
            ew[:, (CH * b + j) * LANE : (CH * b + j + 1) * LANE] = rows(j, b // 4, b % 4 * RB, RB)
        for b in range(OB):
            rw[j * LANE : (j + 1) * LANE, b * LANE : (b + 1) * LANE] = rows(j, 2 + b // 3, b % 3 * LANE, LANE)


def finish_mlp_call(idx, bufs):
    return pl.pallas_call(
        finish_mlp_kernel,
        in_specs=[SMEM] + [ANY] * 4,
        out_shape=[jax.ShapeDtypeStruct((RB, FF), f32), jax.ShapeDtypeStruct((FB, D), f32)],
        scratch_shapes=[pltpu.VMEM((4,) + bufs[0].shape, bf16), pltpu.SemaphoreType.DMA((4,))],
        compiler_params=params(),
        cost_estimate=COST,
        name="finish_mlp",
    )(idx, *bufs)


def unpack_blocks(out, w, base, targets):
    for b, target in enumerate(targets):
        q, off = divmod(b * RB, QO)
        cols = slice(target * LANE, (target + 1) * LANE)
        head = min(RB, QO - off)
        out[:head, cols] = w[q, base + off : base + off + head, :].astype(f32)
        if head < RB:
            out[head:, cols] = w[q + 1, base : base + RB - head, :].astype(f32)


def finish_heads_kernel(idx, *rest):
    bufs = rest[:4]
    hw, ow, g1, b1, ob, g2, b2, rb, hb, eb, w, sems = rest[4:]
    copies = [pltpu.make_async_copy(b, w.at[idx[n]], sems.at[n]) for n, b in enumerate(bufs)]
    for c in copies:
        c.start()
    for c in copies:
        c.wait()
    unpack_blocks(ow, w, 0, range(OB))
    for t in range(THIRDS):
        unpack_blocks(hw, w, (1 + t) * QO, third_blocks(t))
    small = w[0, (1 + THIRDS) * QO :, :].astype(f32)
    for n, o in enumerate((g1, b1, ob, g2, b2, rb)):
        o[...] = small[n : n + 1, :RB]
    hb[...] = small[6:8, :RB]
    eb[...] = small[8 : 8 + CH, :]


def finish_heads_call(idx, bufs):
    vec = jax.ShapeDtypeStruct((1, RB), f32)
    return pl.pallas_call(
        finish_heads_kernel,
        in_specs=[SMEM] + [ANY] * 4,
        out_shape=[jax.ShapeDtypeStruct((RB, 3 * D), f32), jax.ShapeDtypeStruct((RB, D), f32)]
        + [vec] * 6
        + [jax.ShapeDtypeStruct((2, RB), f32), jax.ShapeDtypeStruct((CH, LANE), f32)],
        scratch_shapes=[pltpu.VMEM((4,) + bufs[0].shape, bf16), pltpu.SemaphoreType.DMA((4,))],
        compiler_params=params(),
        cost_estimate=COST,
        name="finish_heads",
    )(idx, *bufs)


def merge_kernel(counts, *refs):
    inputs, outs = refs[: sum(counts)], refs[sum(counts) :]
    per = outs[0].shape[0]
    for i, out in enumerate(outs):

        @pl.loop(0, per)
        def _(k, i=i, out=out):
            at = row = 0
            for n in counts:
                terms = inputs[at : at + n]
                total = terms[0][i * per + k].astype(f32)
                for t in terms[1:]:
                    total += t[i * per + k].astype(f32)
                rows = terms[0].shape[1]
                out[k, row : row + rows, :] = total.astype(bf16)
                at += n
                row += rows


def merge_call(parts, pieces):
    slots = parts[0][0].shape[0]
    rows = sum(p[0].shape[1] for p in parts)
    flat = [v for p in parts for v in p]
    out = jax.ShapeDtypeStruct((slots // pieces, rows, LANE), bf16)
    return pl.pallas_call(
        functools.partial(merge_kernel, tuple(len(p) for p in parts)),
        out_shape=[out] * pieces,
        compiler_params=params(),
        cost_estimate=COST,
        name="merge",
    )(*flat)


def block_major(a):
    return a.reshape(a.shape[0], -1, LANE).transpose(1, 0, 2).reshape(-1, LANE)


def from_block_major(a, rows):
    return a.reshape(-1, rows, LANE).transpose(1, 0, 2).reshape(rows, -1)


def small_rows(g1, b1, hb, ob, g2, b2, eb, rb):
    return jnp.concatenate([v.reshape(NF, -1) for v in (g1, b1, hb, ob, g2, b2, eb, rb)], axis=1)


SMALL = (("g1", RB), ("b1", RB), ("hb", 2 * RB), ("ob", RB), ("g2", RB), ("b2", RB), ("eb", FB), ("rb", RB))


def split_small(sm):
    out, at = {}, 0
    for name, width in SMALL:
        out[name] = sm[:, at : at + width]
        at += width
    return out


def par_of(sm):
    s = {k: v.astype(f32) for k, v in split_small(sm).items()}
    hb = s["hb"].reshape(2 * D)
    zero = jnp.zeros((D,), f32)
    eb = s["eb"].reshape(NF, CH, LANE).transpose(1, 0, 2).reshape(CH, CW)

    def wide(v):
        return jnp.pad(v, (0, FF - v.shape[0]))

    rows = [
        s["g1"].reshape(D),
        s["b1"].reshape(D),
        jnp.concatenate([hb[:D], zero, hb[D:]]),
        s["ob"].reshape(D),
        s["g2"].reshape(D),
        s["b2"].reshape(D),
        zero,
        s["rb"].reshape(D),
        eb[0],
        eb[1],
        eb[2],
    ]
    rows += [zero] * 5
    return jnp.stack([wide(r) for r in rows])


def small_grads(seed_sum, hsums, bsums, hbsum, isums):
    eb = jnp.stack([h[0] for h in hsums]).reshape(CH, NF, LANE).transpose(1, 0, 2).reshape(FF)
    hb = jnp.concatenate([hbsum[0, :D], hbsum[0, 2 * D :]])
    return small_rows(isums[0], isums[1], hb, bsums[2], bsums[0], bsums[1], eb, seed_sum[0])


def chain(counts, ids, patches, upstream, table, hooks):
    n = patches.shape[0]
    start, xhat, seed, seed_sum = start_call(counts, table, ids.reshape(n, 1, SLOTS), patches, upstream)
    xhat = hooks.opened(xhat)
    hw, par = hooks.heads()
    xhat = hooks.at("attend", xhat)
    first, qkv, probs, mixed = attend_call(counts, hw, xhat, par, 0, n, PER)
    mixed = hooks.at("middle", mixed)
    ow = hooks.out()
    middle, second = middle_call(ow, mixed, start, par)
    res, dsec = middle, jnp.zeros((8, LANE), f32)
    hsums = []
    for j in range(CH):
        second = hooks.at("m%d" % j, second)
        res, dsec, hs, *pieces = mlp_call(j, hooks.mlp(j), hooks.order("m%d" % j), second, seed, res, dsec, par)
        hsums.append(hs)
        hooks.last = hs
        hooks.grads("m%d" % j, pieces)
    dsec = hooks.at("branch", dsec)
    dmid, dmixed, bsums, *pieces = branch_call(ow, hooks.order("o"), middle, dsec, seed, mixed, par)
    hooks.grads("o", pieces)
    dprojs, tsums = [], []
    for t in range(THIRDS):
        dmixed = hooks.at("h%d" % t, dmixed)
        dproj, tsum, *pieces = attend_back_call(t, hooks.order("h%d" % t), qkv, probs, dmixed, first)
        dprojs.append(dproj)
        tsums.append(tsum)
        hooks.grads("h%d" % t, pieces)
    dmid = hooks.at("input", dmid)
    pgrad, isums = input_call(hw, dprojs, start, dmid, par)
    grads = hooks.finish(seed_sum, *hsums, bsums, *tsums, isums)
    return res.reshape(n, SLOTS, D), pgrad.reshape(n, SLOTS, D), grads


class Plain:
    def __init__(self, args):
        self.full = {k: lax.all_gather(v, "fsdp", axis=0, tiled=True) for k, v in args.items()}
        self.idx = jnp.arange(4 * NF, dtype=jnp.int32)
        self.got = {}

    def order(self, name):
        return self.idx, NF

    def pieces(self, a, quarter):
        plan = tuple((q, 0, 0, quarter) for q in range(4))
        return self.idx, [a[:, q * quarter : (q + 1) * quarter] for q in range(4)], plan

    def at(self, name, value):
        return value

    def opened(self, xhat):
        return xhat

    def heads(self):
        f = self.full
        sm = small_rows(*(f[k] for k, _ in SMALL))
        w = jax.vmap(block_major)(f["hw"].reshape(NF, RB, 3 * D))
        return self.pieces(w, QH), par_of(sm)

    def out(self):
        return self.pieces(jax.vmap(block_major)(self.full["ow"].reshape(NF, RB, D)), QO)

    def mlp(self, j):
        e = self.full["ew"].reshape(NF, RB, NF, CH, LANE)[:, :, :, j].transpose(0, 2, 1, 3)
        r = self.full["rw"].reshape(NF, CH, LANE, OB, LANE)[:, j].transpose(0, 2, 1, 3)
        w = jnp.concatenate([e.reshape(NF, -1, LANE), r.reshape(NF, -1, LANE)], axis=1)
        return self.pieces(w, QM)

    def grads(self, name, pieces):
        self.got[name] = jnp.concatenate(pieces, axis=1)

    def finish(self, seed_sum, h0, h1, h2, bsums, t0, t1, t2, isums):
        hbsum = jnp.concatenate([t[:, p * WT : (p + 1) * WT] for p in range(3) for t in (t0, t1, t2)], axis=1)
        smalls = small_grads(seed_sum, (h0, h1, h2), bsums, hbsum, isums)
        g = self.got
        hs = jnp.stack([g["h%d" % t].reshape(NF, 3, PT, RB, LANE) for t in range(THIRDS)])
        hw = hs.transpose(1, 4, 2, 0, 3, 5).reshape(D, 3 * D)
        ow = jax.vmap(lambda a: from_block_major(a, RB))(g["o"]).reshape(D, D)
        e = jnp.stack([g["m%d" % j][:, : EB * RB].reshape(NF, NF, RB, LANE) for j in range(CH)])
        ew = e.transpose(1, 3, 2, 0, 4).reshape(D, FF)
        r = jnp.stack([g["m%d" % j][:, EB * RB :].reshape(NF, OB, LANE, LANE) for j in range(CH)])
        rw = r.transpose(1, 0, 3, 2, 4).reshape(FF, D)
        s = {k: v.reshape(-1) for k, v in split_small(smalls).items()}
        s.update(hw=hw, ow=ow, ew=ew, rw=rw)

        def total(v):
            part = lax.psum_scatter(v.astype(bf16), "fsdp", scatter_dimension=0, tiled=True)
            return lax.psum(part, "rep").astype(f32)

        return {k: total(v) for k, v in s.items()}


NR = 4


def moves(dy, dc, dz, dx):
    pairs = []
    for rep in range(NR):
        for f in range(NF):
            to = (rep // 2 ^ dy) * 2 + (rep % 2 ^ dc)
            at = (f // 2 ^ dz) * 2 + (f % 2 ^ dx)
            pairs.append((rep * NF + f, to * NF + at))
    return pairs


def send(a, dy=0, dc=0, dz=0, dx=0):
    return lax.ppermute(a, ("rep", "fsdp"), moves(dy, dc, dz, dx))


def to_core(a):
    return send(a, dc=1)


def together(*values):
    return lax.optimization_barrier(values)


HS = (QH + SM) // 2
NS = QO + 112


def gathered(a):
    return lax.all_gather(a[None], "fsdp", axis=0, tiled=True)


class Fast:
    def __init__(self, args):
        rep, f = lax.axis_index("rep"), lax.axis_index("fsdp")
        self.y, self.c, self.z, self.x = rep // 2, rep % 2, f // 2, f % 2
        q = 2 * self.c + self.y
        self.g, self.moves = {}, {}
        self.quarters = jnp.stack([q, q ^ 1, q ^ 2, q ^ 3]).astype(jnp.int32)
        wide = lax.dynamic_slice_in_dim(args["hw"], q * QH // RB * LANE, -(-QH // RB) * LANE, 1)
        hw = lax.dynamic_slice_in_dim(block_major(wide), q * QH % RB, QH, 0)
        hw = jnp.concatenate([hw, small_shard(args)], axis=0)
        e = args["ew"].reshape(RB, NF, CH, LANE).transpose(2, 1, 0, 3).reshape(CH, -1, LANE)
        r = args["rw"].reshape(CH, LANE, OB, LANE).transpose(0, 2, 1, 3).reshape(CH, -1, LANE)
        m = jnp.concatenate([e, r], axis=1)
        half = lambda v, n: lax.dynamic_slice_in_dim(v, 2 * self.c * n, 2 * n, -2)
        ow, m = half(block_major(args["ow"]), QO).reshape(2, QO, LANE), half(m, QM).reshape(CH, 2, QM, LANE)
        near = jnp.concatenate([ow, m[0], m[1]], axis=1).reshape(-1, LANE)
        self.near, self.far = gathered(near), gathered(m[2].reshape(-1, LANE))
        self.hz = [hw] + [send(hw, dz=k) for k in (1, 2, 3)]

    def halves(self, pieces, row):
        return jnp.stack([v[:row] for v in pieces]), jnp.stack([v[row:] for v in pieces])

    def round_one(self, a, b):
        return jnp.concatenate([a, send(a, dx=1)], axis=0), jnp.concatenate([b, send(b, dy=1)], axis=0)

    def round_two(self, a, b):
        return send(a, dy=1), send(b, dx=1)

    def opened(self, xhat):
        xhat, *hz = together(xhat, *self.hz)
        a, b = self.round_one(*self.halves(hz, HS))
        a2, b2 = self.round_two(a, b)
        self.h = [a, a2, b, b2] + [to_core(v) for v in (a, a2, b, b2)]
        return xhat

    def places(self, order):
        place = []
        for dc in range(2):
            for i in range(2):
                for j in range(2):
                    d = dict(zip(order, (i, j)))
                    for dz in range(4):
                        q = 2 * (self.c ^ dc) + (self.y ^ d["y"])
                        place.append(q * NF + (self.z ^ dz) * 2 + (self.x ^ d["x"]))
        return jnp.stack(place).astype(jnp.int32)

    def heads(self):
        a, b, n = self.places("yx"), self.places("xy"), 2 * NF
        idx = jnp.concatenate([a[:n], b[:n], a[n:], b[n:]])
        one, two = (0, 0, HS), (0, HS, QH - HS)
        plan = tuple((n,) + (one if n % 4 < 2 else two) for n in range(8))
        at = jnp.concatenate([b[:4], b[8:12]]) % NF
        par = par_call(at, self.h[2], self.h[3], QH - HS)
        return (idx, self.h, plan), par

    def at(self, name, value):
        g = self.g
        if name == "middle":
            value, near = together(value, self.near)
            self.near = [near, to_core(near)]
        if name == "m2":
            self.last, far = together(self.last, self.far)
            self.far = [far, to_core(far)]
            value = self.hold(value, self.added("m0"))
            self.y0 = send(g["m0"][1], dy=1)
        if name == "branch":
            value = self.hold(value, self.added("m1"))
            self.y1 = send(g["m1"][1], dy=1)
        if name == "h0":
            parts = [g["m0"][0] + self.y0, g["m1"][0] + self.y1, *self.added("m2", keep=True)]
            value, parts = together(value, jnp.concatenate(parts, axis=1))
            self.m = lax.psum_scatter(parts, "fsdp", scatter_dimension=0, tiled=True)[0]
        if name == "h2":
            g["near"] = merge_call([g["o"], g["h0"]], 2)
            value = self.hold(value, "near")
            self.xn = send(g["near"][1], dx=1)
        if name == "input":
            far = merge_call([g["h1"], g["h2"]], 4)
            near = g["near"][0]
            near = [near[:4] + self.xn[:4], near[4:] + self.xn[4:]]
            value, *both = together(value, *near, *far)
            self.near = [both[0], send(both[1], dy=1)]
            self.far = self.across_back(both[2:])
        return value

    def hold(self, value, *names):
        flat = [v for name in names for v in self.g[name]]
        value, *flat = together(value, *flat)
        for name in names:
            n = len(self.g[name])
            self.g[name], flat = flat[:n], flat[n:]
        return value

    def across_back(self, a):
        return [a[0], send(a[1], dx=1), send(a[2], dy=1), send(a[3], dx=1, dy=1)]

    def spread_z(self, c):
        return [c[0]] + [send(c[k], dz=k) for k in (1, 2, 3)]

    def added(self, name, keep=False):
        a, b = self.g[name]
        n = a.shape[0] // 2
        parts = [a[:n] + b[:n], a[n:] + b[n:]]
        if keep:
            return parts
        self.g[name] = parts
        return name

    def even_places(self):
        q = 2 * (self.c ^ jnp.arange(2)[:, None, None]) + jnp.arange(2)[:, None]
        return (q * NF + jnp.arange(NF)).reshape(-1).astype(jnp.int32)

    def plan(self, rows, row, n):
        return self.even_places(), tuple((dc, y * rows + row, 0, n) for dc in range(2) for y in range(2))

    def out(self):
        idx, plan = self.plan(QO + 2 * QM, 0, QO)
        self.w = self.near
        return idx, self.w, plan

    def mlp(self, j):
        if j == 2:
            idx, plan = self.plan(QM, 0, QM)
            return idx, self.far, plan
        idx, plan = self.plan(QO + 2 * QM, QO + j * QM, QM)
        return idx, self.w, plan

    def order(self, name):
        if name[0] == "m":
            side = jnp.arange(2)[:, None]
            q = 2 * (self.c ^ jnp.arange(2)[:, None, None]) + (side if name == "m2" else self.y ^ side)
            return (q * NF + jnp.arange(NF)).reshape(-1).astype(jnp.int32), 2 * NF
        return self.places("xy" if name in ("o", "h0") else "yx"), 2 * NF

    def grads(self, name, pieces):
        keep, go = pieces
        if name == "m2":
            go, self.y0 = together(go, self.y0)
        if name == "o":
            go, self.y1 = together(go, self.y1)
        if name == "h2":
            go, self.xn = together(go, self.xn)
        self.g[name] = [keep, to_core(go)]

    def whole_shard(self, own):
        across = send(own, dy=1)
        return [own, across, to_core(own), to_core(across)]

    def finish(self, *sums):
        sums = list(sums)
        *self.far, self.near[1], sums[-1] = together(*self.far, self.near[1], sums[-1])
        s = small_grad_call(self.places("yx")[:8] % NF, *sums)
        s = merge_call([[s, to_core(s)]], 2)
        s = self.across_back([s[0], s[1], s[0], s[1]])
        *last, m = together(*merge_call([self.near, self.far, s], 4), self.m)
        last, m = self.spread_z(last), self.whole_shard(m)
        last = self.whole_shard(merge_call([last], 1)[0][0])
        ew, rw = finish_mlp_call(self.quarters, m)
        hw, ow, g1, b1, ob, g2, b2, rb, hb, eb = finish_heads_call(self.quarters, last)
        out = dict(hw=hw, ow=ow, ew=ew, rw=rw)
        out.update(g1=g1, b1=b1, hb=hb, ob=ob, g2=g2, b2=b2, eb=eb, rb=rb)
        return {k: v if k[1] == "w" else v.reshape(-1) for k, v in out.items()}


NAMES = ("g1", "b1", "hw", "hb", "ow", "ob", "g2", "b2", "ew", "eb", "rw", "rb")


def body(fast, patches, visible_count, patch_index, *rest):
    args = dict(zip(NAMES, rest[:12]))
    upstream = rest[12]
    hooks = (Fast if fast else Plain)(args)
    out, pgrad, g = chain(visible_count, patch_index, patches, upstream, frequency_table(), hooks)
    return (out, pgrad) + tuple(g[k] for k in NAMES)


def solution(mesh):
    rows = P(("rep", "fsdp"), None, None)
    mat, vec = P("fsdp", None), P("fsdp")
    weights = tuple(mat if k[1] == "w" else vec for k in NAMES)
    fast = mesh.shape["fsdp"] == NF and mesh.shape["rep"] == 4
    return jax.shard_map(
        functools.partial(body, fast),
        mesh=mesh,
        in_specs=(rows, P(("rep", "fsdp")), P(("rep", "fsdp"), None)) + weights + (rows,),
        out_specs=(rows, rows) + weights,
        check_vma=False,
    )
```

```python
import functools

import numpy as np
import jax
import jax.numpy as jnp
from jax import lax
from jax.experimental import pallas as pl
from jax.experimental.pallas import tpu as pltpu
from jax.sharding import PartitionSpec as P

D = 768
FF = 3072
HEADS = 12
HEAD_DIM = 64
SLOTS = 80
GRID = 14
NF = 8
RB = D // NF
FB = FF // NF
CH = 3
CW = FF // CH
LANE = 128
HB = 3 * D // LANE
OB = D // LANE
EB = CW // LANE
QH = HB * RB // 4
QO = OB * RB // 4
QM = (EB * RB + OB * LANE) // 4
SM = 16

EPS = 1e-06
NEG = -1e30
bf16 = jnp.bfloat16
f32 = jnp.float32
NN = (((1,), (0,)), ((), ()))
NT = (((1,), (1,)), ((), ()))
TN = (((0,), (0,)), ((), ()))
VMEM_LIMIT = 60 << 20
PER = 4
COST = pl.CostEstimate(flops=1000, bytes_accessed=1000, transcendentals=0)


def mm(a, b, dims):
    return lax.dot_general(a, b, dims, preferred_element_type=f32)


def params(limit=VMEM_LIMIT):
    return pltpu.CompilerParams(vmem_limit_bytes=limit)


def whole(shape):
    return pl.BlockSpec(shape, lambda *_: (0,) * len(shape))


ANY = pl.BlockSpec(memory_space=pl.ANY)
SMEM = pl.BlockSpec(memory_space=pltpu.SMEM)


def block_of(w, base, quarter, start, n):
    q, off = divmod(start, quarter)
    if off + n <= quarter:
        return w[q, :, base + off : base + off + n, :].reshape(NF * n, LANE)
    head = quarter - off
    return jnp.concatenate(
        [w[q, :, base + off : base + quarter, :], w[q + 1, :, base : base + n - head, :]], axis=1
    ).reshape(NF * n, LANE)


def put_block(w, base, quarter, start, n, value):
    value = value.reshape(NF, n, LANE)
    q, off = divmod(start, quarter)
    if off + n <= quarter:
        w[q, :, base + off : base + off + n, :] = value
    else:
        head = quarter - off
        w[q, :, base + off : base + quarter, :] = value[:, :head]
        w[q + 1, :, base : base + n - head, :] = value[:, head:]


def columns(w, base, quarter, rows, blocks):
    return jnp.concatenate([block_of(w, base, quarter, b * rows, rows) for b in blocks], axis=1)


def put_columns(w, base, quarter, rows, blocks, value):
    for i, b in enumerate(blocks):
        put_block(w, base, quarter, b * rows, rows, value[:, i * LANE : (i + 1) * LANE])


def piece_copies(bufs, plan, idx, w, sems):
    copies = []
    for buf, source, target, rows in plan:
        for k in range(bufs[buf].shape[0]):
            n = len(copies)
            copies.append(
                pltpu.make_async_copy(
                    bufs[buf].at[k, pl.ds(source, rows)],
                    w.at[idx[n] // NF, idx[n] % NF, pl.ds(target, rows)],
                    sems.at[n],
                )
            )
    return copies


def n_copies(bufs, plan):
    return sum(bufs[entry[0]].shape[0] for entry in plan)


def send_copies(stage, idx, outs, sems):
    copies = []
    for out in outs:
        for k in range(out.shape[0]):
            n = len(copies)
            copies.append(
                pltpu.make_async_copy(stage.at[idx[n] // NF, idx[n] % NF], out.at[k], sems.at[n])
            )
    return copies


def frequency_table():
    quarter = D // 4
    frequency = 1.0 / 10000.0 ** (jnp.arange(quarter, dtype=f32) / quarter)
    angle = jnp.arange(16, dtype=f32)[:, None] * frequency
    table = jnp.concatenate([jnp.sin(angle), jnp.cos(angle)], axis=-1)
    high = table.astype(bf16)
    rest = table - high.astype(f32)
    middle = rest.astype(bf16)
    low = (rest - middle.astype(f32)).astype(bf16)
    return jnp.concatenate([high, middle, low], axis=0)


def normalised(v):
    c = v - jnp.mean(v, axis=-1, keepdims=True)
    r = lax.rsqrt(jnp.mean(c * c, axis=-1, keepdims=True) + EPS)
    return c * r, r


def norm_back(xhat, r, gain, d):
    e = gain * d
    return r * (
        e - jnp.mean(e, axis=-1, keepdims=True) - xhat * jnp.mean(e * xhat, axis=-1, keepdims=True)
    )


def start_kernel(G, cnt, table, ids, patches, upstream, start, xhat, seed, seed_sum):
    step = pl.program_id(0)

    @pl.when(step == 0)
    def _():
        seed_sum[...] = jnp.zeros_like(seed_sum)

    tab = table[...]
    place = lax.broadcasted_iota(jnp.int32, (48, SLOTS), 0) % 16
    row = lax.broadcasted_iota(jnp.int32, (SLOTS, D), 0)
    total = jnp.zeros((SLOTS, D), f32)
    for g in range(G):
        pid = ids[g]
        by_row = jnp.where(place == pid // GRID, 1.0, 0.0).astype(bf16)
        by_col = jnp.where(place == pid % GRID, 1.0, 0.0).astype(bf16)
        position = jnp.concatenate([mm(by_row, tab, TN), mm(by_col, tab, TN)], axis=1)
        v = patches[g].astype(f32) + position
        here = pl.ds(g * SLOTS, SLOTS)
        start[here, :] = v
        xhat[here, :] = normalised(v)[0]
        s = jnp.where(row < cnt[step * G + g], upstream[g].astype(f32), 0.0)
        seed[here, :] = s.astype(bf16)
        total += s
    seed_sum[...] += jnp.sum(total, axis=0, keepdims=True)


def start_call(counts, table, ids, patches, upstream):
    n = patches.shape[0]
    G = 4 if n % 4 == 0 else 1
    rows = n * SLOTS
    blk = pl.BlockSpec((G * SLOTS, D), lambda i: (i, 0))
    img = pl.BlockSpec((G, SLOTS, D), lambda i: (i, 0, 0))
    return pl.pallas_call(
        functools.partial(start_kernel, G),
        grid=(n // G,),
        in_specs=[SMEM, whole(table.shape), pl.BlockSpec((G, 1, SLOTS), lambda i: (i, 0, 0)), img, img],
        out_specs=[blk, blk, blk, whole((1, D))],
        out_shape=[
            jax.ShapeDtypeStruct((rows, D), f32),
            jax.ShapeDtypeStruct((rows, D), f32),
            jax.ShapeDtypeStruct((rows, D), bf16),
            jax.ShapeDtypeStruct((1, D), f32),
        ],
        compiler_params=params(),
        cost_estimate=COST,
        name="start",
    )(counts, table, ids, patches, upstream)


def head_masks():
    lane = lax.broadcasted_iota(jnp.int32, (SLOTS, LANE), 1)
    return lane < HEAD_DIM


def both_heads(x, left):
    zero = jnp.zeros_like(x)
    return jnp.concatenate([jnp.where(left, x, zero), jnp.where(left, zero, x)], axis=0)


def attend_kernel(G, base, plan, nbuf, cnt, idx, xhat, par, *rest):
    bufs = rest[:nbuf]
    first, qkv, probs, mixed, whole_w, w, sems, wsem = rest[nbuf:]
    step = pl.program_id(0)

    @pl.when(step == 0)
    def _():
        copies = piece_copies(bufs, plan, idx, w, sems)
        for c in copies:
            c.start()
        for c in copies:
            c.wait()
        pltpu.make_async_copy(w, whole_w, wsem.at[0]).start()

    x = (xhat[...] * par[0:1, :D] + par[1:2, :D]).astype(bf16)
    first[...] = x
    for part in range(3):
        cols = slice(part * D, (part + 1) * D)
        wp = columns(w, 0, QH, RB, range(part * OB, (part + 1) * OB))
        qkv[:, cols] = (mm(x, wp, NN) + par[2:3, cols]).astype(bf16)
    left = head_masks()
    key = lax.broadcasted_iota(jnp.int32, (SLOTS, SLOTS), 0)

    todo = []
    for g in range(G):
        live = key < cnt[base + step * G + g]
        rows = slice(g * SLOTS, (g + 1) * SLOTS)
        todo += [(g, p, rows, p * LANE, live) for p in range(HEADS // 2)]
    scores = [
        mm(both_heads(qkv[rows, D + c : D + c + LANE], left), qkv[rows, c : c + LANE], NT)
        for _, _, rows, c, _ in todo
    ]
    pts = []
    for s, (_, _, _, _, live) in zip(scores, todo):
        halves = []
        for h in range(2):
            sh = jnp.where(live, s[h * SLOTS : (h + 1) * SLOTS] * HEAD_DIM**-0.5, NEG)
            e = jnp.exp(sh - jnp.max(sh, axis=0, keepdims=True))
            halves.append(e * (1.0 / jnp.sum(e, axis=0, keepdims=True)))
        pts.append(jnp.concatenate(halves, axis=0).astype(bf16))
    for pt, (g, p, rows, c, _) in zip(pts, todo):
        probs[g, p] = pt
        v = both_heads(qkv[rows, 2 * D + c : 2 * D + c + LANE], left)
        mixed[rows, c : c + LANE] = mm(pt, v, TN).astype(bf16)

    @pl.when(step == pl.num_programs(0) - 1)
    def _():
        pltpu.make_async_copy(w, whole_w, wsem.at[0]).wait()


def attend_call(counts, w, xhat, par, base, n, G):
    idx, bufs, plan = w
    rows = n * SLOTS
    skip = base // G

    def blk(width):
        return pl.BlockSpec((G * SLOTS, width), lambda i: (i, 0))

    return pl.pallas_call(
        functools.partial(attend_kernel, G, base, plan, len(bufs)),
        grid=(n // G,),
        in_specs=[SMEM, SMEM, pl.BlockSpec((G * SLOTS, D), lambda i: (i + skip, 0)), whole(par.shape)] + [ANY] * len(bufs),
        out_specs=[
            blk(D),
            blk(3 * D),
            pl.BlockSpec((G, HEADS // 2, 2 * SLOTS, SLOTS), lambda i: (i, 0, 0, 0)),
            blk(D),
            ANY,
        ],
        out_shape=[
            jax.ShapeDtypeStruct((rows, D), bf16),
            jax.ShapeDtypeStruct((rows, 3 * D), bf16),
            jax.ShapeDtypeStruct((n, HEADS // 2, 2 * SLOTS, SLOTS), bf16),
            jax.ShapeDtypeStruct((rows, D), bf16),
            jax.ShapeDtypeStruct((4, NF, QH, LANE), bf16),
        ],
        scratch_shapes=[
            pltpu.VMEM((4, NF, QH, LANE), bf16),
            pltpu.SemaphoreType.DMA((n_copies(bufs, plan),)),
            pltpu.SemaphoreType.DMA((1,)),
        ],
        compiler_params=params(),
        cost_estimate=COST,
        name="attend",
    )(counts, idx, xhat, par, *bufs)


def row_block(rows):
    return 240 if rows % 240 == 0 else SLOTS


def middle_call(w, mixed, start, par):
    idx, bufs, plan = w
    rows = mixed.shape[0]
    B = row_block(rows)
    blk = pl.BlockSpec((B, D), lambda i: (i, 0))
    return pl.pallas_call(
        functools.partial(middle_kernel, plan, len(bufs)),
        grid=(rows // B,),
        in_specs=[SMEM, blk, blk, whole(par.shape)] + [ANY] * len(bufs),
        out_specs=[blk, blk],
        out_shape=[jax.ShapeDtypeStruct((rows, D), f32), jax.ShapeDtypeStruct((rows, D), bf16)],
        scratch_shapes=[
            pltpu.VMEM((4, NF, QO, LANE), bf16),
            pltpu.SemaphoreType.DMA((4 * NF,)),
        ],
        compiler_params=params(),
        cost_estimate=COST,
        name="middle",
    )(idx, mixed, start, par, *bufs)


def gelu_and_slope(h):
    a = jnp.abs(h)
    e = jnp.exp(-0.5 * (h * h))
    t = 1.0 / (1.0 + 0.23164189 * a)
    poly = t * (
        0.127414796
        + t * (-0.142248368 + t * (0.7107068705 + t * (-0.7265760135 + t * 0.5307027145)))
    )
    tail = poly * e
    phi = jnp.where(h >= 0, 1.0 - tail, tail)
    return h * phi, phi + h * e * 0.3989422804014327


def mlp_kernel(chunk, n_out, plans, counts, *refs):
    fresh = chunk == 0
    refs = list(refs)

    def take(n):
        out, refs[:] = refs[:n], refs[n:]
        return out

    (oidx,) = take(1)
    loads = [(plan, *take(1), take(n)) for plan, n in zip(plans, counts)]
    if fresh:
        mixed, start, seed, par, middle, second, res, dsec, hsum = take(9)
    else:
        second, seed, res_in, dsec_in, par, res, dsec, hsum = take(8)
    outs = take(n_out)
    ws = take(len(loads))
    ge, gr, stage, sems, osems = refs
    w = ws[0]
    step = pl.program_id(0)
    half = EB // 2

    def work(first, last):
        if first:
            copies, at = [], 0
            for (plan, idx, bufs), place in zip(loads, ws):
                n = n_copies(bufs, plan)
                copies += piece_copies(bufs, plan, idx, place, sems.at[pl.ds(at, n)])
                at += n
            for c in copies:
                c.start()
            for c in copies:
                c.wait()
        s = seed[...]
        if fresh:
            m = start[...] + mm(mixed[...], columns(ws[1], 0, QO, RB, range(OB)), NN) + par[3:4, :D]
            middle[...] = m
            x = (normalised(m)[0] * par[4:5, :D] + par[5:6, :D]).astype(bf16)
            second[...] = x
            acc, dacc = m + par[7:8, :D], None
        else:
            x = second[...]
            acc, dacc = res_in[...], dsec_in[...]
        for t in range(2):
            we = columns(w, 0, QM, RB, range(t * half, (t + 1) * half))
            fs = slice(t * half, (t + 1) * half)
            wr = jnp.concatenate(
                [
                    w[2 + b // 3, fs, (b % 3) * LANE : (b % 3 + 1) * LANE, :].reshape(half * LANE, LANE)
                    for b in range(OB)
                ],
                axis=1,
            )
            cols = slice(t * half * LANE, (t + 1) * half * LANE)
            h = mm(x, we, NN) + par[8 + chunk : 9 + chunk, cols]
            active, slope = gelu_and_slope(h)
            a = active.astype(bf16)
            d = (mm(s, wr, NT) * slope).astype(bf16)
            sums = jnp.sum(d.astype(f32), axis=0, keepdims=True)
            hsum[0:1, cols] = sums if first else hsum[0:1, cols] + sums
            acc = acc + mm(a, wr, NN)
            g = mm(d, we, NT)
            dacc = g if dacc is None else dacc + g
            e, r = mm(x, d, TN), mm(a, s, TN)
            if not first:
                e, r = e + ge[:, cols], r + gr[cols, :]
            if last:
                for i in range(half):
                    b = t * half + i
                    stage[b // 4, :, (b % 4) * RB : (b % 4 + 1) * RB, :] = (
                        e[:, i * LANE : (i + 1) * LANE].astype(bf16).reshape(NF, RB, LANE)
                    )
                for b in range(OB):
                    stage[2 + b // 3, fs, (b % 3) * LANE : (b % 3 + 1) * LANE, :] = (
                        r[:, b * LANE : (b + 1) * LANE].astype(bf16).reshape(half, LANE, LANE)
                    )
            else:
                ge[:, cols], gr[cols, :] = e, r
        if last:
            copies = send_copies(stage, oidx, outs, osems)
            for c in copies:
                c.start()
        res[...] = acc.astype(res.dtype)
        dsec[...] = dacc
        if last:
            for c in copies:
                c.wait()

    end = pl.num_programs(0) - 1
    pl.when(step == 0)(functools.partial(work, True, False))
    pl.when((step > 0) & (step < end))(functools.partial(work, False, False))
    pl.when(step == end)(functools.partial(work, False, True))


def mlp_call(chunk, weights, order, values, par):
    oidx, per = order
    rows = values[0].shape[0]
    B = row_block(rows)
    fresh, last = chunk == 0, chunk == CH - 1
    blk = pl.BlockSpec((B, D), lambda i: (i, 0))
    pieces = [jax.ShapeDtypeStruct((per, QM, LANE), bf16)] * (4 * NF // per)

    def out(kind):
        return jax.ShapeDtypeStruct((rows, D), kind)

    outs = ([out(f32), out(bf16)] if fresh else []) + [out(bf16 if last else f32), out(f32)]
    loads, specs = [], []
    for idx, bufs, _ in weights:
        loads += [idx, *bufs]
        specs += [SMEM] + [ANY] * len(bufs)
    return pl.pallas_call(
        functools.partial(
            mlp_kernel, chunk, len(pieces), tuple(w[2] for w in weights), tuple(len(w[1]) for w in weights)
        ),
        grid=(rows // B,),
        in_specs=[SMEM] + specs + [blk] * len(values) + [whole(par.shape)],
        out_specs=[blk] * len(outs) + [whole((1, CW))] + [ANY] * len(pieces),
        out_shape=outs + [jax.ShapeDtypeStruct((1, CW), f32)] + pieces,
        scratch_shapes=[pltpu.VMEM((4, NF, n, LANE), bf16) for n in (QM, QO)[: len(weights)]]
        + [
            pltpu.VMEM((D, CW), f32),
            pltpu.VMEM((CW, D), f32),
            pltpu.VMEM((4, NF, QM, LANE), bf16),
            pltpu.SemaphoreType.DMA((sum(n_copies(w[1], w[2]) for w in weights),)),
            pltpu.SemaphoreType.DMA((4 * NF,)),
        ],
        compiler_params=params(),
        cost_estimate=COST,
        name="mlp",
    )(oidx, *loads, *values, par)


def branch_kernel(plan, nbuf, idx, oidx, middle, dsec, seed, mixed, par, *rest):
    bufs = rest[:nbuf]
    dmid, dmixed, sums = rest[nbuf : nbuf + 3]
    outs = rest[nbuf + 3 : -5]
    w, acc, stage, sems, osems = rest[-5:]
    step = pl.program_id(0)

    @pl.when(step == 0)
    def _():
        copies = piece_copies(bufs, plan, idx, w, sems)
        for c in copies:
            c.start()
        acc[...] = jnp.zeros_like(acc)
        sums[...] = jnp.zeros_like(sums)
        for c in copies:
            c.wait()

    d = dsec[...]
    xhat, r = normalised(middle[...])
    dm = seed[...].astype(f32) + norm_back(xhat, r, par[4:5, :D], d)
    db = dm.astype(bf16)
    dmid[...] = db
    sums[0:1, :] += jnp.sum(d * xhat, axis=0, keepdims=True)
    sums[1:2, :] += jnp.sum(d, axis=0, keepdims=True)
    sums[2:3, :] += jnp.sum(db.astype(f32), axis=0, keepdims=True)
    acc[...] += mm(mixed[...], db, TN)
    dmixed[...] = mm(db, columns(w, 0, QO, RB, range(OB)), NT).astype(bf16)

    @pl.when(step == pl.num_programs(0) - 1)
    def _():
        put_columns(stage, 0, QO, RB, range(OB), acc[...].astype(bf16))
        copies = send_copies(stage, oidx, outs, osems)
        for c in copies:
            c.start()
        for c in copies:
            c.wait()


def branch_call(w, order, middle, dsec, seed, mixed, par):
    idx, bufs, plan = w
    oidx, per = order
    pieces = [jax.ShapeDtypeStruct((per, QO, LANE), bf16)] * (4 * NF // per)
    rows = mixed.shape[0]
    B = row_block(rows)
    blk = pl.BlockSpec((B, D), lambda i: (i, 0))
    return pl.pallas_call(
        functools.partial(branch_kernel, plan, len(bufs)),
        grid=(rows // B,),
        in_specs=[SMEM, SMEM, blk, blk, blk, blk, whole(par.shape)] + [ANY] * len(bufs),
        out_specs=[blk, blk, whole((8, D))] + [ANY] * len(pieces),
        out_shape=[
            jax.ShapeDtypeStruct((rows, D), bf16),
            jax.ShapeDtypeStruct((rows, D), bf16),
            jax.ShapeDtypeStruct((8, D), f32),
        ]
        + pieces,
        scratch_shapes=[
            pltpu.VMEM((4, NF, QO, LANE), bf16),
            pltpu.VMEM((D, D), f32),
            pltpu.VMEM((4, NF, QO, LANE), bf16),
            pltpu.SemaphoreType.DMA((4 * NF,)),
            pltpu.SemaphoreType.DMA((4 * NF,)),
        ],
        compiler_params=params(),
        cost_estimate=COST,
        name="branch",
    )(idx, oidx, middle, dsec, seed, mixed, par, *bufs)


THIRDS = 3
PT = HEADS // 2 // THIRDS
WT = PT * LANE


def attend_back_kernel(G, oidx, q_ref, k_ref, v_ref, probs, dmixed, first, *rest):
    dproj, sums = rest[:2]
    outs = rest[2:-3]
    acc, stage, osems = rest[-3:]
    step = pl.program_id(0)

    @pl.when(step == 0)
    def _():
        acc[...] = jnp.zeros_like(acc)
        sums[...] = jnp.zeros_like(sums)

    left = head_masks()
    scale = HEAD_DIM**-0.5

    todo = []
    for g in range(G):
        rows = slice(g * SLOTS, (g + 1) * SLOTS)
        for p in range(PT):
            todo.append((g, p, rows, slice(p * LANE, (p + 1) * LANE)))
    dos = [dmixed[rows, c] for _, _, rows, c in todo]
    pts = [probs[i, p] for i, p, _, _ in todo]
    dps = [
        mm(both_heads(v_ref[rows, c], left), do, NT) for (_, _, rows, c), do in zip(todo, dos)
    ]
    dvs = [mm(pt, do, NN) for pt, do in zip(pts, dos)]
    dss = []
    for pt, dp in zip(pts, dps):
        prob = pt.astype(f32)
        parts = []
        for h in range(2):
            ph = prob[h * SLOTS : (h + 1) * SLOTS]
            dh = dp[h * SLOTS : (h + 1) * SLOTS]
            parts.append(ph * (dh - jnp.sum(ph * dh, axis=0, keepdims=True)))
        dss.append(jnp.concatenate(parts, axis=0).astype(bf16))
    dks = [mm(ds, q_ref[rows, c], NN) for ds, (_, _, rows, c) in zip(dss, todo)]
    dqs = [mm(ds, both_heads(k_ref[rows, c], left), TN) for ds, (_, _, rows, c) in zip(dss, todo)]
    for (_, p, rows, c), dq, dk2, dv2 in zip(todo, dqs, dks, dvs):
        dk = jnp.where(left, dk2[:SLOTS], dk2[SLOTS:]) * scale
        dv = jnp.where(left, dv2[:SLOTS], dv2[SLOTS:])
        dproj[rows, p * LANE : (p + 1) * LANE] = (dq * scale).astype(bf16)
        dproj[rows, WT + p * LANE : WT + (p + 1) * LANE] = dk.astype(bf16)
        dproj[rows, 2 * WT + p * LANE : 2 * WT + (p + 1) * LANE] = dv.astype(bf16)

    dall = dproj[...]
    sums[0:1, :] += jnp.sum(dall.astype(f32), axis=0, keepdims=True)
    acc[...] += mm(first[...], dall, TN)

    @pl.when(step == pl.num_programs(0) - 1)
    def _():
        put_columns(stage, 0, QO, RB, range(OB), acc[...].astype(bf16))
        copies = send_copies(stage, oidx, outs, osems)
        for c in copies:
            c.start()
        for c in copies:
            c.wait()


def attend_back_call(t, order, qkv, probs, dmixed, first, G=6):
    oidx, per = order
    rows = first.shape[0]
    n = rows // SLOTS
    G = G if n % G == 0 else 2
    pieces = [jax.ShapeDtypeStruct((per, QO, LANE), bf16)] * (4 * NF // per)

    def blk(width, col):
        return pl.BlockSpec((G * SLOTS, width), lambda i: (i, col))

    return pl.pallas_call(
        functools.partial(attend_back_kernel, G),
        grid=(n // G,),
        in_specs=[
            SMEM,
            blk(WT, t),
            blk(WT, THIRDS + t),
            blk(WT, 2 * THIRDS + t),
            pl.BlockSpec((G, PT, 2 * SLOTS, SLOTS), lambda i: (i, t, 0, 0)),
            blk(WT, t),
            blk(D, 0),
        ],
        out_specs=[blk(3 * WT, 0), whole((8, 3 * WT))] + [ANY] * len(pieces),
        out_shape=[jax.ShapeDtypeStruct((rows, 3 * WT), bf16), jax.ShapeDtypeStruct((8, 3 * WT), f32)]
        + pieces,
        scratch_shapes=[
            pltpu.VMEM((D, 3 * WT), f32),
            pltpu.VMEM((4, NF, QO, LANE), bf16),
            pltpu.SemaphoreType.DMA((4 * NF,)),
        ],
        compiler_params=params(),
        cost_estimate=COST,
        name="attend_back",
    )(oidx, qkv, qkv, qkv, probs, dmixed, first)


def third_blocks(t):
    return [part * OB + t * PT + p for part in range(3) for p in range(PT)]


def input_kernel(whole_w, d0, d1, d2, start, dmid, par, *rest):
    out, sums, w, sems = rest

    @pl.when(pl.program_id(0) == 0)
    def _():
        copy = pltpu.make_async_copy(whole_w, w, sems.at[0])
        copy.start()
        sums[...] = jnp.zeros_like(sums)
        copy.wait()

    d = None
    for n, dproj in enumerate((d0, d1, d2)):
        t = mm(dproj[...], columns(w, 0, QH, RB, third_blocks(n)), NT)
        d = t if d is None else d + t
    xhat, r = normalised(start[...])
    sums[0:1, :] += jnp.sum(d * xhat, axis=0, keepdims=True)
    sums[1:2, :] += jnp.sum(d, axis=0, keepdims=True)
    out[...] = (dmid[...].astype(f32) + norm_back(xhat, r, par[0:1, :D], d)).astype(bf16)


def input_call(w, dprojs, start, dmid, par):
    rows = start.shape[0]
    B = row_block(rows)
    blk = pl.BlockSpec((B, D), lambda i: (i, 0))
    return pl.pallas_call(
        input_kernel,
        grid=(rows // B,),
        in_specs=[ANY, blk, blk, blk, blk, blk, whole(par.shape)],
        out_specs=[blk, whole((8, D))],
        out_shape=[jax.ShapeDtypeStruct((rows, D), bf16), jax.ShapeDtypeStruct((8, D), f32)],
        scratch_shapes=[
            pltpu.VMEM((4, NF, QH, LANE), bf16),
            pltpu.SemaphoreType.DMA((1,)),
        ],
        compiler_params=params(),
        cost_estimate=COST,
        name="input_back",
    )(w, *dprojs, start, dmid, par)


SEGMENTS = ("g1", "b1", "ob", "g2", "b2", "rb")
BASE = (0, 6, 30, 36, 42, 48)
BASE_Q, BASE_V, BASE_E, VROWS = 12, 24, 56, 80
TURNS = ((0, 0), (1, 0), (1, 1), (2, 0), (2, 1), (3, 0))


def small_maps(f_of):
    col = lax.broadcasted_iota(jnp.int32, (VROWS, NF * SM), 1)
    row = lax.broadcasted_iota(jnp.int32, (VROWS, NF * SM), 0)
    slot, i = col // SM, col % SM
    f = jnp.zeros_like(col)
    for n in range(NF):
        f = jnp.where(slot == n, f_of[n], f)
    seg = f
    base = jnp.full_like(col, -VROWS)
    for n, b in enumerate(BASE):
        base = jnp.where(i == n, b, base)
    for n in (6, 7):
        s = 2 * f + (n - 6)
        late = s >= NF
        base = jnp.where(i == n, jnp.where(late, BASE_V, BASE_Q), base)
        seg = jnp.where(i == n, jnp.where(late, s - NF, s), seg)
    at = base + 3 * seg // 4
    lane_in = lax.broadcasted_iota(jnp.int32, (LANE, LANE), 0)
    lane_out = lax.broadcasted_iota(jnp.int32, (LANE, LANE), 1)
    maps = []
    for m, second in TURNS:
        pick = jnp.where((row == at + second) & (seg % 4 == m), 1.0, 0.0).astype(bf16)
        shift = 96 * m % LANE - LANE * second
        lanes = jnp.where((lane_in < RB) & (lane_out == lane_in + shift), 1.0, 0.0).astype(bf16)
        maps.append((pick, lanes))
    whole_row = BASE_E + (i - 8) * NF + f
    pick = jnp.where((row == whole_row) & (i >= 8) & (i < 8 + CH), 1.0, 0.0).astype(bf16)
    maps.append((pick, jnp.where(lane_in == lane_out, 1.0, 0.0).astype(bf16)))
    return maps


PAR_ROWS = ((0, 0, 6), (1, 6, 6), (2, 12, 18), (3, 30, 6), (4, 36, 6), (5, 42, 6), (7, 48, 6), (8, 56, 8), (9, 64, 8), (10, 72, 8))


def par_kernel(row, idx, one, two, par, small, sems):
    copies = [
        pltpu.make_async_copy(v.at[pl.ds(0, 4), pl.ds(row, SM)], small.at[pl.ds(4 * n, 4)], sems.at[n])
        for n, v in enumerate((one, two))
    ]
    for c in copies:
        c.start()
    for c in copies:
        c.wait()
    source = small[...].reshape(NF * SM, LANE)
    flat = jnp.zeros((VROWS, LANE), f32)
    for pick, lanes in small_maps([idx[n] for n in range(NF)]):
        flat += mm(mm(pick, source, NN).astype(bf16), lanes, NN)
    par[...] = jnp.zeros_like(par)
    for r, start, n in PAR_ROWS:
        for i in range(n):
            par[r : r + 1, i * LANE : (i + 1) * LANE] = flat[start + i : start + i + 1, :]


def par_call(idx, one, two, row):
    return pl.pallas_call(
        functools.partial(par_kernel, row),
        in_specs=[SMEM, ANY, ANY],
        out_shape=jax.ShapeDtypeStruct((16, FF), f32),
        scratch_shapes=[pltpu.VMEM((NF, SM, LANE), bf16), pltpu.SemaphoreType.DMA((2,))],
        compiler_params=params(),
        cost_estimate=COST,
        name="small_params",
    )(idx, one, two)


def small_grad_kernel(idx, seed_sum, h0, h1, h2, bsums, t0, t1, t2, isums, out, flat):
    flat[...] = jnp.zeros_like(flat)

    def place(start, value):
        for i in range(value.shape[1] // LANE):
            flat[start + i : start + i + 1, :] = value[:, i * LANE : (i + 1) * LANE]

    place(0, isums[0:1, :])
    place(6, isums[1:2, :])
    for t, v in enumerate((t0, t1, t2)):
        place(BASE_Q + PT * t, v[0:1, :WT])
        place(BASE_V + PT * t, v[0:1, 2 * WT :])
    place(30, bsums[2:3, :])
    place(36, bsums[0:1, :])
    place(42, bsums[1:2, :])
    place(48, seed_sum[...])
    for j, h in enumerate((h0, h1, h2)):
        place(BASE_E + j * NF, h[...])
    source = flat[...].astype(bf16)
    total = jnp.zeros((NF * SM, LANE), f32)
    for pick, lanes in small_maps([idx[n] for n in range(NF)]):
        total += mm(mm(pick, source, TN).astype(bf16), lanes, NT)
    out[...] = total.astype(bf16).reshape(NF, SM, LANE)


def small_grad_call(idx, *sums):
    return pl.pallas_call(
        small_grad_kernel,
        in_specs=[SMEM] + [whole(v.shape) for v in sums],
        out_shape=jax.ShapeDtypeStruct((NF, SM, LANE), bf16),
        scratch_shapes=[pltpu.VMEM((VROWS, LANE), f32)],
        compiler_params=params(),
        cost_estimate=COST,
        name="small_grads",
    )(idx, *sums)


def finish_mlp_kernel(idx, *rest):
    bufs = rest[:4]
    ew, rw, w, sems = rest[4:]
    copies = [pltpu.make_async_copy(b, w.at[idx[n]], sems.at[n]) for n, b in enumerate(bufs)]
    for c in copies:
        c.start()
    for c in copies:
        c.wait()

    def rows(j, q, r, n):
        if j == 0:
            return w[q, r : r + n, :].astype(f32)
        r += (2 * j - 1 + q % 2) * QM
        return w[q - q % 2, r : r + n, :].astype(f32) + w[q - q % 2 + 1, r : r + n, :].astype(f32)

    for j in range(CH):
        for b in range(EB):
            ew[:, (CH * b + j) * LANE : (CH * b + j + 1) * LANE] = rows(j, b // 4, b % 4 * RB, RB)
        for b in range(OB):
            rw[j * LANE : (j + 1) * LANE, b * LANE : (b + 1) * LANE] = rows(j, 2 + b // 3, b % 3 * LANE, LANE)


def finish_mlp_call(idx, bufs):
    return pl.pallas_call(
        finish_mlp_kernel,
        in_specs=[SMEM] + [ANY] * 4,
        out_shape=[jax.ShapeDtypeStruct((RB, FF), f32), jax.ShapeDtypeStruct((FB, D), f32)],
        scratch_shapes=[pltpu.VMEM((4,) + bufs[0].shape, bf16), pltpu.SemaphoreType.DMA((4,))],
        compiler_params=params(),
        cost_estimate=COST,
        name="finish_mlp",
    )(idx, *bufs)


def unpack_blocks(out, w, base, targets):
    for b, target in enumerate(targets):
        q, off = divmod(b * RB, QO)
        cols = slice(target * LANE, (target + 1) * LANE)
        head = min(RB, QO - off)
        out[:head, cols] = w[q, base + off : base + off + head, :].astype(f32)
        if head < RB:
            out[head:, cols] = w[q + 1, base : base + RB - head, :].astype(f32)


def finish_heads_kernel(idx, *rest):
    bufs = rest[:4]
    hw, ow, g1, b1, ob, g2, b2, rb, hb, eb, w, sems = rest[4:]
    copies = [pltpu.make_async_copy(b, w.at[idx[n]], sems.at[n]) for n, b in enumerate(bufs)]
    for c in copies:
        c.start()
    for c in copies:
        c.wait()
    unpack_blocks(ow, w, 0, range(OB))
    for t in range(THIRDS):
        unpack_blocks(hw, w, (1 + t) * QO, third_blocks(t))
    small = w[0, (1 + THIRDS) * QO :, :].astype(f32)
    for n, o in enumerate((g1, b1, ob, g2, b2, rb)):
        o[...] = small[n : n + 1, :RB]
    for n in range(2):
        hb[:, n * RB : (n + 1) * RB] = small[6 + n : 7 + n, :RB]
    for n in range(CH):
        eb[:, n * LANE : (n + 1) * LANE] = small[8 + n : 9 + n, :]


def finish_heads_call(idx, bufs):
    vec = jax.ShapeDtypeStruct((1, RB), f32)
    return pl.pallas_call(
        finish_heads_kernel,
        in_specs=[SMEM] + [ANY] * 4,
        out_shape=[jax.ShapeDtypeStruct((RB, 3 * D), f32), jax.ShapeDtypeStruct((RB, D), f32)]
        + [vec] * 6
        + [jax.ShapeDtypeStruct((1, 2 * RB), f32), jax.ShapeDtypeStruct((1, FB), f32)],
        scratch_shapes=[pltpu.VMEM((4,) + bufs[0].shape, bf16), pltpu.SemaphoreType.DMA((4,))],
        compiler_params=params(),
        cost_estimate=COST,
        name="finish_heads",
    )(idx, *bufs)


def pieces_of(ref, start, n):
    parts = []
    while n:
        b, r = divmod(start, RB)
        take = min(n, RB - r)
        parts.append(ref[r : r + take, b * LANE : (b + 1) * LANE])
        start, n = start + take, n - take
    return parts


def prepare_kernel(me, ew, rw, ow, hw, g1, b1, ob, g2, b2, rb, hb, eb, near, far, heads, small):
    small[...] = jnp.zeros_like(small)
    for n, v in enumerate((g1, b1, ob, g2, b2, rb)):
        small[n : n + 1, :RB] = v[...].astype(f32)
    for n in range(2):
        small[6 + n : 7 + n, :RB] = hb[:, n * RB : (n + 1) * RB].astype(f32)
    for n in range(CH):
        small[8 + n : 9 + n, :] = eb[:, n * LANE : (n + 1) * LANE].astype(f32)

    def put(out, row, parts):
        for p in parts:
            out[row : row + p.shape[0], :] = p
            row += p.shape[0]
        return row

    def quarter(j, q):
        if q < 2:
            return [ew[:, (CH * b + j) * LANE : (CH * b + j + 1) * LANE] for b in range(4 * q, 4 * q + 4)]
        blocks = range(3 * (q - 2), 3 * (q - 2) + 3)
        return [rw[j * LANE : (j + 1) * LANE, b * LANE : (b + 1) * LANE] for b in blocks]

    for q in range(4):

        @pl.when(me[0] == q)
        def _(q=q):
            row = put(heads, 0, pieces_of(hw, q * QH, QH))
            heads[row:, :] = small[...].astype(bf16)
            row = 0
            for p in (q - q % 2, q - q % 2 + 1):
                row = put(near, row, pieces_of(ow, p * QO, QO))
                row = put(near, row, quarter(0, p))
            put(near, row, quarter(1, q))
            row = 0
            for p in (q - q % 2, q - q % 2 + 1):
                row = put(far, row, quarter(2, p))


def prepare_call(q, *arrays):
    return pl.pallas_call(
        prepare_kernel,
        in_specs=[SMEM] + [whole(v.shape) for v in arrays],
        out_shape=[
            jax.ShapeDtypeStruct((2 * (QO + QM) + QM, LANE), bf16),
            jax.ShapeDtypeStruct((2 * QM, LANE), bf16),
            jax.ShapeDtypeStruct((QH + SM, LANE), bf16),
        ],
        scratch_shapes=[pltpu.VMEM((SM, LANE), f32)],
        compiler_params=params(),
        cost_estimate=COST,
        name="prepare",
    )(q, *arrays)


def merge_kernel(counts, *refs):
    inputs, outs = refs[: sum(counts)], refs[sum(counts) :]
    per = outs[0].shape[0]
    for i, out in enumerate(outs):

        @pl.loop(0, per)
        def _(k, i=i, out=out):
            at = row = 0
            for n in counts:
                terms = inputs[at : at + n]
                total = terms[0][i * per + k].astype(f32)
                for t in terms[1:]:
                    total += t[i * per + k].astype(f32)
                rows = terms[0].shape[1]
                out[k, row : row + rows, :] = total.astype(bf16)
                at += n
                row += rows


def merge_call(parts, pieces):
    slots = parts[0][0].shape[0]
    rows = sum(p[0].shape[1] for p in parts)
    flat = [v for p in parts for v in p]
    out = jax.ShapeDtypeStruct((slots // pieces, rows, LANE), bf16)
    return pl.pallas_call(
        functools.partial(merge_kernel, tuple(len(p) for p in parts)),
        out_shape=[out] * pieces,
        compiler_params=params(),
        cost_estimate=COST,
        name="merge",
    )(*flat)


def block_major(a):
    return a.reshape(a.shape[0], -1, LANE).transpose(1, 0, 2).reshape(-1, LANE)


def from_block_major(a, rows):
    return a.reshape(-1, rows, LANE).transpose(1, 0, 2).reshape(rows, -1)


def small_rows(g1, b1, hb, ob, g2, b2, eb, rb):
    return jnp.concatenate([v.reshape(NF, -1) for v in (g1, b1, hb, ob, g2, b2, eb, rb)], axis=1)


SMALL = (("g1", RB), ("b1", RB), ("hb", 2 * RB), ("ob", RB), ("g2", RB), ("b2", RB), ("eb", FB), ("rb", RB))


def split_small(sm):
    out, at = {}, 0
    for name, width in SMALL:
        out[name] = sm[:, at : at + width]
        at += width
    return out


def par_of(sm):
    s = {k: v.astype(f32) for k, v in split_small(sm).items()}
    hb = s["hb"].reshape(2 * D)
    zero = jnp.zeros((D,), f32)
    eb = s["eb"].reshape(NF, CH, LANE).transpose(1, 0, 2).reshape(CH, CW)

    def wide(v):
        return jnp.pad(v, (0, FF - v.shape[0]))

    rows = [
        s["g1"].reshape(D),
        s["b1"].reshape(D),
        jnp.concatenate([hb[:D], zero, hb[D:]]),
        s["ob"].reshape(D),
        s["g2"].reshape(D),
        s["b2"].reshape(D),
        zero,
        s["rb"].reshape(D),
        eb[0],
        eb[1],
        eb[2],
    ]
    rows += [zero] * 5
    return jnp.stack([wide(r) for r in rows])


def small_grads(seed_sum, hsums, bsums, hbsum, isums):
    eb = jnp.stack([h[0] for h in hsums]).reshape(CH, NF, LANE).transpose(1, 0, 2).reshape(FF)
    hb = jnp.concatenate([hbsum[0, :D], hbsum[0, 2 * D :]])
    return small_rows(isums[0], isums[1], hb, bsums[2], bsums[0], bsums[1], eb, seed_sum[0])


def chain(counts, ids, patches, upstream, table, hooks):
    n = patches.shape[0]
    start, xhat, seed, seed_sum = start_call(counts, table, ids.reshape(n, 1, SLOTS), patches, upstream)
    xhat = hooks.opened(xhat)
    hw, par = hooks.heads()
    xhat = hooks.at("attend", xhat)
    first, qkv, probs, mixed, whole_w = attend_call(counts, hw, xhat, par, 0, n, PER)
    mixed = hooks.at("middle", mixed)
    ow = hooks.out()
    hsums, res, dsec = [], None, None
    for j in range(CH):
        if j:
            second = hooks.at("m%d" % j, second)
            values, weights = (second, seed, res, dsec), [hooks.mlp(j)]
        else:
            values, weights = (mixed, start, seed), [hooks.mlp(0), ow]
        done = mlp_call(j, weights, hooks.order("m%d" % j), values, par)
        if j == 0:
            middle, second, *done = done
        res, dsec, hs, *pieces = done
        hsums.append(hs)
        hooks.last = hs
        hooks.grads("m%d" % j, pieces)
    dsec = hooks.at("branch", dsec)
    dmid, dmixed, bsums, *pieces = branch_call(ow, hooks.order("o"), middle, dsec, seed, mixed, par)
    hooks.grads("o", pieces)
    dprojs, tsums = [], []
    for t in range(THIRDS):
        dmixed = hooks.at("h%d" % t, dmixed)
        dproj, tsum, *pieces = attend_back_call(t, hooks.order("h%d" % t), qkv, probs, dmixed, first)
        dprojs.append(dproj)
        tsums.append(tsum)
        hooks.grads("h%d" % t, pieces)
    dmid = hooks.at("input", dmid)
    pgrad, isums = input_call(whole_w, dprojs, start, dmid, par)
    grads = hooks.finish(seed_sum, *hsums, bsums, *tsums, isums)
    return res.reshape(n, SLOTS, D), pgrad.reshape(n, SLOTS, D), grads


class Plain:
    def __init__(self, args):
        self.full = {k: lax.all_gather(v, "fsdp", axis=0, tiled=True) for k, v in args.items()}
        self.idx = jnp.arange(4 * NF, dtype=jnp.int32)
        self.got = {}

    def order(self, name):
        return self.idx, NF

    def pieces(self, a, quarter):
        plan = tuple((q, 0, 0, quarter) for q in range(4))
        return self.idx, [a[:, q * quarter : (q + 1) * quarter] for q in range(4)], plan

    def at(self, name, value):
        return value

    def opened(self, xhat):
        return xhat

    def heads(self):
        f = self.full
        sm = small_rows(*(f[k] for k, _ in SMALL))
        w = jax.vmap(block_major)(f["hw"].reshape(NF, RB, 3 * D))
        return self.pieces(w, QH), par_of(sm)

    def out(self):
        return self.pieces(jax.vmap(block_major)(self.full["ow"].reshape(NF, RB, D)), QO)

    def mlp(self, j):
        e = self.full["ew"].reshape(NF, RB, NF, CH, LANE)[:, :, :, j].transpose(0, 2, 1, 3)
        r = self.full["rw"].reshape(NF, CH, LANE, OB, LANE)[:, j].transpose(0, 2, 1, 3)
        w = jnp.concatenate([e.reshape(NF, -1, LANE), r.reshape(NF, -1, LANE)], axis=1)
        return self.pieces(w, QM)

    def grads(self, name, pieces):
        self.got[name] = jnp.concatenate(pieces, axis=1)

    def finish(self, seed_sum, h0, h1, h2, bsums, t0, t1, t2, isums):
        hbsum = jnp.concatenate([t[:, p * WT : (p + 1) * WT] for p in range(3) for t in (t0, t1, t2)], axis=1)
        smalls = small_grads(seed_sum, (h0, h1, h2), bsums, hbsum, isums)
        g = self.got
        hs = jnp.stack([g["h%d" % t].reshape(NF, 3, PT, RB, LANE) for t in range(THIRDS)])
        hw = hs.transpose(1, 4, 2, 0, 3, 5).reshape(D, 3 * D)
        ow = jax.vmap(lambda a: from_block_major(a, RB))(g["o"]).reshape(D, D)
        e = jnp.stack([g["m%d" % j][:, : EB * RB].reshape(NF, NF, RB, LANE) for j in range(CH)])
        ew = e.transpose(1, 3, 2, 0, 4).reshape(D, FF)
        r = jnp.stack([g["m%d" % j][:, EB * RB :].reshape(NF, OB, LANE, LANE) for j in range(CH)])
        rw = r.transpose(1, 0, 3, 2, 4).reshape(FF, D)
        s = {k: v.reshape(-1) for k, v in split_small(smalls).items()}
        s.update(hw=hw, ow=ow, ew=ew, rw=rw)

        def total(v):
            part = lax.psum_scatter(v.astype(bf16), "fsdp", scatter_dimension=0, tiled=True)
            return lax.psum(part, "rep").astype(f32)

        return {k: total(v) for k, v in s.items()}


NR = 4


def moves(dy, dc, dz, dx):
    pairs = []
    for rep in range(NR):
        for f in range(NF):
            to = (rep // 2 ^ dy) * 2 + (rep % 2 ^ dc)
            at = (f // 2 ^ dz) * 2 + (f % 2 ^ dx)
            pairs.append((rep * NF + f, to * NF + at))
    return pairs


def send(a, dy=0, dc=0, dz=0, dx=0):
    return lax.ppermute(a, ("rep", "fsdp"), moves(dy, dc, dz, dx))


def to_core(a):
    return send(a, dc=1)


def together(*values):
    return lax.optimization_barrier(values)


HS = (QH + SM) // 2
NS = QO + 112


def gathered(a):
    return lax.all_gather(a[None], "fsdp", axis=0, tiled=True)


class Fast:
    def __init__(self, args):
        rep, f = lax.axis_index("rep"), lax.axis_index("fsdp")
        self.y, self.c, self.z, self.x = rep // 2, rep % 2, f // 2, f % 2
        q = 2 * self.c + self.y
        self.g, self.moves = {}, {}
        self.quarters = jnp.stack([q, q ^ 1, q ^ 2, q ^ 3]).astype(jnp.int32)
        near, far, hw = prepare_call(
            q.astype(jnp.int32).reshape(1),
            *(args[k] for k in ("ew", "rw", "ow", "hw")),
            *(args[k].reshape(1, -1) for k in SEGMENTS + ("hb", "eb")),
        )
        self.near, self.far = gathered(near), gathered(far)
        self.hz = [hw] + [send(hw, dz=k) for k in (1, 2, 3)]

    def halves(self, pieces, row):
        return jnp.stack([v[:row] for v in pieces]), jnp.stack([v[row:] for v in pieces])

    def round_one(self, a, b):
        return jnp.concatenate([a, send(a, dx=1)], axis=0), jnp.concatenate([b, send(b, dy=1)], axis=0)

    def round_two(self, a, b):
        return send(a, dy=1), send(b, dx=1)

    def opened(self, xhat):
        xhat, *hz = together(xhat, *self.hz)
        a, b = self.round_one(*self.halves(hz, HS))
        a2, b2 = self.round_two(a, b)
        self.h = [a, a2, b, b2] + [to_core(v) for v in (a, a2, b, b2)]
        return xhat

    def places(self, order):
        place = []
        for dc in range(2):
            for i in range(2):
                for j in range(2):
                    d = dict(zip(order, (i, j)))
                    for dz in range(4):
                        q = 2 * (self.c ^ dc) + (self.y ^ d["y"])
                        place.append(q * NF + (self.z ^ dz) * 2 + (self.x ^ d["x"]))
        return jnp.stack(place).astype(jnp.int32)

    def heads(self):
        a, b, n = self.places("yx"), self.places("xy"), 2 * NF
        idx = jnp.concatenate([a[:n], b[:n], a[n:], b[n:]])
        one, two = (0, 0, HS), (0, HS, QH - HS)
        plan = tuple((n,) + (one if n % 4 < 2 else two) for n in range(8))
        at = jnp.concatenate([b[:4], b[8:12]]) % NF
        par = par_call(at, self.h[2], self.h[3], QH - HS)
        return (idx, self.h, plan), par

    def at(self, name, value):
        g = self.g
        if name == "middle":
            value, near = together(value, self.near)
            self.near = [near, to_core(near)]
            self.c1 = send(near[:, 2 * (QO + QM) :], dy=1)
        if name == "m1":
            self.last, c1 = together(self.last, self.c1)
            self.c1 = [c1, to_core(c1)]
        if name == "m2":
            self.last, far = together(self.last, self.far)
            self.far = [far, to_core(far)]
            value = self.hold(value, self.added("m0"))
            self.y0 = send(g["m0"][1], dy=1)
        if name == "branch":
            parts = [g["m0"][0] + self.y0, *self.added("m1", keep=True), *self.added("m2", keep=True)]
            value, parts = together(value, jnp.concatenate(parts, axis=1))
            self.m = lax.psum_scatter(parts, "fsdp", scatter_dimension=0, tiled=True)[0]
        if name == "h2":
            g["near"] = merge_call([g["o"], g["h0"]], 2)
            value = self.hold(value, "near")
            self.xn = send(g["near"][1], dx=1)
        if name == "input":
            far = merge_call([g["h1"], g["h2"]], 4)
            near = g["near"][0]
            near = [near[:4] + self.xn[:4], near[4:] + self.xn[4:]]
            value, *both = together(value, *near, *far)
            self.near = [both[0], send(both[1], dy=1)]
            self.far = self.across_back(both[2:])
        return value

    def hold(self, value, *names):
        flat = [v for name in names for v in self.g[name]]
        value, *flat = together(value, *flat)
        for name in names:
            n = len(self.g[name])
            self.g[name], flat = flat[:n], flat[n:]
        return value

    def across_back(self, a):
        return [a[0], send(a[1], dx=1), send(a[2], dy=1), send(a[3], dx=1, dy=1)]

    def spread_z(self, c):
        return [c[0]] + [send(c[k], dz=k) for k in (1, 2, 3)]

    def added(self, name, keep=False):
        a, b = self.g[name]
        n = a.shape[0] // 2
        parts = [a[:n] + b[:n], a[n:] + b[n:]]
        if keep:
            return parts
        self.g[name] = parts
        return name

    def even_places(self):
        q = 2 * (self.c ^ jnp.arange(2)[:, None, None]) + jnp.arange(2)[:, None]
        return (q * NF + jnp.arange(NF)).reshape(-1).astype(jnp.int32)

    def plan(self, rows, row, n):
        return self.even_places(), tuple((dc, y * rows + row, 0, n) for dc in range(2) for y in range(2))

    def out(self):
        idx, plan = self.plan(QO + QM, 0, QO)
        self.w = self.near
        return idx, self.w, plan

    def mlp(self, j):
        if j == 2:
            idx, plan = self.plan(QM, 0, QM)
            return idx, self.far, plan
        if j == 0:
            idx, plan = self.plan(QO + QM, QO, QM)
            return idx, self.w, plan
        side, row = jnp.arange(2)[:, None, None], 2 * (QO + QM)
        q = 2 * (self.c ^ side) + (self.y ^ side.reshape(2, 1))
        idx = (q * NF + jnp.arange(NF)).reshape(-1).astype(jnp.int32)
        return idx, [self.w[0], self.c1[0], self.w[1], self.c1[1]], ((0, row, 0, QM), (1, 0, 0, QM), (2, row, 0, QM), (3, 0, 0, QM))

    def order(self, name):
        if name[0] == "m":
            side = jnp.arange(2)[:, None]
            q = 2 * (self.c ^ jnp.arange(2)[:, None, None]) + (self.y ^ side if name == "m0" else side)
            return (q * NF + jnp.arange(NF)).reshape(-1).astype(jnp.int32), 2 * NF
        return self.places("xy" if name in ("o", "h0") else "yx"), 2 * NF

    def grads(self, name, pieces):
        keep, go = pieces
        if name == "m2":
            go, self.y0 = together(go, self.y0)
        if name == "h2":
            go, self.xn = together(go, self.xn)
        self.g[name] = [keep, to_core(go)]

    def whole_shard(self, own):
        across = send(own, dy=1)
        return [own, across, to_core(own), to_core(across)]

    def finish(self, *sums):
        sums = list(sums)
        *self.far, self.near[1], sums[-1] = together(*self.far, self.near[1], sums[-1])
        s = small_grad_call(self.places("yx")[:8] % NF, *sums)
        s = merge_call([[s, to_core(s)]], 2)
        s = self.across_back([s[0], s[1], s[0], s[1]])
        last = self.spread_z(merge_call([self.near, self.far, s], 4))
        m, last[0] = together(self.m, last[0])
        across = send(m, dy=1)
        last, m, across = together(merge_call([last], 1)[0][0], m, across)
        ew, rw = finish_mlp_call(self.quarters, [m, across, to_core(m), to_core(across)])
        over, ew, rw = together(send(last, dy=1), ew, rw)
        last = [last, over, to_core(last), to_core(over)]
        hw, ow, g1, b1, ob, g2, b2, rb, hb, eb = finish_heads_call(self.quarters, last)
        out = dict(hw=hw, ow=ow, ew=ew, rw=rw)
        out.update(g1=g1, b1=b1, hb=hb, ob=ob, g2=g2, b2=b2, eb=eb, rb=rb)
        return {k: v if k[1] == "w" else v.reshape(-1) for k, v in out.items()}


NAMES = ("g1", "b1", "hw", "hb", "ow", "ob", "g2", "b2", "ew", "eb", "rw", "rb")


def body(fast, patches, visible_count, patch_index, *rest):
    args = dict(zip(NAMES, rest[:12]))
    upstream = rest[12]
    hooks = (Fast if fast else Plain)(args)
    out, pgrad, g = chain(visible_count, patch_index, patches, upstream, frequency_table(), hooks)
    return (out, pgrad) + tuple(g[k] for k in NAMES)


def solution(mesh):
    rows = P(("rep", "fsdp"), None, None)
    mat, vec = P("fsdp", None), P("fsdp")
    weights = tuple(mat if k[1] == "w" else vec for k in NAMES)
    fast = mesh.shape["fsdp"] == NF and mesh.shape["rep"] == 4
    return jax.shard_map(
        functools.partial(body, fast),
        mesh=mesh,
        in_specs=(rows, P(("rep", "fsdp")), P(("rep", "fsdp"), None)) + weights + (rows,),
        out_specs=(rows, rows) + weights,
        check_vma=False,
    )
```

```python
import functools

import numpy as np
import jax
import jax.numpy as jnp
from jax import lax
from jax.experimental import pallas as pl
from jax.experimental.pallas import tpu as pltpu
from jax.sharding import PartitionSpec as P

D = 768
FF = 3072
HEADS = 12
HEAD_DIM = 64
SLOTS = 80
GRID = 14
NF = 8
RB = D // NF
FB = FF // NF
CH = 3
CW = FF // CH
LANE = 128
HB = 3 * D // LANE
OB = D // LANE
EB = CW // LANE
QH = HB * RB // 4
QO = OB * RB // 4
QM = (EB * RB + OB * LANE) // 4
SM = 16

EPS = 1e-06
NEG = -1e30
bf16 = jnp.bfloat16
f32 = jnp.float32
NN = (((1,), (0,)), ((), ()))
NT = (((1,), (1,)), ((), ()))
TN = (((0,), (0,)), ((), ()))
VMEM_LIMIT = 63 << 20
PER = 4
COST = pl.CostEstimate(flops=1000, bytes_accessed=1000, transcendentals=0)


def mm(a, b, dims):
    return lax.dot_general(a, b, dims, preferred_element_type=f32)


def params(limit=VMEM_LIMIT):
    return pltpu.CompilerParams(vmem_limit_bytes=limit)


def whole(shape):
    return pl.BlockSpec(shape, lambda *_: (0,) * len(shape))


ANY = pl.BlockSpec(memory_space=pl.ANY)
SMEM = pl.BlockSpec(memory_space=pltpu.SMEM)


def block_of(w, base, quarter, start, n):
    q, off = divmod(start, quarter)
    if off + n <= quarter:
        return w[q, :, base + off : base + off + n, :].reshape(NF * n, LANE)
    head = quarter - off
    return jnp.concatenate(
        [w[q, :, base + off : base + quarter, :], w[q + 1, :, base : base + n - head, :]], axis=1
    ).reshape(NF * n, LANE)


def put_block(w, base, quarter, start, n, value):
    value = value.reshape(NF, n, LANE)
    q, off = divmod(start, quarter)
    if off + n <= quarter:
        w[q, :, base + off : base + off + n, :] = value
    else:
        head = quarter - off
        w[q, :, base + off : base + quarter, :] = value[:, :head]
        w[q + 1, :, base : base + n - head, :] = value[:, head:]


def columns(w, base, quarter, rows, blocks):
    return jnp.concatenate([block_of(w, base, quarter, b * rows, rows) for b in blocks], axis=1)


def put_columns(w, base, quarter, rows, blocks, value):
    for i, b in enumerate(blocks):
        put_block(w, base, quarter, b * rows, rows, value[:, i * LANE : (i + 1) * LANE])


def piece_copies(bufs, plan, idx, w, sems):
    copies = []
    for buf, source, target, rows in plan:
        for k in range(bufs[buf].shape[0]):
            n = len(copies)
            copies.append(
                pltpu.make_async_copy(
                    bufs[buf].at[k, pl.ds(source, rows)],
                    w.at[idx[n] // NF, idx[n] % NF, pl.ds(target, rows)],
                    sems.at[n],
                )
            )
    return copies


def n_copies(bufs, plan):
    return sum(bufs[entry[0]].shape[0] for entry in plan)


def send_copies(stage, idx, outs, sems):
    copies = []
    for out in outs:
        for k in range(out.shape[0]):
            n = len(copies)
            copies.append(
                pltpu.make_async_copy(stage.at[idx[n] // NF, idx[n] % NF], out.at[k], sems.at[n])
            )
    return copies


def frequency_table():
    quarter = D // 4
    frequency = 1.0 / 10000.0 ** (jnp.arange(quarter, dtype=f32) / quarter)
    angle = jnp.arange(16, dtype=f32)[:, None] * frequency
    table = jnp.concatenate([jnp.sin(angle), jnp.cos(angle)], axis=-1)
    high = table.astype(bf16)
    rest = table - high.astype(f32)
    middle = rest.astype(bf16)
    low = (rest - middle.astype(f32)).astype(bf16)
    return jnp.concatenate([high, middle, low], axis=0)


def normalised(v):
    c = v - jnp.mean(v, axis=-1, keepdims=True)
    r = lax.rsqrt(jnp.mean(c * c, axis=-1, keepdims=True) + EPS)
    return c * r, r


def norm_back(xhat, r, gain, d):
    e = gain * d
    return r * (
        e - jnp.mean(e, axis=-1, keepdims=True) - xhat * jnp.mean(e * xhat, axis=-1, keepdims=True)
    )


def start_kernel(G, cnt, table, ids, patches, upstream, start, xhat, seed, seed_sum):
    step = pl.program_id(0)

    @pl.when(step == 0)
    def _():
        seed_sum[...] = jnp.zeros_like(seed_sum)

    tab = table[...]
    place = lax.broadcasted_iota(jnp.int32, (48, SLOTS), 0) % 16
    row = lax.broadcasted_iota(jnp.int32, (SLOTS, D), 0)
    total = jnp.zeros((SLOTS, D), f32)
    for g in range(G):
        pid = ids[g]
        by_row = jnp.where(place == pid // GRID, 1.0, 0.0).astype(bf16)
        by_col = jnp.where(place == pid % GRID, 1.0, 0.0).astype(bf16)
        position = jnp.concatenate([mm(by_row, tab, TN), mm(by_col, tab, TN)], axis=1)
        v = patches[g].astype(f32) + position
        here = pl.ds(g * SLOTS, SLOTS)
        start[here, :] = v
        xhat[here, :] = normalised(v)[0]
        s = jnp.where(row < cnt[step * G + g], upstream[g].astype(f32), 0.0)
        seed[here, :] = s.astype(bf16)
        total += s
    seed_sum[...] += jnp.sum(total, axis=0, keepdims=True)


def start_call(counts, table, ids, patches, upstream):
    n = patches.shape[0]
    G = 4 if n % 4 == 0 else 1
    rows = n * SLOTS
    blk = pl.BlockSpec((G * SLOTS, D), lambda i: (i, 0))
    img = pl.BlockSpec((G, SLOTS, D), lambda i: (i, 0, 0))
    return pl.pallas_call(
        functools.partial(start_kernel, G),
        grid=(n // G,),
        in_specs=[SMEM, whole(table.shape), pl.BlockSpec((G, 1, SLOTS), lambda i: (i, 0, 0)), img, img],
        out_specs=[blk, blk, blk, whole((1, D))],
        out_shape=[
            jax.ShapeDtypeStruct((rows, D), f32),
            jax.ShapeDtypeStruct((rows, D), f32),
            jax.ShapeDtypeStruct((rows, D), bf16),
            jax.ShapeDtypeStruct((1, D), f32),
        ],
        compiler_params=params(),
        cost_estimate=COST,
        name="start",
    )(counts, table, ids, patches, upstream)


def head_masks():
    lane = lax.broadcasted_iota(jnp.int32, (SLOTS, LANE), 1)
    return lane < HEAD_DIM


def both_heads(x, left):
    zero = jnp.zeros_like(x)
    return jnp.concatenate([jnp.where(left, x, zero), jnp.where(left, zero, x)], axis=0)


def attend_kernel(G, base, plan, nbuf, cnt, idx, xhat, par, *rest):
    bufs = rest[:nbuf]
    first, qkv, probs, mixed, whole_w, w, sems, wsem = rest[nbuf:]
    step = pl.program_id(0)

    @pl.when(step == 0)
    def _():
        copies = piece_copies(bufs, plan, idx, w, sems)
        for c in copies:
            c.start()
        for c in copies:
            c.wait()
        pltpu.make_async_copy(w, whole_w, wsem.at[0]).start()

    x = (xhat[...] * par[0:1, :D] + par[1:2, :D]).astype(bf16)
    first[...] = x
    for part in range(3):
        cols = slice(part * D, (part + 1) * D)
        wp = columns(w, 0, QH, RB, range(part * OB, (part + 1) * OB))
        qkv[:, cols] = (mm(x, wp, NN) + par[2:3, cols]).astype(bf16)
    left = head_masks()
    key = lax.broadcasted_iota(jnp.int32, (SLOTS, SLOTS), 0)

    todo = []
    for g in range(G):
        live = key < cnt[base + step * G + g]
        rows = slice(g * SLOTS, (g + 1) * SLOTS)
        todo += [(g, p, rows, p * LANE, live) for p in range(HEADS // 2)]
    scores = [
        mm(both_heads(qkv[rows, D + c : D + c + LANE], left), qkv[rows, c : c + LANE], NT)
        for _, _, rows, c, _ in todo
    ]
    pts = []
    for s, (_, _, _, _, live) in zip(scores, todo):
        halves = []
        for h in range(2):
            sh = jnp.where(live, s[h * SLOTS : (h + 1) * SLOTS] * HEAD_DIM**-0.5, NEG)
            e = jnp.exp(sh - jnp.max(sh, axis=0, keepdims=True))
            halves.append(e * (1.0 / jnp.sum(e, axis=0, keepdims=True)))
        pts.append(jnp.concatenate(halves, axis=0).astype(bf16))
    for pt, (g, p, rows, c, _) in zip(pts, todo):
        probs[g, p] = pt
        v = both_heads(qkv[rows, 2 * D + c : 2 * D + c + LANE], left)
        mixed[rows, c : c + LANE] = mm(pt, v, TN).astype(bf16)

    @pl.when(step == pl.num_programs(0) - 1)
    def _():
        pltpu.make_async_copy(w, whole_w, wsem.at[0]).wait()


def attend_call(counts, w, xhat, par, base, n, G):
    idx, bufs, plan = w
    rows = n * SLOTS
    skip = base // G

    def blk(width):
        return pl.BlockSpec((G * SLOTS, width), lambda i: (i, 0))

    return pl.pallas_call(
        functools.partial(attend_kernel, G, base, plan, len(bufs)),
        grid=(n // G,),
        in_specs=[SMEM, SMEM, pl.BlockSpec((G * SLOTS, D), lambda i: (i + skip, 0)), whole(par.shape)] + [ANY] * len(bufs),
        out_specs=[
            blk(D),
            blk(3 * D),
            pl.BlockSpec((G, HEADS // 2, 2 * SLOTS, SLOTS), lambda i: (i, 0, 0, 0)),
            blk(D),
            ANY,
        ],
        out_shape=[
            jax.ShapeDtypeStruct((rows, D), bf16),
            jax.ShapeDtypeStruct((rows, 3 * D), bf16),
            jax.ShapeDtypeStruct((n, HEADS // 2, 2 * SLOTS, SLOTS), bf16),
            jax.ShapeDtypeStruct((rows, D), bf16),
            jax.ShapeDtypeStruct((4, NF, QH, LANE), bf16),
        ],
        scratch_shapes=[
            pltpu.VMEM((4, NF, QH, LANE), bf16),
            pltpu.SemaphoreType.DMA((n_copies(bufs, plan),)),
            pltpu.SemaphoreType.DMA((1,)),
        ],
        compiler_params=params(),
        cost_estimate=COST,
        name="attend",
    )(counts, idx, xhat, par, *bufs)


def row_block(rows):
    return 240 if rows % 240 == 0 else SLOTS


def middle_call(w, mixed, start, par):
    idx, bufs, plan = w
    rows = mixed.shape[0]
    B = row_block(rows)
    blk = pl.BlockSpec((B, D), lambda i: (i, 0))
    return pl.pallas_call(
        functools.partial(middle_kernel, plan, len(bufs)),
        grid=(rows // B,),
        in_specs=[SMEM, blk, blk, whole(par.shape)] + [ANY] * len(bufs),
        out_specs=[blk, blk],
        out_shape=[jax.ShapeDtypeStruct((rows, D), f32), jax.ShapeDtypeStruct((rows, D), bf16)],
        scratch_shapes=[
            pltpu.VMEM((4, NF, QO, LANE), bf16),
            pltpu.SemaphoreType.DMA((4 * NF,)),
        ],
        compiler_params=params(),
        cost_estimate=COST,
        name="middle",
    )(idx, mixed, start, par, *bufs)


def gelu_and_slope(h):
    a = jnp.abs(h)
    e = jnp.exp(-0.5 * (h * h))
    t = 1.0 / (1.0 + 0.23164189 * a)
    poly = t * (
        0.127414796
        + t * (-0.142248368 + t * (0.7107068705 + t * (-0.7265760135 + t * 0.5307027145)))
    )
    tail = poly * e
    phi = jnp.where(h >= 0, 1.0 - tail, tail)
    return h * phi, phi + h * e * 0.3989422804014327


def mlp_kernel(chunk, n_out, plans, counts, *refs):
    fresh = chunk == 0
    refs = list(refs)

    def take(n):
        out, refs[:] = refs[:n], refs[n:]
        return out

    (oidx,) = take(1)
    loads = [(plan, *take(1), take(n)) for plan, n in zip(plans, counts)]
    if fresh:
        mixed, start, seed, par, middle, second, res, dsec, hsum = take(9)
    else:
        second, seed, res_in, dsec_in, par, res, dsec, hsum = take(8)
    outs = take(n_out)
    ws = take(len(loads))
    ge, gr, stage, sems, osems = refs
    w = ws[0]
    step = pl.program_id(0)
    half = EB // 2

    def work(first, last):
        if first:
            copies, at = [], 0
            for (plan, idx, bufs), place in zip(loads, ws):
                n = n_copies(bufs, plan)
                copies += piece_copies(bufs, plan, idx, place, sems.at[pl.ds(at, n)])
                at += n
            for c in copies:
                c.start()
            for c in copies:
                c.wait()
        s = seed[...]
        if fresh:
            m = start[...] + mm(mixed[...], columns(ws[1], 0, QO, RB, range(OB)), NN) + par[3:4, :D]
            middle[...] = m
            x = (normalised(m)[0] * par[4:5, :D] + par[5:6, :D]).astype(bf16)
            second[...] = x
            acc, dacc = m + par[7:8, :D], None
        else:
            x = second[...]
            acc, dacc = res_in[...], dsec_in[...]
        for t in range(2):
            we = columns(w, 0, QM, RB, range(t * half, (t + 1) * half))
            fs = slice(t * half, (t + 1) * half)
            wr = jnp.concatenate(
                [
                    w[2 + b // 3, fs, (b % 3) * LANE : (b % 3 + 1) * LANE, :].reshape(half * LANE, LANE)
                    for b in range(OB)
                ],
                axis=1,
            )
            cols = slice(t * half * LANE, (t + 1) * half * LANE)
            h = mm(x, we, NN) + par[8 + chunk : 9 + chunk, cols]
            active, slope = gelu_and_slope(h)
            a = active.astype(bf16)
            d = (mm(s, wr, NT) * slope).astype(bf16)
            sums = jnp.sum(d.astype(f32), axis=0, keepdims=True)
            hsum[0:1, cols] = sums if first else hsum[0:1, cols] + sums
            acc = acc + mm(a, wr, NN)
            g = mm(d, we, NT)
            dacc = g if dacc is None else dacc + g
            e, r = mm(x, d, TN), mm(a, s, TN)
            if not first:
                e, r = e + ge[:, cols], r + gr[cols, :]
            if last:
                for i in range(half):
                    b = t * half + i
                    stage[b // 4, :, (b % 4) * RB : (b % 4 + 1) * RB, :] = (
                        e[:, i * LANE : (i + 1) * LANE].astype(bf16).reshape(NF, RB, LANE)
                    )
                for b in range(OB):
                    stage[2 + b // 3, fs, (b % 3) * LANE : (b % 3 + 1) * LANE, :] = (
                        r[:, b * LANE : (b + 1) * LANE].astype(bf16).reshape(half, LANE, LANE)
                    )
            else:
                ge[:, cols], gr[cols, :] = e, r
        if last:
            copies = send_copies(stage, oidx, outs, osems)
            for c in copies:
                c.start()
        res[...] = acc.astype(res.dtype)
        dsec[...] = dacc
        if last:
            for c in copies:
                c.wait()

    end = pl.num_programs(0) - 1
    pl.when(step == 0)(functools.partial(work, True, False))
    pl.when((step > 0) & (step < end))(functools.partial(work, False, False))
    pl.when(step == end)(functools.partial(work, False, True))


def mlp_call(chunk, weights, order, values, par):
    oidx, per = order
    rows = values[0].shape[0]
    B = row_block(rows)
    fresh, last = chunk == 0, chunk == CH - 1
    blk = pl.BlockSpec((B, D), lambda i: (i, 0))
    pieces = [jax.ShapeDtypeStruct((per, QM, LANE), bf16)] * (4 * NF // per)

    def out(kind):
        return jax.ShapeDtypeStruct((rows, D), kind)

    outs = ([out(f32), out(bf16)] if fresh else []) + [out(bf16 if last else f32), out(f32)]
    loads, specs = [], []
    for idx, bufs, _ in weights:
        loads += [idx, *bufs]
        specs += [SMEM] + [ANY] * len(bufs)
    return pl.pallas_call(
        functools.partial(
            mlp_kernel, chunk, len(pieces), tuple(w[2] for w in weights), tuple(len(w[1]) for w in weights)
        ),
        grid=(rows // B,),
        in_specs=[SMEM] + specs + [blk] * len(values) + [whole(par.shape)],
        out_specs=[blk] * len(outs) + [whole((1, CW))] + [ANY] * len(pieces),
        out_shape=outs + [jax.ShapeDtypeStruct((1, CW), f32)] + pieces,
        scratch_shapes=[pltpu.VMEM((4, NF, n, LANE), bf16) for n in (QM, QO)[: len(weights)]]
        + [
            pltpu.VMEM((D, CW), f32),
            pltpu.VMEM((CW, D), f32),
            pltpu.VMEM((4, NF, QM, LANE), bf16),
            pltpu.SemaphoreType.DMA((sum(n_copies(w[1], w[2]) for w in weights),)),
            pltpu.SemaphoreType.DMA((4 * NF,)),
        ],
        compiler_params=params(),
        cost_estimate=COST,
        name="mlp",
    )(oidx, *loads, *values, par)


def branch_kernel(plan, nbuf, idx, oidx, middle, dsec, seed, mixed, par, *rest):
    bufs = rest[:nbuf]
    dmid, dmixed, sums = rest[nbuf : nbuf + 3]
    outs = rest[nbuf + 3 : -5]
    w, acc, stage, sems, osems = rest[-5:]
    step = pl.program_id(0)

    @pl.when(step == 0)
    def _():
        copies = piece_copies(bufs, plan, idx, w, sems)
        for c in copies:
            c.start()
        acc[...] = jnp.zeros_like(acc)
        sums[...] = jnp.zeros_like(sums)
        for c in copies:
            c.wait()

    d = dsec[...]
    xhat, r = normalised(middle[...])
    dm = seed[...].astype(f32) + norm_back(xhat, r, par[4:5, :D], d)
    db = dm.astype(bf16)
    dmid[...] = db
    sums[0:1, :] += jnp.sum(d * xhat, axis=0, keepdims=True)
    sums[1:2, :] += jnp.sum(d, axis=0, keepdims=True)
    sums[2:3, :] += jnp.sum(db.astype(f32), axis=0, keepdims=True)
    acc[...] += mm(mixed[...], db, TN)
    dmixed[...] = mm(db, columns(w, 0, QO, RB, range(OB)), NT).astype(bf16)

    @pl.when(step == pl.num_programs(0) - 1)
    def _():
        put_columns(stage, 0, QO, RB, range(OB), acc[...].astype(bf16))
        copies = send_copies(stage, oidx, outs, osems)
        for c in copies:
            c.start()
        for c in copies:
            c.wait()


def branch_call(w, order, middle, dsec, seed, mixed, par):
    idx, bufs, plan = w
    oidx, per = order
    pieces = [jax.ShapeDtypeStruct((per, QO, LANE), bf16)] * (4 * NF // per)
    rows = mixed.shape[0]
    B = row_block(rows)
    blk = pl.BlockSpec((B, D), lambda i: (i, 0))
    return pl.pallas_call(
        functools.partial(branch_kernel, plan, len(bufs)),
        grid=(rows // B,),
        in_specs=[SMEM, SMEM, blk, blk, blk, blk, whole(par.shape)] + [ANY] * len(bufs),
        out_specs=[blk, blk, whole((8, D))] + [ANY] * len(pieces),
        out_shape=[
            jax.ShapeDtypeStruct((rows, D), bf16),
            jax.ShapeDtypeStruct((rows, D), bf16),
            jax.ShapeDtypeStruct((8, D), f32),
        ]
        + pieces,
        scratch_shapes=[
            pltpu.VMEM((4, NF, QO, LANE), bf16),
            pltpu.VMEM((D, D), f32),
            pltpu.VMEM((4, NF, QO, LANE), bf16),
            pltpu.SemaphoreType.DMA((4 * NF,)),
            pltpu.SemaphoreType.DMA((4 * NF,)),
        ],
        compiler_params=params(),
        cost_estimate=COST,
        name="branch",
    )(idx, oidx, middle, dsec, seed, mixed, par, *bufs)


THIRDS = 3
PT = HEADS // 2 // THIRDS
WT = PT * LANE


def attend_back_kernel(G, oidx, q_ref, k_ref, v_ref, probs, dmixed, first, *rest):
    dproj, sums = rest[:2]
    outs = rest[2:-3]
    acc, stage, osems = rest[-3:]
    step = pl.program_id(0)

    @pl.when(step == 0)
    def _():
        acc[...] = jnp.zeros_like(acc)
        sums[...] = jnp.zeros_like(sums)

    left = head_masks()
    scale = HEAD_DIM**-0.5

    todo = []
    for g in range(G):
        rows = slice(g * SLOTS, (g + 1) * SLOTS)
        for p in range(PT):
            todo.append((g, p, rows, slice(p * LANE, (p + 1) * LANE)))
    dos = [dmixed[rows, c] for _, _, rows, c in todo]
    pts = [probs[i, p] for i, p, _, _ in todo]
    dps = [
        mm(both_heads(v_ref[rows, c], left), do, NT) for (_, _, rows, c), do in zip(todo, dos)
    ]
    dvs = [mm(pt, do, NN) for pt, do in zip(pts, dos)]
    dss = []
    for pt, dp in zip(pts, dps):
        prob = pt.astype(f32)
        parts = []
        for h in range(2):
            ph = prob[h * SLOTS : (h + 1) * SLOTS]
            dh = dp[h * SLOTS : (h + 1) * SLOTS]
            parts.append(ph * (dh - jnp.sum(ph * dh, axis=0, keepdims=True)))
        dss.append(jnp.concatenate(parts, axis=0).astype(bf16))
    dks = [mm(ds, q_ref[rows, c], NN) for ds, (_, _, rows, c) in zip(dss, todo)]
    dqs = [mm(ds, both_heads(k_ref[rows, c], left), TN) for ds, (_, _, rows, c) in zip(dss, todo)]
    for (_, p, rows, c), dq, dk2, dv2 in zip(todo, dqs, dks, dvs):
        dk = jnp.where(left, dk2[:SLOTS], dk2[SLOTS:]) * scale
        dv = jnp.where(left, dv2[:SLOTS], dv2[SLOTS:])
        dproj[rows, p * LANE : (p + 1) * LANE] = (dq * scale).astype(bf16)
        dproj[rows, WT + p * LANE : WT + (p + 1) * LANE] = dk.astype(bf16)
        dproj[rows, 2 * WT + p * LANE : 2 * WT + (p + 1) * LANE] = dv.astype(bf16)

    dall = dproj[...]
    sums[0:1, :] += jnp.sum(dall.astype(f32), axis=0, keepdims=True)
    acc[...] += mm(first[...], dall, TN)

    @pl.when(step == pl.num_programs(0) - 1)
    def _():
        put_columns(stage, 0, QO, RB, range(OB), acc[...].astype(bf16))
        copies = send_copies(stage, oidx, outs, osems)
        for c in copies:
            c.start()
        for c in copies:
            c.wait()


def attend_back_call(t, order, qkv, probs, dmixed, first, G=6):
    oidx, per = order
    rows = first.shape[0]
    n = rows // SLOTS
    G = G if n % G == 0 else 2
    pieces = [jax.ShapeDtypeStruct((per, QO, LANE), bf16)] * (4 * NF // per)

    def blk(width, col):
        return pl.BlockSpec((G * SLOTS, width), lambda i: (i, col))

    return pl.pallas_call(
        functools.partial(attend_back_kernel, G),
        grid=(n // G,),
        in_specs=[
            SMEM,
            blk(WT, t),
            blk(WT, THIRDS + t),
            blk(WT, 2 * THIRDS + t),
            pl.BlockSpec((G, PT, 2 * SLOTS, SLOTS), lambda i: (i, t, 0, 0)),
            blk(WT, t),
            blk(D, 0),
        ],
        out_specs=[blk(3 * WT, 0), whole((8, 3 * WT))] + [ANY] * len(pieces),
        out_shape=[jax.ShapeDtypeStruct((rows, 3 * WT), bf16), jax.ShapeDtypeStruct((8, 3 * WT), f32)]
        + pieces,
        scratch_shapes=[
            pltpu.VMEM((D, 3 * WT), f32),
            pltpu.VMEM((4, NF, QO, LANE), bf16),
            pltpu.SemaphoreType.DMA((4 * NF,)),
        ],
        compiler_params=params(),
        cost_estimate=COST,
        name="attend_back",
    )(oidx, qkv, qkv, qkv, probs, dmixed, first)


def third_blocks(t):
    return [part * OB + t * PT + p for part in range(3) for p in range(PT)]


def input_kernel(whole_w, d0, d1, d2, start, dmid, par, *rest):
    out, sums, w, sems = rest

    @pl.when(pl.program_id(0) == 0)
    def _():
        copy = pltpu.make_async_copy(whole_w, w, sems.at[0])
        copy.start()
        sums[...] = jnp.zeros_like(sums)
        copy.wait()

    d = None
    for n, dproj in enumerate((d0, d1, d2)):
        t = mm(dproj[...], columns(w, 0, QH, RB, third_blocks(n)), NT)
        d = t if d is None else d + t
    xhat, r = normalised(start[...])
    sums[0:1, :] += jnp.sum(d * xhat, axis=0, keepdims=True)
    sums[1:2, :] += jnp.sum(d, axis=0, keepdims=True)
    out[...] = (dmid[...].astype(f32) + norm_back(xhat, r, par[0:1, :D], d)).astype(bf16)


def input_call(w, dprojs, start, dmid, par):
    rows = start.shape[0]
    B = row_block(rows)
    blk = pl.BlockSpec((B, D), lambda i: (i, 0))
    return pl.pallas_call(
        input_kernel,
        grid=(rows // B,),
        in_specs=[ANY, blk, blk, blk, blk, blk, whole(par.shape)],
        out_specs=[blk, whole((8, D))],
        out_shape=[jax.ShapeDtypeStruct((rows, D), bf16), jax.ShapeDtypeStruct((8, D), f32)],
        scratch_shapes=[
            pltpu.VMEM((4, NF, QH, LANE), bf16),
            pltpu.SemaphoreType.DMA((1,)),
        ],
        compiler_params=params(),
        cost_estimate=COST,
        name="input_back",
    )(w, *dprojs, start, dmid, par)


SEGMENTS = ("g1", "b1", "ob", "g2", "b2", "rb")
BASE = (0, 6, 30, 36, 42, 48)
BASE_Q, BASE_V, BASE_E, VROWS = 12, 24, 56, 80
TURNS = ((0, 0), (1, 0), (1, 1), (2, 0), (2, 1), (3, 0))


def small_maps(f_of):
    col = lax.broadcasted_iota(jnp.int32, (VROWS, NF * SM), 1)
    row = lax.broadcasted_iota(jnp.int32, (VROWS, NF * SM), 0)
    slot, i = col // SM, col % SM
    f = jnp.zeros_like(col)
    for n in range(NF):
        f = jnp.where(slot == n, f_of[n], f)
    seg = f
    base = jnp.full_like(col, -VROWS)
    for n, b in enumerate(BASE):
        base = jnp.where(i == n, b, base)
    for n in (6, 7):
        s = 2 * f + (n - 6)
        late = s >= NF
        base = jnp.where(i == n, jnp.where(late, BASE_V, BASE_Q), base)
        seg = jnp.where(i == n, jnp.where(late, s - NF, s), seg)
    at = base + 3 * seg // 4
    lane_in = lax.broadcasted_iota(jnp.int32, (LANE, LANE), 0)
    lane_out = lax.broadcasted_iota(jnp.int32, (LANE, LANE), 1)
    maps = []
    for m, second in TURNS:
        pick = jnp.where((row == at + second) & (seg % 4 == m), 1.0, 0.0).astype(bf16)
        shift = 96 * m % LANE - LANE * second
        lanes = jnp.where((lane_in < RB) & (lane_out == lane_in + shift), 1.0, 0.0).astype(bf16)
        maps.append((pick, lanes))
    whole_row = BASE_E + (i - 8) * NF + f
    pick = jnp.where((row == whole_row) & (i >= 8) & (i < 8 + CH), 1.0, 0.0).astype(bf16)
    maps.append((pick, jnp.where(lane_in == lane_out, 1.0, 0.0).astype(bf16)))
    return maps


PAR_ROWS = ((0, 0, 6), (1, 6, 6), (2, 12, 18), (3, 30, 6), (4, 36, 6), (5, 42, 6), (7, 48, 6), (8, 56, 8), (9, 64, 8), (10, 72, 8))


def par_kernel(row, idx, one, two, par, small, sems):
    copies = [
        pltpu.make_async_copy(v.at[pl.ds(0, 4), pl.ds(row, SM)], small.at[pl.ds(4 * n, 4)], sems.at[n])
        for n, v in enumerate((one, two))
    ]
    for c in copies:
        c.start()
    for c in copies:
        c.wait()
    source = small[...].reshape(NF * SM, LANE)
    flat = jnp.zeros((VROWS, LANE), f32)
    for pick, lanes in small_maps([idx[n] for n in range(NF)]):
        flat += mm(mm(pick, source, NN).astype(bf16), lanes, NN)
    par[...] = jnp.zeros_like(par)
    for r, start, n in PAR_ROWS:
        for i in range(n):
            par[r : r + 1, i * LANE : (i + 1) * LANE] = flat[start + i : start + i + 1, :]


def par_call(idx, one, two, row):
    return pl.pallas_call(
        functools.partial(par_kernel, row),
        in_specs=[SMEM, ANY, ANY],
        out_shape=jax.ShapeDtypeStruct((16, FF), f32),
        scratch_shapes=[pltpu.VMEM((NF, SM, LANE), bf16), pltpu.SemaphoreType.DMA((2,))],
        compiler_params=params(),
        cost_estimate=COST,
        name="small_params",
    )(idx, one, two)


def small_grad_kernel(idx, seed_sum, h0, h1, h2, bsums, t0, t1, t2, isums, out, flat):
    flat[...] = jnp.zeros_like(flat)

    def place(start, value):
        for i in range(value.shape[1] // LANE):
            flat[start + i : start + i + 1, :] = value[:, i * LANE : (i + 1) * LANE]

    place(0, isums[0:1, :])
    place(6, isums[1:2, :])
    for t, v in enumerate((t0, t1, t2)):
        place(BASE_Q + PT * t, v[0:1, :WT])
        place(BASE_V + PT * t, v[0:1, 2 * WT :])
    place(30, bsums[2:3, :])
    place(36, bsums[0:1, :])
    place(42, bsums[1:2, :])
    place(48, seed_sum[...])
    for j, h in enumerate((h0, h1, h2)):
        place(BASE_E + j * NF, h[...])
    source = flat[...].astype(bf16)
    total = jnp.zeros((NF * SM, LANE), f32)
    for pick, lanes in small_maps([idx[n] for n in range(NF)]):
        total += mm(mm(pick, source, TN).astype(bf16), lanes, NT)
    out[...] = total.astype(bf16).reshape(NF, SM, LANE)


def small_grad_call(idx, *sums):
    return pl.pallas_call(
        small_grad_kernel,
        in_specs=[SMEM] + [whole(v.shape) for v in sums],
        out_shape=jax.ShapeDtypeStruct((NF, SM, LANE), bf16),
        scratch_shapes=[pltpu.VMEM((VROWS, LANE), f32)],
        compiler_params=params(),
        cost_estimate=COST,
        name="small_grads",
    )(idx, *sums)


def finish_mlp_kernel(idx, *rest):
    bufs = rest[:4]
    ew, rw, w, sems = rest[4:]
    copies = [pltpu.make_async_copy(b, w.at[idx[n]], sems.at[n]) for n, b in enumerate(bufs)]
    for c in copies:
        c.start()
    for c in copies:
        c.wait()

    def rows(j, q, r, n):
        if j == 0:
            return w[q, r : r + n, :].astype(f32)
        r += (2 * j - 1 + q % 2) * QM
        return w[q - q % 2, r : r + n, :].astype(f32) + w[q - q % 2 + 1, r : r + n, :].astype(f32)

    for j in range(CH):
        for b in range(EB):
            ew[:, (CH * b + j) * LANE : (CH * b + j + 1) * LANE] = rows(j, b // 4, b % 4 * RB, RB)
        for b in range(OB):
            rw[j * LANE : (j + 1) * LANE, b * LANE : (b + 1) * LANE] = rows(j, 2 + b // 3, b % 3 * LANE, LANE)


def finish_mlp_call(idx, bufs):
    return pl.pallas_call(
        finish_mlp_kernel,
        in_specs=[SMEM] + [ANY] * 4,
        out_shape=[jax.ShapeDtypeStruct((RB, FF), f32), jax.ShapeDtypeStruct((FB, D), f32)],
        scratch_shapes=[pltpu.VMEM((4,) + bufs[0].shape, bf16), pltpu.SemaphoreType.DMA((4,))],
        compiler_params=params(),
        cost_estimate=COST,
        name="finish_mlp",
    )(idx, *bufs)


def unpack_blocks(out, w, base, targets):
    for b, target in enumerate(targets):
        q, off = divmod(b * RB, QO)
        cols = slice(target * LANE, (target + 1) * LANE)
        head = min(RB, QO - off)
        out[:head, cols] = w[q, base + off : base + off + head, :].astype(f32)
        if head < RB:
            out[head:, cols] = w[q + 1, base : base + RB - head, :].astype(f32)


def finish_heads_kernel(idx, *rest):
    bufs = rest[:4]
    hw, ow, g1, b1, ob, g2, b2, rb, hb, eb, w, line, sems = rest[4:]
    copies = [pltpu.make_async_copy(b, w.at[idx[n]], sems.at[n]) for n, b in enumerate(bufs)]
    for c in copies:
        c.start()
    for c in copies:
        c.wait()
    unpack_blocks(ow, w, 0, range(OB))
    for t in range(THIRDS):
        unpack_blocks(hw, w, (1 + t) * QO, third_blocks(t))
    small = w[0, (1 + THIRDS) * QO :, :].astype(f32)
    for n, o in enumerate((g1, b1, ob, g2, b2, rb)):
        o[...] = small[n : n + 1, :RB]
    for n in range(2):
        line[:, n * RB : (n + 1) * RB] = small[6 + n : 7 + n, :RB]
    hb[...] = line[...].reshape(2 * RB)
    eb[...] = jnp.concatenate([small[8 + n : 9 + n, :] for n in range(CH)], axis=1).reshape(FB)


def finish_heads_call(idx, bufs):
    vec = jax.ShapeDtypeStruct((1, RB), f32)
    return pl.pallas_call(
        finish_heads_kernel,
        in_specs=[SMEM] + [ANY] * 4,
        out_shape=[jax.ShapeDtypeStruct((RB, 3 * D), f32), jax.ShapeDtypeStruct((RB, D), f32)]
        + [vec] * 6
        + [jax.ShapeDtypeStruct((2 * RB,), f32), jax.ShapeDtypeStruct((FB,), f32)],
        scratch_shapes=[
            pltpu.VMEM((4,) + bufs[0].shape, bf16),
            pltpu.VMEM((1, 2 * RB), f32),
            pltpu.SemaphoreType.DMA((4,)),
        ],
        compiler_params=params(),
        cost_estimate=COST,
        name="finish_heads",
    )(idx, *bufs)


def pieces_of(ref, start, n):
    parts = []
    while n:
        b, r = divmod(start, RB)
        take = min(n, RB - r)
        parts.append(ref[r : r + take, b * LANE : (b + 1) * LANE])
        start, n = start + take, n - take
    return parts


def put(out, row, parts):
    for p in parts:
        out[row : row + p.shape[0], :] = p
        row += p.shape[0]
    return row


def prepare_kernel(me, ew, rw, ow, near, far):
    def quarter(j, q):
        if q < 2:
            return [ew[:, (CH * b + j) * LANE : (CH * b + j + 1) * LANE] for b in range(4 * q, 4 * q + 4)]
        blocks = range(3 * (q - 2), 3 * (q - 2) + 3)
        return [rw[j * LANE : (j + 1) * LANE, b * LANE : (b + 1) * LANE] for b in blocks]

    for q in range(4):

        @pl.when(me[0] == q)
        def _(q=q):
            row = 0
            for p in (q - q % 2, q - q % 2 + 1):
                row = put(near, row, pieces_of(ow, p * QO, QO))
                row = put(near, row, quarter(0, p))
            put(near, row, quarter(1, q))
            row = 0
            for p in (q - q % 2, q - q % 2 + 1):
                row = put(far, row, quarter(2, p))


def prepare_heads_kernel(me, hw, g1, b1, ob, g2, b2, rb, hb, eb, heads, small):
    small[...] = jnp.zeros_like(small)
    for n, v in enumerate((g1, b1, ob, g2, b2, rb)):
        small[n : n + 1, :RB] = v[...].astype(f32)
    for n in range(2):
        small[6 + n : 7 + n, :RB] = hb[...].astype(f32).reshape(1, 2 * RB)[:, n * RB : (n + 1) * RB]
    for n in range(CH):
        small[8 + n : 9 + n, :] = eb[...].astype(f32).reshape(1, FB)[:, n * LANE : (n + 1) * LANE]


    for q in range(4):

        @pl.when(me[0] == q)
        def _(q=q):
            row = put(heads, 0, pieces_of(hw, q * QH, QH))
            heads[row:, :] = small[...].astype(bf16)


def prepare_call(q, *arrays):
    rows = 2 * (QO + QM) + QM, 2 * QM
    return pl.pallas_call(
        prepare_kernel,
        in_specs=[SMEM] + [whole(v.shape) for v in arrays],
        out_shape=[jax.ShapeDtypeStruct((n, LANE), bf16) for n in rows],
        compiler_params=params(),
        cost_estimate=COST,
        name="prepare",
    )(q, *arrays)


def prepare_heads_call(q, *arrays):
    return pl.pallas_call(
        prepare_heads_kernel,
        in_specs=[SMEM] + [whole(v.shape) for v in arrays],
        out_shape=jax.ShapeDtypeStruct((QH + SM, LANE), bf16),
        scratch_shapes=[pltpu.VMEM((SM, LANE), f32)],
        compiler_params=params(),
        cost_estimate=COST,
        name="prepare_heads",
    )(q, *arrays)


def merge_kernel(counts, *refs):
    inputs, outs = refs[: sum(counts)], refs[sum(counts) :]
    per = outs[0].shape[0]
    for i, out in enumerate(outs):

        at = row = 0
        for n in counts:
            terms = inputs[at : at + n]
            mine = slice(i * per, (i + 1) * per)
            total = terms[0][mine].astype(f32)
            for t in terms[1:]:
                total += t[mine].astype(f32)
            rows = terms[0].shape[1]
            out[:, row : row + rows, :] = total.astype(bf16)
            at += n
            row += rows


def merge_call(parts, pieces):
    slots = parts[0][0].shape[0]
    rows = sum(p[0].shape[1] for p in parts)
    flat = [v for p in parts for v in p]
    out = jax.ShapeDtypeStruct((slots // pieces, rows, LANE), bf16)
    return pl.pallas_call(
        functools.partial(merge_kernel, tuple(len(p) for p in parts)),
        out_shape=[out] * pieces,
        compiler_params=params(),
        cost_estimate=COST,
        name="merge",
    )(*flat)


def block_major(a):
    return a.reshape(a.shape[0], -1, LANE).transpose(1, 0, 2).reshape(-1, LANE)


def from_block_major(a, rows):
    return a.reshape(-1, rows, LANE).transpose(1, 0, 2).reshape(rows, -1)


def small_rows(g1, b1, hb, ob, g2, b2, eb, rb):
    return jnp.concatenate([v.reshape(NF, -1) for v in (g1, b1, hb, ob, g2, b2, eb, rb)], axis=1)


SMALL = (("g1", RB), ("b1", RB), ("hb", 2 * RB), ("ob", RB), ("g2", RB), ("b2", RB), ("eb", FB), ("rb", RB))


def split_small(sm):
    out, at = {}, 0
    for name, width in SMALL:
        out[name] = sm[:, at : at + width]
        at += width
    return out


def par_of(sm):
    s = {k: v.astype(f32) for k, v in split_small(sm).items()}
    hb = s["hb"].reshape(2 * D)
    zero = jnp.zeros((D,), f32)
    eb = s["eb"].reshape(NF, CH, LANE).transpose(1, 0, 2).reshape(CH, CW)

    def wide(v):
        return jnp.pad(v, (0, FF - v.shape[0]))

    rows = [
        s["g1"].reshape(D),
        s["b1"].reshape(D),
        jnp.concatenate([hb[:D], zero, hb[D:]]),
        s["ob"].reshape(D),
        s["g2"].reshape(D),
        s["b2"].reshape(D),
        zero,
        s["rb"].reshape(D),
        eb[0],
        eb[1],
        eb[2],
    ]
    rows += [zero] * 5
    return jnp.stack([wide(r) for r in rows])


def small_grads(seed_sum, hsums, bsums, hbsum, isums):
    eb = jnp.stack([h[0] for h in hsums]).reshape(CH, NF, LANE).transpose(1, 0, 2).reshape(FF)
    hb = jnp.concatenate([hbsum[0, :D], hbsum[0, 2 * D :]])
    return small_rows(isums[0], isums[1], hb, bsums[2], bsums[0], bsums[1], eb, seed_sum[0])


def chain(counts, ids, patches, upstream, table, hooks):
    n = patches.shape[0]
    start, xhat, seed, seed_sum = start_call(counts, table, ids.reshape(n, 1, SLOTS), patches, upstream)
    xhat = hooks.opened(xhat)
    hw, par = hooks.heads()
    xhat = hooks.at("attend", xhat)
    first, qkv, probs, mixed, whole_w = attend_call(counts, hw, xhat, par, 0, n, PER)
    mixed = hooks.at("middle", mixed)
    ow = hooks.out()
    hsums, res, dsec = [], None, None
    for j in range(CH):
        if j:
            second = hooks.at("m%d" % j, second)
            values, weights = (second, seed, res, dsec), [hooks.mlp(j)]
        else:
            values, weights = (mixed, start, seed), [hooks.mlp(0), ow]
        done = mlp_call(j, weights, hooks.order("m%d" % j), values, par)
        if j == 0:
            middle, second, *done = done
        res, dsec, hs, *pieces = done
        hsums.append(hs)
        hooks.last = hs
        hooks.grads("m%d" % j, pieces)
    dsec = hooks.at("branch", dsec)
    dmid, dmixed, bsums, *pieces = branch_call(ow, hooks.order("o"), middle, dsec, seed, mixed, par)
    hooks.grads("o", pieces)
    dprojs, tsums = [], []
    for t in range(THIRDS):
        dmixed = hooks.at("h%d" % t, dmixed)
        dproj, tsum, *pieces = attend_back_call(t, hooks.order("h%d" % t), qkv, probs, dmixed, first)
        dprojs.append(dproj)
        tsums.append(tsum)
        hooks.grads("h%d" % t, pieces)
    dmid = hooks.at("input", dmid)
    pgrad, isums = input_call(whole_w, dprojs, start, dmid, par)
    grads = hooks.finish(seed_sum, *hsums, bsums, *tsums, isums)
    return res.reshape(n, SLOTS, D), pgrad.reshape(n, SLOTS, D), grads


class Plain:
    def __init__(self, args):
        self.full = {k: lax.all_gather(v, "fsdp", axis=0, tiled=True) for k, v in args.items()}
        self.idx = jnp.arange(4 * NF, dtype=jnp.int32)
        self.got = {}

    def order(self, name):
        return self.idx, NF

    def pieces(self, a, quarter):
        plan = tuple((q, 0, 0, quarter) for q in range(4))
        return self.idx, [a[:, q * quarter : (q + 1) * quarter] for q in range(4)], plan

    def at(self, name, value):
        return value

    def opened(self, xhat):
        return xhat

    def heads(self):
        f = self.full
        sm = small_rows(*(f[k] for k, _ in SMALL))
        w = jax.vmap(block_major)(f["hw"].reshape(NF, RB, 3 * D))
        return self.pieces(w, QH), par_of(sm)

    def out(self):
        return self.pieces(jax.vmap(block_major)(self.full["ow"].reshape(NF, RB, D)), QO)

    def mlp(self, j):
        e = self.full["ew"].reshape(NF, RB, NF, CH, LANE)[:, :, :, j].transpose(0, 2, 1, 3)
        r = self.full["rw"].reshape(NF, CH, LANE, OB, LANE)[:, j].transpose(0, 2, 1, 3)
        w = jnp.concatenate([e.reshape(NF, -1, LANE), r.reshape(NF, -1, LANE)], axis=1)
        return self.pieces(w, QM)

    def grads(self, name, pieces):
        self.got[name] = jnp.concatenate(pieces, axis=1)

    def finish(self, seed_sum, h0, h1, h2, bsums, t0, t1, t2, isums):
        hbsum = jnp.concatenate([t[:, p * WT : (p + 1) * WT] for p in range(3) for t in (t0, t1, t2)], axis=1)
        smalls = small_grads(seed_sum, (h0, h1, h2), bsums, hbsum, isums)
        g = self.got
        hs = jnp.stack([g["h%d" % t].reshape(NF, 3, PT, RB, LANE) for t in range(THIRDS)])
        hw = hs.transpose(1, 4, 2, 0, 3, 5).reshape(D, 3 * D)
        ow = jax.vmap(lambda a: from_block_major(a, RB))(g["o"]).reshape(D, D)
        e = jnp.stack([g["m%d" % j][:, : EB * RB].reshape(NF, NF, RB, LANE) for j in range(CH)])
        ew = e.transpose(1, 3, 2, 0, 4).reshape(D, FF)
        r = jnp.stack([g["m%d" % j][:, EB * RB :].reshape(NF, OB, LANE, LANE) for j in range(CH)])
        rw = r.transpose(1, 0, 3, 2, 4).reshape(FF, D)
        s = {k: v.reshape(-1) for k, v in split_small(smalls).items()}
        s.update(hw=hw, ow=ow, ew=ew, rw=rw)

        def total(v):
            part = lax.psum_scatter(v.astype(bf16), "fsdp", scatter_dimension=0, tiled=True)
            return lax.psum(part, "rep").astype(f32)

        return {k: total(v) for k, v in s.items()}


NR = 4


def moves(dy, dc, dz, dx):
    pairs = []
    for rep in range(NR):
        for f in range(NF):
            to = (rep // 2 ^ dy) * 2 + (rep % 2 ^ dc)
            at = (f // 2 ^ dz) * 2 + (f % 2 ^ dx)
            pairs.append((rep * NF + f, to * NF + at))
    return pairs


def send(a, dy=0, dc=0, dz=0, dx=0):
    return lax.ppermute(a, ("rep", "fsdp"), moves(dy, dc, dz, dx))


def to_core(a):
    return send(a, dc=1)


def together(*values):
    return lax.optimization_barrier(values)


HS = (QH + SM) // 2
NS = QO + 112


def gathered(a):
    return lax.all_gather(a[None], "fsdp", axis=0, tiled=True)


class Fast:
    def __init__(self, args):
        rep, f = lax.axis_index("rep"), lax.axis_index("fsdp")
        self.y, self.c, self.z, self.x = rep // 2, rep % 2, f // 2, f % 2
        q = 2 * self.c + self.y
        self.g, self.moves = {}, {}
        self.quarters = jnp.stack([q, q ^ 1, q ^ 2, q ^ 3]).astype(jnp.int32)
        me = q.astype(jnp.int32).reshape(1)
        hw = prepare_heads_call(
            me, args["hw"], *(args[k].reshape(1, -1) for k in SEGMENTS), args["hb"], args["eb"]
        )
        hw, ow = together(hw, args["ow"])
        near, far = prepare_call(me, args["ew"], args["rw"], ow)
        self.near, self.far = gathered(near), gathered(far)
        self.hz = [hw] + [send(hw, dz=k) for k in (1, 2, 3)]

    def halves(self, pieces, row):
        return jnp.stack([v[:row] for v in pieces]), jnp.stack([v[row:] for v in pieces])

    def round_one(self, a, b):
        return jnp.concatenate([a, send(a, dx=1)], axis=0), jnp.concatenate([b, send(b, dy=1)], axis=0)

    def round_two(self, a, b):
        return send(a, dy=1), send(b, dx=1)

    def opened(self, xhat):
        xhat, *hz = together(xhat, *self.hz)
        a, b = self.round_one(*self.halves(hz, HS))
        a2, b2 = self.round_two(a, b)
        self.h = [a, a2, b, b2] + [to_core(v) for v in (a, a2, b, b2)]
        return xhat

    def places(self, order):
        place = []
        for dc in range(2):
            for i in range(2):
                for j in range(2):
                    d = dict(zip(order, (i, j)))
                    for dz in range(4):
                        q = 2 * (self.c ^ dc) + (self.y ^ d["y"])
                        place.append(q * NF + (self.z ^ dz) * 2 + (self.x ^ d["x"]))
        return jnp.stack(place).astype(jnp.int32)

    def heads(self):
        a, b, n = self.places("yx"), self.places("xy"), 2 * NF
        idx = jnp.concatenate([a[:n], b[:n], a[n:], b[n:]])
        one, two = (0, 0, HS), (0, HS, QH - HS)
        plan = tuple((n,) + (one if n % 4 < 2 else two) for n in range(8))
        at = jnp.concatenate([b[:4], b[8:12]]) % NF
        par = par_call(at, self.h[2], self.h[3], QH - HS)
        return (idx, self.h, plan), par

    def at(self, name, value):
        g = self.g
        if name == "middle":
            value, near = together(value, self.near)
            self.near = [near, to_core(near)]
            self.c1 = send(near[:, 2 * (QO + QM) :], dy=1)
        if name == "m1":
            self.last, c1 = together(self.last, self.c1)
            self.c1 = [c1, to_core(c1)]
        if name == "m2":
            self.last, far = together(self.last, self.far)
            self.far = [far, to_core(far)]
            value = self.hold(value, self.added("m0"))
            self.y0 = send(g["m0"][1], dy=1)
        if name == "branch":
            parts = [g["m0"][0] + self.y0, *self.added("m1", keep=True), *self.added("m2", keep=True)]
            value, parts = together(value, jnp.concatenate(parts, axis=1))
            self.m = lax.psum_scatter(parts, "fsdp", scatter_dimension=0, tiled=True)[0]
        if name == "h2":
            g["near"] = merge_call([g["o"], g["h0"]], 2)
            value = self.hold(value, "near")
            self.xn = send(g["near"][1], dx=1)
        if name == "input":
            far = merge_call([g["h1"], g["h2"]], 4)
            near = g["near"][0]
            near = [near[:4] + self.xn[:4], near[4:] + self.xn[4:]]
            value, *both = together(value, *near, *far)
            self.near = [both[0], send(both[1], dy=1)]
            self.far = self.across_back(both[2:])
        return value

    def hold(self, value, *names):
        flat = [v for name in names for v in self.g[name]]
        value, *flat = together(value, *flat)
        for name in names:
            n = len(self.g[name])
            self.g[name], flat = flat[:n], flat[n:]
        return value

    def across_back(self, a):
        return [a[0], send(a[1], dx=1), send(a[2], dy=1), send(a[3], dx=1, dy=1)]

    def spread_z(self, c):
        return [c[0]] + [send(c[k], dz=k) for k in (1, 2, 3)]

    def added(self, name, keep=False):
        a, b = self.g[name]
        n = a.shape[0] // 2
        parts = [a[:n] + b[:n], a[n:] + b[n:]]
        if keep:
            return parts
        self.g[name] = parts
        return name

    def even_places(self):
        q = 2 * (self.c ^ jnp.arange(2)[:, None, None]) + jnp.arange(2)[:, None]
        return (q * NF + jnp.arange(NF)).reshape(-1).astype(jnp.int32)

    def plan(self, rows, row, n):
        return self.even_places(), tuple((dc, y * rows + row, 0, n) for dc in range(2) for y in range(2))

    def out(self):
        idx, plan = self.plan(QO + QM, 0, QO)
        self.w = self.near
        return idx, self.w, plan

    def mlp(self, j):
        if j == 2:
            idx, plan = self.plan(QM, 0, QM)
            return idx, self.far, plan
        if j == 0:
            idx, plan = self.plan(QO + QM, QO, QM)
            return idx, self.w, plan
        side, row = jnp.arange(2)[:, None, None], 2 * (QO + QM)
        q = 2 * (self.c ^ side) + (self.y ^ side.reshape(2, 1))
        idx = (q * NF + jnp.arange(NF)).reshape(-1).astype(jnp.int32)
        return idx, [self.w[0], self.c1[0], self.w[1], self.c1[1]], ((0, row, 0, QM), (1, 0, 0, QM), (2, row, 0, QM), (3, 0, 0, QM))

    def order(self, name):
        if name[0] == "m":
            side = jnp.arange(2)[:, None]
            q = 2 * (self.c ^ jnp.arange(2)[:, None, None]) + (self.y ^ side if name == "m0" else side)
            return (q * NF + jnp.arange(NF)).reshape(-1).astype(jnp.int32), 2 * NF
        return self.places("xy" if name in ("o", "h0") else "yx"), 2 * NF

    def grads(self, name, pieces):
        keep, go = pieces
        if name == "m2":
            go, self.y0 = together(go, self.y0)
        if name == "h2":
            go, self.xn = together(go, self.xn)
        self.g[name] = [keep, to_core(go)]

    def whole_shard(self, own):
        across = send(own, dy=1)
        return [own, across, to_core(own), to_core(across)]

    def finish(self, *sums):
        sums = list(sums)
        *self.far, self.near[1], sums[-1] = together(*self.far, self.near[1], sums[-1])
        s = small_grad_call(self.places("yx")[:8] % NF, *sums)
        s = merge_call([[s, to_core(s)]], 2)
        s = self.across_back([s[0], s[1], s[0], s[1]])
        last = self.spread_z(merge_call([self.near, self.far, s], 4))
        m, last[0] = together(self.m, last[0])
        across = send(m, dy=1)
        last, m, across = together(merge_call([last], 1)[0][0], m, across)
        ew, rw = finish_mlp_call(self.quarters, [m, across, to_core(m), to_core(across)])
        over, ew, rw = together(send(last, dy=1), ew, rw)
        last = [last, over, to_core(last), to_core(over)]
        hw, ow, g1, b1, ob, g2, b2, rb, hb, eb = finish_heads_call(self.quarters, last)
        out = dict(hw=hw, ow=ow, ew=ew, rw=rw)
        out.update(g1=g1, b1=b1, hb=hb, ob=ob, g2=g2, b2=b2, eb=eb, rb=rb)
        return {k: v if k[1] == "w" else v.reshape(-1) for k, v in out.items()}


NAMES = ("g1", "b1", "hw", "hb", "ow", "ob", "g2", "b2", "ew", "eb", "rw", "rb")


def body(fast, patches, visible_count, patch_index, *rest):
    args = dict(zip(NAMES, rest[:12]))
    upstream = rest[12]
    hooks = (Fast if fast else Plain)(args)
    out, pgrad, g = chain(visible_count, patch_index, patches, upstream, frequency_table(), hooks)
    return (out, pgrad) + tuple(g[k] for k in NAMES)


def solution(mesh):
    rows = P(("rep", "fsdp"), None, None)
    mat, vec = P("fsdp", None), P("fsdp")
    weights = tuple(mat if k[1] == "w" else vec for k in NAMES)
    fast = mesh.shape["fsdp"] == NF and mesh.shape["rep"] == 4
    return jax.shard_map(
        functools.partial(body, fast),
        mesh=mesh,
        in_specs=(rows, P(("rep", "fsdp")), P(("rep", "fsdp"), None)) + weights + (rows,),
        out_specs=(rows, rows) + weights,
        check_vma=False,
    )
```

```python
import functools

import numpy as np
import jax
import jax.numpy as jnp
from jax import lax
from jax.experimental import pallas as pl
from jax.experimental.pallas import tpu as pltpu
from jax.sharding import PartitionSpec as P

D = 768
FF = 3072
HEADS = 12
HEAD_DIM = 64
SLOTS = 80
GRID = 14
NF = 8
RB = D // NF
FB = FF // NF
CH = 3
CW = FF // CH
LANE = 128
HB = 3 * D // LANE
OB = D // LANE
EB = CW // LANE
QH = HB * RB // 4
QO = OB * RB // 4
QM = (EB * RB + OB * LANE) // 4
SM = 16

EPS = 1e-06
NEG = -1e30
bf16 = jnp.bfloat16
f32 = jnp.float32
NN = (((1,), (0,)), ((), ()))
NT = (((1,), (1,)), ((), ()))
TN = (((0,), (0,)), ((), ()))
VMEM_LIMIT = 63 << 20
PER = 4
COST = pl.CostEstimate(flops=1000, bytes_accessed=1000, transcendentals=0)


def mm(a, b, dims):
    return lax.dot_general(a, b, dims, preferred_element_type=f32)


def params(limit=VMEM_LIMIT):
    return pltpu.CompilerParams(vmem_limit_bytes=limit)


def whole(shape):
    return pl.BlockSpec(shape, lambda *_: (0,) * len(shape))


ANY = pl.BlockSpec(memory_space=pl.ANY)
SMEM = pl.BlockSpec(memory_space=pltpu.SMEM)


def block_of(w, base, quarter, start, n):
    q, off = divmod(start, quarter)
    if off + n <= quarter:
        return w[q, :, base + off : base + off + n, :].reshape(NF * n, LANE)
    head = quarter - off
    return jnp.concatenate(
        [w[q, :, base + off : base + quarter, :], w[q + 1, :, base : base + n - head, :]], axis=1
    ).reshape(NF * n, LANE)


def put_block(w, base, quarter, start, n, value):
    value = value.reshape(NF, n, LANE)
    q, off = divmod(start, quarter)
    if off + n <= quarter:
        w[q, :, base + off : base + off + n, :] = value
    else:
        head = quarter - off
        w[q, :, base + off : base + quarter, :] = value[:, :head]
        w[q + 1, :, base : base + n - head, :] = value[:, head:]


def columns(w, base, quarter, rows, blocks):
    return jnp.concatenate([block_of(w, base, quarter, b * rows, rows) for b in blocks], axis=1)


def put_columns(w, base, quarter, rows, blocks, value):
    for i, b in enumerate(blocks):
        put_block(w, base, quarter, b * rows, rows, value[:, i * LANE : (i + 1) * LANE])


def piece_copies(bufs, plan, idx, w, sems):
    copies = []
    for buf, source, target, rows in plan:
        for k in range(bufs[buf].shape[0]):
            n = len(copies)
            copies.append(
                pltpu.make_async_copy(
                    bufs[buf].at[k, pl.ds(source, rows)],
                    w.at[idx[n] // NF, idx[n] % NF, pl.ds(target, rows)],
                    sems.at[n],
                )
            )
    return copies


def n_copies(bufs, plan):
    return sum(bufs[entry[0]].shape[0] for entry in plan)


def send_copies(stage, idx, outs, sems):
    copies = []
    for out in outs:
        for k in range(out.shape[0]):
            n = len(copies)
            copies.append(
                pltpu.make_async_copy(stage.at[idx[n] // NF, idx[n] % NF], out.at[k], sems.at[n])
            )
    return copies


def frequency_table():
    quarter = D // 4
    frequency = 1.0 / 10000.0 ** (jnp.arange(quarter, dtype=f32) / quarter)
    angle = jnp.arange(16, dtype=f32)[:, None] * frequency
    table = jnp.concatenate([jnp.sin(angle), jnp.cos(angle)], axis=-1)
    high = table.astype(bf16)
    rest = table - high.astype(f32)
    middle = rest.astype(bf16)
    low = (rest - middle.astype(f32)).astype(bf16)
    return jnp.concatenate([high, middle, low], axis=0)


def normalised(v):
    c = v - jnp.mean(v, axis=-1, keepdims=True)
    r = lax.rsqrt(jnp.mean(c * c, axis=-1, keepdims=True) + EPS)
    return c * r, r


def norm_back(xhat, r, gain, d):
    e = gain * d
    return r * (
        e - jnp.mean(e, axis=-1, keepdims=True) - xhat * jnp.mean(e * xhat, axis=-1, keepdims=True)
    )


def start_kernel(G, cnt, table, ids, patches, upstream, start, xhat, seed, seed_sum):
    step = pl.program_id(0)

    @pl.when(step == 0)
    def _():
        seed_sum[...] = jnp.zeros_like(seed_sum)

    tab = table[...]
    place = lax.broadcasted_iota(jnp.int32, (48, SLOTS), 0) % 16
    row = lax.broadcasted_iota(jnp.int32, (SLOTS, D), 0)
    total = jnp.zeros((SLOTS, D), f32)
    for g in range(G):
        pid = ids[g]
        by_row = jnp.where(place == pid // GRID, 1.0, 0.0).astype(bf16)
        by_col = jnp.where(place == pid % GRID, 1.0, 0.0).astype(bf16)
        position = jnp.concatenate([mm(by_row, tab, TN), mm(by_col, tab, TN)], axis=1)
        v = patches[g].astype(f32) + position
        here = pl.ds(g * SLOTS, SLOTS)
        start[here, :] = v
        xhat[here, :] = normalised(v)[0]
        s = jnp.where(row < cnt[step * G + g], upstream[g].astype(f32), 0.0)
        seed[here, :] = s.astype(bf16)
        total += s
    seed_sum[...] += jnp.sum(total, axis=0, keepdims=True)


def start_call(counts, table, ids, patches, upstream):
    n = patches.shape[0]
    G = 4 if n % 4 == 0 else 1
    rows = n * SLOTS
    blk = pl.BlockSpec((G * SLOTS, D), lambda i: (i, 0))
    img = pl.BlockSpec((G, SLOTS, D), lambda i: (i, 0, 0))
    return pl.pallas_call(
        functools.partial(start_kernel, G),
        grid=(n // G,),
        in_specs=[SMEM, whole(table.shape), pl.BlockSpec((G, 1, SLOTS), lambda i: (i, 0, 0)), img, img],
        out_specs=[blk, blk, blk, whole((1, D))],
        out_shape=[
            jax.ShapeDtypeStruct((rows, D), f32),
            jax.ShapeDtypeStruct((rows, D), f32),
            jax.ShapeDtypeStruct((rows, D), bf16),
            jax.ShapeDtypeStruct((1, D), f32),
        ],
        compiler_params=params(),
        cost_estimate=COST,
        name="start",
    )(counts, table, ids, patches, upstream)


def head_masks():
    lane = lax.broadcasted_iota(jnp.int32, (SLOTS, LANE), 1)
    return lane < HEAD_DIM


def both_heads(x, left):
    zero = jnp.zeros_like(x)
    return jnp.concatenate([jnp.where(left, x, zero), jnp.where(left, zero, x)], axis=0)


def attend_kernel(G, base, plan, nbuf, cnt, idx, xhat, par, *rest):
    bufs = rest[:nbuf]
    first, qkv, probs, mixed, whole_w, w, sems, wsem = rest[nbuf:]
    step = pl.program_id(0)

    @pl.when(step == 0)
    def _():
        copies = piece_copies(bufs, plan, idx, w, sems)
        for c in copies:
            c.start()
        for c in copies:
            c.wait()
        pltpu.make_async_copy(w, whole_w, wsem.at[0]).start()

    x = (xhat[...] * par[0:1, :D] + par[1:2, :D]).astype(bf16)
    first[...] = x
    for part in range(3):
        cols = slice(part * D, (part + 1) * D)
        wp = columns(w, 0, QH, RB, range(part * OB, (part + 1) * OB))
        qkv[:, cols] = (mm(x, wp, NN) + par[2:3, cols]).astype(bf16)
    left = head_masks()
    key = lax.broadcasted_iota(jnp.int32, (SLOTS, SLOTS), 0)

    todo = []
    for g in range(G):
        live = key < cnt[base + step * G + g]
        rows = slice(g * SLOTS, (g + 1) * SLOTS)
        todo += [(g, p, rows, p * LANE, live) for p in range(HEADS // 2)]
    scores = [
        mm(both_heads(qkv[rows, D + c : D + c + LANE], left), qkv[rows, c : c + LANE], NT)
        for _, _, rows, c, _ in todo
    ]
    pts = []
    for s, (_, _, _, _, live) in zip(scores, todo):
        halves = []
        for h in range(2):
            sh = jnp.where(live, s[h * SLOTS : (h + 1) * SLOTS] * HEAD_DIM**-0.5, NEG)
            e = jnp.exp(sh - jnp.max(sh, axis=0, keepdims=True))
            halves.append(e * (1.0 / jnp.sum(e, axis=0, keepdims=True)))
        pts.append(jnp.concatenate(halves, axis=0).astype(bf16))
    for pt, (g, p, rows, c, _) in zip(pts, todo):
        probs[g, p] = pt
        v = both_heads(qkv[rows, 2 * D + c : 2 * D + c + LANE], left)
        mixed[rows, c : c + LANE] = mm(pt, v, TN).astype(bf16)

    @pl.when(step == pl.num_programs(0) - 1)
    def _():
        pltpu.make_async_copy(w, whole_w, wsem.at[0]).wait()


def attend_call(counts, w, xhat, par, base, n, G):
    idx, bufs, plan = w
    rows = n * SLOTS
    skip = base // G

    def blk(width):
        return pl.BlockSpec((G * SLOTS, width), lambda i: (i, 0))

    return pl.pallas_call(
        functools.partial(attend_kernel, G, base, plan, len(bufs)),
        grid=(n // G,),
        in_specs=[SMEM, SMEM, pl.BlockSpec((G * SLOTS, D), lambda i: (i + skip, 0)), whole(par.shape)] + [ANY] * len(bufs),
        out_specs=[
            blk(D),
            blk(3 * D),
            pl.BlockSpec((G, HEADS // 2, 2 * SLOTS, SLOTS), lambda i: (i, 0, 0, 0)),
            blk(D),
            ANY,
        ],
        out_shape=[
            jax.ShapeDtypeStruct((rows, D), bf16),
            jax.ShapeDtypeStruct((rows, 3 * D), bf16),
            jax.ShapeDtypeStruct((n, HEADS // 2, 2 * SLOTS, SLOTS), bf16),
            jax.ShapeDtypeStruct((rows, D), bf16),
            jax.ShapeDtypeStruct((4, NF, QH, LANE), bf16),
        ],
        scratch_shapes=[
            pltpu.VMEM((4, NF, QH, LANE), bf16),
            pltpu.SemaphoreType.DMA((n_copies(bufs, plan),)),
            pltpu.SemaphoreType.DMA((1,)),
        ],
        compiler_params=params(),
        cost_estimate=COST,
        name="attend",
    )(counts, idx, xhat, par, *bufs)


def row_block(rows):
    return 240 if rows % 240 == 0 else SLOTS


def middle_call(w, mixed, start, par):
    idx, bufs, plan = w
    rows = mixed.shape[0]
    B = row_block(rows)
    blk = pl.BlockSpec((B, D), lambda i: (i, 0))
    return pl.pallas_call(
        functools.partial(middle_kernel, plan, len(bufs)),
        grid=(rows // B,),
        in_specs=[SMEM, blk, blk, whole(par.shape)] + [ANY] * len(bufs),
        out_specs=[blk, blk],
        out_shape=[jax.ShapeDtypeStruct((rows, D), f32), jax.ShapeDtypeStruct((rows, D), bf16)],
        scratch_shapes=[
            pltpu.VMEM((4, NF, QO, LANE), bf16),
            pltpu.SemaphoreType.DMA((4 * NF,)),
        ],
        compiler_params=params(),
        cost_estimate=COST,
        name="middle",
    )(idx, mixed, start, par, *bufs)


def gelu_and_slope(h):
    a = jnp.abs(h)
    e = jnp.exp(-0.5 * (h * h))
    t = 1.0 / (1.0 + 0.23164189 * a)
    poly = t * (
        0.127414796
        + t * (-0.142248368 + t * (0.7107068705 + t * (-0.7265760135 + t * 0.5307027145)))
    )
    tail = poly * e
    phi = jnp.where(h >= 0, 1.0 - tail, tail)
    return h * phi, phi + h * e * 0.3989422804014327


def mlp_kernel(chunk, n_out, plans, counts, *refs):
    fresh = chunk == 0
    refs = list(refs)

    def take(n):
        out, refs[:] = refs[:n], refs[n:]
        return out

    (oidx,) = take(1)
    loads = [(plan, *take(1), take(n)) for plan, n in zip(plans, counts)]
    if fresh:
        mixed, start, seed, par, middle, second, res, dsec, hsum = take(9)
    else:
        second, seed, res_in, dsec_in, par, res, dsec, hsum = take(8)
    outs = take(n_out)
    ws = take(len(loads))
    ge, gr, stage, sems, osems = refs
    w = ws[0]
    step = pl.program_id(0)
    half = EB // 2

    def work(first, last):
        if first:
            copies, at = [], 0
            for (plan, idx, bufs), place in zip(loads, ws):
                n = n_copies(bufs, plan)
                copies += piece_copies(bufs, plan, idx, place, sems.at[pl.ds(at, n)])
                at += n
            for c in copies:
                c.start()
            for c in copies:
                c.wait()
        s = seed[...]
        if fresh:
            m = start[...] + mm(mixed[...], columns(ws[1], 0, QO, RB, range(OB)), NN) + par[3:4, :D]
            middle[...] = m
            x = (normalised(m)[0] * par[4:5, :D] + par[5:6, :D]).astype(bf16)
            second[...] = x
            acc, dacc = m + par[7:8, :D], None
        else:
            x = second[...]
            acc, dacc = res_in[...], dsec_in[...]
        for t in range(2):
            we = columns(w, 0, QM, RB, range(t * half, (t + 1) * half))
            fs = slice(t * half, (t + 1) * half)
            wr = jnp.concatenate(
                [
                    w[2 + b // 3, fs, (b % 3) * LANE : (b % 3 + 1) * LANE, :].reshape(half * LANE, LANE)
                    for b in range(OB)
                ],
                axis=1,
            )
            cols = slice(t * half * LANE, (t + 1) * half * LANE)
            h = mm(x, we, NN) + par[8 + chunk : 9 + chunk, cols]
            active, slope = gelu_and_slope(h)
            a = active.astype(bf16)
            d = (mm(s, wr, NT) * slope).astype(bf16)
            sums = jnp.sum(d.astype(f32), axis=0, keepdims=True)
            hsum[0:1, cols] = sums if first else hsum[0:1, cols] + sums
            acc = acc + mm(a, wr, NN)
            g = mm(d, we, NT)
            dacc = g if dacc is None else dacc + g
            e, r = mm(x, d, TN), mm(a, s, TN)
            if not first:
                e, r = e + ge[:, cols], r + gr[cols, :]
            if last:
                for i in range(half):
                    b = t * half + i
                    stage[b // 4, :, (b % 4) * RB : (b % 4 + 1) * RB, :] = (
                        e[:, i * LANE : (i + 1) * LANE].astype(bf16).reshape(NF, RB, LANE)
                    )
                for b in range(OB):
                    stage[2 + b // 3, fs, (b % 3) * LANE : (b % 3 + 1) * LANE, :] = (
                        r[:, b * LANE : (b + 1) * LANE].astype(bf16).reshape(half, LANE, LANE)
                    )
            else:
                ge[:, cols], gr[cols, :] = e, r
        if last:
            copies = send_copies(stage, oidx, outs, osems)
            for c in copies:
                c.start()
        res[...] = acc.astype(res.dtype)
        dsec[...] = dacc
        if last:
            for c in copies:
                c.wait()

    end = pl.num_programs(0) - 1
    pl.when(step == 0)(functools.partial(work, True, False))
    pl.when((step > 0) & (step < end))(functools.partial(work, False, False))
    pl.when(step == end)(functools.partial(work, False, True))


def mlp_call(chunk, weights, order, values, par):
    oidx, per = order
    rows = values[0].shape[0]
    B = row_block(rows)
    fresh, last = chunk == 0, chunk == CH - 1
    blk = pl.BlockSpec((B, D), lambda i: (i, 0))
    pieces = [jax.ShapeDtypeStruct((per, QM, LANE), bf16)] * (4 * NF // per)

    def out(kind):
        return jax.ShapeDtypeStruct((rows, D), kind)

    outs = ([out(f32), out(bf16)] if fresh else []) + [out(bf16 if last else f32), out(f32)]
    loads, specs = [], []
    for idx, bufs, _ in weights:
        loads += [idx, *bufs]
        specs += [SMEM] + [ANY] * len(bufs)
    return pl.pallas_call(
        functools.partial(
            mlp_kernel, chunk, len(pieces), tuple(w[2] for w in weights), tuple(len(w[1]) for w in weights)
        ),
        grid=(rows // B,),
        in_specs=[SMEM] + specs + [blk] * len(values) + [whole(par.shape)],
        out_specs=[blk] * len(outs) + [whole((1, CW))] + [ANY] * len(pieces),
        out_shape=outs + [jax.ShapeDtypeStruct((1, CW), f32)] + pieces,
        scratch_shapes=[pltpu.VMEM((4, NF, n, LANE), bf16) for n in (QM, QO)[: len(weights)]]
        + [
            pltpu.VMEM((D, CW), f32),
            pltpu.VMEM((CW, D), f32),
            pltpu.VMEM((4, NF, QM, LANE), bf16),
            pltpu.SemaphoreType.DMA((sum(n_copies(w[1], w[2]) for w in weights),)),
            pltpu.SemaphoreType.DMA((4 * NF,)),
        ],
        compiler_params=params(),
        cost_estimate=COST,
        name="mlp",
    )(oidx, *loads, *values, par)


def branch_kernel(plan, nbuf, idx, oidx, middle, dsec, seed, mixed, par, *rest):
    bufs = rest[:nbuf]
    dmid, dmixed, sums = rest[nbuf : nbuf + 3]
    outs = rest[nbuf + 3 : -5]
    w, acc, stage, sems, osems = rest[-5:]
    step = pl.program_id(0)

    @pl.when(step == 0)
    def _():
        copies = piece_copies(bufs, plan, idx, w, sems)
        for c in copies:
            c.start()
        acc[...] = jnp.zeros_like(acc)
        sums[...] = jnp.zeros_like(sums)
        for c in copies:
            c.wait()

    d = dsec[...]
    xhat, r = normalised(middle[...])
    dm = seed[...].astype(f32) + norm_back(xhat, r, par[4:5, :D], d)
    db = dm.astype(bf16)
    dmid[...] = db
    sums[0:1, :] += jnp.sum(d * xhat, axis=0, keepdims=True)
    sums[1:2, :] += jnp.sum(d, axis=0, keepdims=True)
    sums[2:3, :] += jnp.sum(db.astype(f32), axis=0, keepdims=True)
    acc[...] += mm(mixed[...], db, TN)
    dmixed[...] = mm(db, columns(w, 0, QO, RB, range(OB)), NT).astype(bf16)

    @pl.when(step == pl.num_programs(0) - 1)
    def _():
        put_columns(stage, 0, QO, RB, range(OB), acc[...].astype(bf16))
        copies = send_copies(stage, oidx, outs, osems)
        for c in copies:
            c.start()
        for c in copies:
            c.wait()


def branch_call(w, order, middle, dsec, seed, mixed, par):
    idx, bufs, plan = w
    oidx, per = order
    pieces = [jax.ShapeDtypeStruct((per, QO, LANE), bf16)] * (4 * NF // per)
    rows = mixed.shape[0]
    B = row_block(rows)
    blk = pl.BlockSpec((B, D), lambda i: (i, 0))
    return pl.pallas_call(
        functools.partial(branch_kernel, plan, len(bufs)),
        grid=(rows // B,),
        in_specs=[SMEM, SMEM, blk, blk, blk, blk, whole(par.shape)] + [ANY] * len(bufs),
        out_specs=[blk, blk, whole((8, D))] + [ANY] * len(pieces),
        out_shape=[
            jax.ShapeDtypeStruct((rows, D), bf16),
            jax.ShapeDtypeStruct((rows, D), bf16),
            jax.ShapeDtypeStruct((8, D), f32),
        ]
        + pieces,
        scratch_shapes=[
            pltpu.VMEM((4, NF, QO, LANE), bf16),
            pltpu.VMEM((D, D), f32),
            pltpu.VMEM((4, NF, QO, LANE), bf16),
            pltpu.SemaphoreType.DMA((4 * NF,)),
            pltpu.SemaphoreType.DMA((4 * NF,)),
        ],
        compiler_params=params(),
        cost_estimate=COST,
        name="branch",
    )(idx, oidx, middle, dsec, seed, mixed, par, *bufs)


THIRDS = 3
PT = HEADS // 2 // THIRDS
WT = PT * LANE


def attend_back_kernel(G, oidx, q_ref, k_ref, v_ref, probs, dmixed, first, *rest):
    dproj, sums = rest[:2]
    outs = rest[2:-3]
    acc, stage, osems = rest[-3:]
    step = pl.program_id(0)

    @pl.when(step == 0)
    def _():
        acc[...] = jnp.zeros_like(acc)
        sums[...] = jnp.zeros_like(sums)

    left = head_masks()
    scale = HEAD_DIM**-0.5

    todo = []
    for g in range(G):
        rows = slice(g * SLOTS, (g + 1) * SLOTS)
        for p in range(PT):
            todo.append((g, p, rows, slice(p * LANE, (p + 1) * LANE)))
    dos = [dmixed[rows, c] for _, _, rows, c in todo]
    pts = [probs[i, p] for i, p, _, _ in todo]
    dps = [
        mm(both_heads(v_ref[rows, c], left), do, NT) for (_, _, rows, c), do in zip(todo, dos)
    ]
    dvs = [mm(pt, do, NN) for pt, do in zip(pts, dos)]
    dss = []
    for pt, dp in zip(pts, dps):
        prob = pt.astype(f32)
        parts = []
        for h in range(2):
            ph = prob[h * SLOTS : (h + 1) * SLOTS]
            dh = dp[h * SLOTS : (h + 1) * SLOTS]
            parts.append(ph * (dh - jnp.sum(ph * dh, axis=0, keepdims=True)))
        dss.append(jnp.concatenate(parts, axis=0).astype(bf16))
    dks = [mm(ds, q_ref[rows, c], NN) for ds, (_, _, rows, c) in zip(dss, todo)]
    dqs = [mm(ds, both_heads(k_ref[rows, c], left), TN) for ds, (_, _, rows, c) in zip(dss, todo)]
    for (_, p, rows, c), dq, dk2, dv2 in zip(todo, dqs, dks, dvs):
        dk = jnp.where(left, dk2[:SLOTS], dk2[SLOTS:]) * scale
        dv = jnp.where(left, dv2[:SLOTS], dv2[SLOTS:])
        dproj[rows, p * LANE : (p + 1) * LANE] = (dq * scale).astype(bf16)
        dproj[rows, WT + p * LANE : WT + (p + 1) * LANE] = dk.astype(bf16)
        dproj[rows, 2 * WT + p * LANE : 2 * WT + (p + 1) * LANE] = dv.astype(bf16)

    dall = dproj[...]
    sums[0:1, :] += jnp.sum(dall.astype(f32), axis=0, keepdims=True)
    acc[...] += mm(first[...], dall, TN)

    @pl.when(step == pl.num_programs(0) - 1)
    def _():
        put_columns(stage, 0, QO, RB, range(OB), acc[...].astype(bf16))
        copies = send_copies(stage, oidx, outs, osems)
        for c in copies:
            c.start()
        for c in copies:
            c.wait()


def attend_back_call(t, order, qkv, probs, dmixed, first, G=6):
    oidx, per = order
    rows = first.shape[0]
    n = rows // SLOTS
    G = G if n % G == 0 else 2
    pieces = [jax.ShapeDtypeStruct((per, QO, LANE), bf16)] * (4 * NF // per)

    def blk(width, col):
        return pl.BlockSpec((G * SLOTS, width), lambda i: (i, col))

    return pl.pallas_call(
        functools.partial(attend_back_kernel, G),
        grid=(n // G,),
        in_specs=[
            SMEM,
            blk(WT, t),
            blk(WT, THIRDS + t),
            blk(WT, 2 * THIRDS + t),
            pl.BlockSpec((G, PT, 2 * SLOTS, SLOTS), lambda i: (i, t, 0, 0)),
            blk(WT, t),
            blk(D, 0),
        ],
        out_specs=[blk(3 * WT, 0), whole((8, 3 * WT))] + [ANY] * len(pieces),
        out_shape=[jax.ShapeDtypeStruct((rows, 3 * WT), bf16), jax.ShapeDtypeStruct((8, 3 * WT), f32)]
        + pieces,
        scratch_shapes=[
            pltpu.VMEM((D, 3 * WT), f32),
            pltpu.VMEM((4, NF, QO, LANE), bf16),
            pltpu.SemaphoreType.DMA((4 * NF,)),
        ],
        compiler_params=params(),
        cost_estimate=COST,
        name="attend_back",
    )(oidx, qkv, qkv, qkv, probs, dmixed, first)


def third_blocks(t):
    return [part * OB + t * PT + p for part in range(3) for p in range(PT)]


def input_kernel(whole_w, d0, d1, d2, start, dmid, par, *rest):
    out, sums, w, sems = rest

    @pl.when(pl.program_id(0) == 0)
    def _():
        copy = pltpu.make_async_copy(whole_w, w, sems.at[0])
        copy.start()
        sums[...] = jnp.zeros_like(sums)
        copy.wait()

    d = None
    for n, dproj in enumerate((d0, d1, d2)):
        t = mm(dproj[...], columns(w, 0, QH, RB, third_blocks(n)), NT)
        d = t if d is None else d + t
    xhat, r = normalised(start[...])
    sums[0:1, :] += jnp.sum(d * xhat, axis=0, keepdims=True)
    sums[1:2, :] += jnp.sum(d, axis=0, keepdims=True)
    out[...] = (dmid[...].astype(f32) + norm_back(xhat, r, par[0:1, :D], d)).astype(bf16)


def input_call(w, dprojs, start, dmid, par):
    rows = start.shape[0]
    B = row_block(rows)
    blk = pl.BlockSpec((B, D), lambda i: (i, 0))
    return pl.pallas_call(
        input_kernel,
        grid=(rows // B,),
        in_specs=[ANY, blk, blk, blk, blk, blk, whole(par.shape)],
        out_specs=[blk, whole((8, D))],
        out_shape=[jax.ShapeDtypeStruct((rows, D), bf16), jax.ShapeDtypeStruct((8, D), f32)],
        scratch_shapes=[
            pltpu.VMEM((4, NF, QH, LANE), bf16),
            pltpu.SemaphoreType.DMA((1,)),
        ],
        compiler_params=params(),
        cost_estimate=COST,
        name="input_back",
    )(w, *dprojs, start, dmid, par)


SEGMENTS = ("g1", "b1", "ob", "g2", "b2", "rb")
BASE = (0, 6, 30, 36, 42, 48)
BASE_Q, BASE_V, BASE_E, VROWS = 12, 24, 56, 80
TURNS = ((0, 0), (1, 0), (1, 1), (2, 0), (2, 1), (3, 0))


def small_maps(f_of):
    col = lax.broadcasted_iota(jnp.int32, (VROWS, NF * SM), 1)
    row = lax.broadcasted_iota(jnp.int32, (VROWS, NF * SM), 0)
    slot, i = col // SM, col % SM
    f = jnp.zeros_like(col)
    for n in range(NF):
        f = jnp.where(slot == n, f_of[n], f)
    seg = f
    base = jnp.full_like(col, -VROWS)
    for n, b in enumerate(BASE):
        base = jnp.where(i == n, b, base)
    for n in (6, 7):
        s = 2 * f + (n - 6)
        late = s >= NF
        base = jnp.where(i == n, jnp.where(late, BASE_V, BASE_Q), base)
        seg = jnp.where(i == n, jnp.where(late, s - NF, s), seg)
    at = base + 3 * seg // 4
    lane_in = lax.broadcasted_iota(jnp.int32, (LANE, LANE), 0)
    lane_out = lax.broadcasted_iota(jnp.int32, (LANE, LANE), 1)
    maps = []
    for m, second in TURNS:
        pick = jnp.where((row == at + second) & (seg % 4 == m), 1.0, 0.0).astype(bf16)
        shift = 96 * m % LANE - LANE * second
        lanes = jnp.where((lane_in < RB) & (lane_out == lane_in + shift), 1.0, 0.0).astype(bf16)
        maps.append((pick, lanes))
    whole_row = BASE_E + (i - 8) * NF + f
    pick = jnp.where((row == whole_row) & (i >= 8) & (i < 8 + CH), 1.0, 0.0).astype(bf16)
    maps.append((pick, jnp.where(lane_in == lane_out, 1.0, 0.0).astype(bf16)))
    return maps


PAR_ROWS = ((0, 0, 6), (1, 6, 6), (2, 12, 18), (3, 30, 6), (4, 36, 6), (5, 42, 6), (7, 48, 6), (8, 56, 8), (9, 64, 8), (10, 72, 8))


def par_kernel(row, idx, one, two, par, small, sems):
    copies = [
        pltpu.make_async_copy(v.at[pl.ds(0, 4), pl.ds(row, SM)], small.at[pl.ds(4 * n, 4)], sems.at[n])
        for n, v in enumerate((one, two))
    ]
    for c in copies:
        c.start()
    for c in copies:
        c.wait()
    source = small[...].reshape(NF * SM, LANE)
    flat = jnp.zeros((VROWS, LANE), f32)
    for pick, lanes in small_maps([idx[n] for n in range(NF)]):
        flat += mm(mm(pick, source, NN).astype(bf16), lanes, NN)
    par[...] = jnp.zeros_like(par)
    for r, start, n in PAR_ROWS:
        for i in range(n):
            par[r : r + 1, i * LANE : (i + 1) * LANE] = flat[start + i : start + i + 1, :]


def par_call(idx, one, two, row):
    return pl.pallas_call(
        functools.partial(par_kernel, row),
        in_specs=[SMEM, ANY, ANY],
        out_shape=jax.ShapeDtypeStruct((16, FF), f32),
        scratch_shapes=[pltpu.VMEM((NF, SM, LANE), bf16), pltpu.SemaphoreType.DMA((2,))],
        compiler_params=params(),
        cost_estimate=COST,
        name="small_params",
    )(idx, one, two)


def small_grad_kernel(idx, seed_sum, h0, h1, h2, bsums, t0, t1, t2, isums, out, flat):
    flat[...] = jnp.zeros_like(flat)

    def place(start, value):
        for i in range(value.shape[1] // LANE):
            flat[start + i : start + i + 1, :] = value[:, i * LANE : (i + 1) * LANE]

    place(0, isums[0:1, :])
    place(6, isums[1:2, :])
    for t, v in enumerate((t0, t1, t2)):
        place(BASE_Q + PT * t, v[0:1, :WT])
        place(BASE_V + PT * t, v[0:1, 2 * WT :])
    place(30, bsums[2:3, :])
    place(36, bsums[0:1, :])
    place(42, bsums[1:2, :])
    place(48, seed_sum[...])
    for j, h in enumerate((h0, h1, h2)):
        place(BASE_E + j * NF, h[...])
    source = flat[...].astype(bf16)
    total = jnp.zeros((NF * SM, LANE), f32)
    for pick, lanes in small_maps([idx[n] for n in range(NF)]):
        total += mm(mm(pick, source, TN).astype(bf16), lanes, NT)
    out[...] = total.astype(bf16).reshape(NF, SM, LANE)


def small_grad_call(idx, *sums):
    return pl.pallas_call(
        small_grad_kernel,
        in_specs=[SMEM] + [whole(v.shape) for v in sums],
        out_shape=jax.ShapeDtypeStruct((NF, SM, LANE), bf16),
        scratch_shapes=[pltpu.VMEM((VROWS, LANE), f32)],
        compiler_params=params(),
        cost_estimate=COST,
        name="small_grads",
    )(idx, *sums)


def finish_mlp_kernel(idx, *rest):
    bufs = rest[:4]
    ew, rw, w, sems = rest[4:]
    copies = [pltpu.make_async_copy(b, w.at[idx[n]], sems.at[n]) for n, b in enumerate(bufs)]
    for c in copies:
        c.start()
    for c in copies:
        c.wait()

    def rows(j, q, r, n):
        if j == 0:
            return w[q, r : r + n, :].astype(f32)
        r += (2 * j - 1 + q % 2) * QM
        return w[q - q % 2, r : r + n, :].astype(f32) + w[q - q % 2 + 1, r : r + n, :].astype(f32)

    for j in range(CH):
        for b in range(EB):
            ew[:, (CH * b + j) * LANE : (CH * b + j + 1) * LANE] = rows(j, b // 4, b % 4 * RB, RB)
        for b in range(OB):
            rw[j * LANE : (j + 1) * LANE, b * LANE : (b + 1) * LANE] = rows(j, 2 + b // 3, b % 3 * LANE, LANE)


def finish_mlp_call(idx, bufs):
    return pl.pallas_call(
        finish_mlp_kernel,
        in_specs=[SMEM] + [ANY] * 4,
        out_shape=[jax.ShapeDtypeStruct((RB, FF), f32), jax.ShapeDtypeStruct((FB, D), f32)],
        scratch_shapes=[pltpu.VMEM((4,) + bufs[0].shape, bf16), pltpu.SemaphoreType.DMA((4,))],
        compiler_params=params(),
        cost_estimate=COST,
        name="finish_mlp",
    )(idx, *bufs)


def unpack_blocks(out, w, base, targets):
    for b, target in enumerate(targets):
        q, off = divmod(b * RB, QO)
        cols = slice(target * LANE, (target + 1) * LANE)
        head = min(RB, QO - off)
        out[:head, cols] = w[q, base + off : base + off + head, :].astype(f32)
        if head < RB:
            out[head:, cols] = w[q + 1, base : base + RB - head, :].astype(f32)


def finish_heads_kernel(idx, *rest):
    bufs = rest[:4]
    hw, ow, g1, b1, ob, g2, b2, rb, hb, eb, w, line, sems = rest[4:]
    copies = [pltpu.make_async_copy(b, w.at[idx[n]], sems.at[n]) for n, b in enumerate(bufs)]
    for c in copies:
        c.start()
    for c in copies:
        c.wait()
    unpack_blocks(ow, w, 0, range(OB))
    for t in range(THIRDS):
        unpack_blocks(hw, w, (1 + t) * QO, third_blocks(t))
    small = w[0, (1 + THIRDS) * QO :, :].astype(f32)
    for n, o in enumerate((g1, b1, ob, g2, b2, rb)):
        o[...] = small[n : n + 1, :RB]
    for n in range(2):
        line[:, n * RB : (n + 1) * RB] = small[6 + n : 7 + n, :RB]
    hb[...] = line[...].reshape(2 * RB)
    eb[...] = jnp.concatenate([small[8 + n : 9 + n, :] for n in range(CH)], axis=1).reshape(FB)


def finish_heads_call(idx, bufs):
    vec = jax.ShapeDtypeStruct((1, RB), f32)
    return pl.pallas_call(
        finish_heads_kernel,
        in_specs=[SMEM] + [ANY] * 4,
        out_shape=[jax.ShapeDtypeStruct((RB, 3 * D), f32), jax.ShapeDtypeStruct((RB, D), f32)]
        + [vec] * 6
        + [jax.ShapeDtypeStruct((2 * RB,), f32), jax.ShapeDtypeStruct((FB,), f32)],
        scratch_shapes=[
            pltpu.VMEM((4,) + bufs[0].shape, bf16),
            pltpu.VMEM((1, 2 * RB), f32),
            pltpu.SemaphoreType.DMA((4,)),
        ],
        compiler_params=params(),
        cost_estimate=COST,
        name="finish_heads",
    )(idx, *bufs)


def pieces_of(ref, start, n):
    parts = []
    while n:
        b, r = divmod(start, RB)
        take = min(n, RB - r)
        parts.append(ref[r : r + take, b * LANE : (b + 1) * LANE])
        start, n = start + take, n - take
    return parts


def put(out, row, parts):
    for p in parts:
        out[row : row + p.shape[0], :] = p
        row += p.shape[0]
    return row


def prepare_kernel(me, ew, rw, ow, near, far):
    def quarter(j, q):
        if q < 2:
            return [ew[:, (CH * b + j) * LANE : (CH * b + j + 1) * LANE] for b in range(4 * q, 4 * q + 4)]
        blocks = range(3 * (q - 2), 3 * (q - 2) + 3)
        return [rw[j * LANE : (j + 1) * LANE, b * LANE : (b + 1) * LANE] for b in blocks]

    for q in range(4):

        @pl.when(me[0] == q)
        def _(q=q):
            row = 0
            for p in (q - q % 2, q - q % 2 + 1):
                row = put(near, row, pieces_of(ow, p * QO, QO))
                row = put(near, row, quarter(0, p))
            put(near, row, quarter(1, q))
            row = 0
            for p in (q - q % 2, q - q % 2 + 1):
                row = put(far, row, quarter(2, p))


def prepare_heads_kernel(me, hw, g1, b1, ob, g2, b2, rb, hb, eb, heads, small):
    small[...] = jnp.zeros_like(small)
    for n, v in enumerate((g1, b1, ob, g2, b2, rb)):
        small[n : n + 1, :RB] = v[...].astype(f32)
    for n in range(2):
        small[6 + n : 7 + n, :RB] = hb[...].astype(f32).reshape(1, 2 * RB)[:, n * RB : (n + 1) * RB]
    for n in range(CH):
        small[8 + n : 9 + n, :] = eb[...].astype(f32).reshape(1, FB)[:, n * LANE : (n + 1) * LANE]


    for q in range(4):

        @pl.when(me[0] == q)
        def _(q=q):
            row = put(heads, 0, pieces_of(hw, q * QH, QH))
            heads[row:, :] = small[...].astype(bf16)


def prepare_call(q, *arrays):
    rows = 2 * (QO + QM) + QM, 2 * QM
    return pl.pallas_call(
        prepare_kernel,
        in_specs=[SMEM] + [whole(v.shape) for v in arrays],
        out_shape=[jax.ShapeDtypeStruct((n, LANE), bf16) for n in rows],
        compiler_params=params(),
        cost_estimate=COST,
        name="prepare",
    )(q, *arrays)


def prepare_heads_call(q, *arrays):
    return pl.pallas_call(
        prepare_heads_kernel,
        in_specs=[SMEM] + [whole(v.shape) for v in arrays],
        out_shape=jax.ShapeDtypeStruct((QH + SM, LANE), bf16),
        scratch_shapes=[pltpu.VMEM((SM, LANE), f32)],
        compiler_params=params(),
        cost_estimate=COST,
        name="prepare_heads",
    )(q, *arrays)


def merge_kernel(counts, *refs):
    inputs, outs = refs[: sum(counts)], refs[sum(counts) :]
    per = outs[0].shape[0]
    for i, out in enumerate(outs):

        at = row = 0
        for n in counts:
            terms = inputs[at : at + n]
            mine = slice(i * per, (i + 1) * per)
            total = terms[0][mine].astype(f32)
            for t in terms[1:]:
                total += t[mine].astype(f32)
            rows = terms[0].shape[1]
            out[:, row : row + rows, :] = total.astype(bf16)
            at += n
            row += rows


def merge_call(parts, pieces):
    slots = parts[0][0].shape[0]
    rows = sum(p[0].shape[1] for p in parts)
    flat = [v for p in parts for v in p]
    out = jax.ShapeDtypeStruct((slots // pieces, rows, LANE), bf16)
    return pl.pallas_call(
        functools.partial(merge_kernel, tuple(len(p) for p in parts)),
        out_shape=[out] * pieces,
        compiler_params=params(),
        cost_estimate=COST,
        name="merge",
    )(*flat)


def block_major(a):
    return a.reshape(a.shape[0], -1, LANE).transpose(1, 0, 2).reshape(-1, LANE)


def from_block_major(a, rows):
    return a.reshape(-1, rows, LANE).transpose(1, 0, 2).reshape(rows, -1)


def small_rows(g1, b1, hb, ob, g2, b2, eb, rb):
    return jnp.concatenate([v.reshape(NF, -1) for v in (g1, b1, hb, ob, g2, b2, eb, rb)], axis=1)


SMALL = (("g1", RB), ("b1", RB), ("hb", 2 * RB), ("ob", RB), ("g2", RB), ("b2", RB), ("eb", FB), ("rb", RB))


def split_small(sm):
    out, at = {}, 0
    for name, width in SMALL:
        out[name] = sm[:, at : at + width]
        at += width
    return out


def par_of(sm):
    s = {k: v.astype(f32) for k, v in split_small(sm).items()}
    hb = s["hb"].reshape(2 * D)
    zero = jnp.zeros((D,), f32)
    eb = s["eb"].reshape(NF, CH, LANE).transpose(1, 0, 2).reshape(CH, CW)

    def wide(v):
        return jnp.pad(v, (0, FF - v.shape[0]))

    rows = [
        s["g1"].reshape(D),
        s["b1"].reshape(D),
        jnp.concatenate([hb[:D], zero, hb[D:]]),
        s["ob"].reshape(D),
        s["g2"].reshape(D),
        s["b2"].reshape(D),
        zero,
        s["rb"].reshape(D),
        eb[0],
        eb[1],
        eb[2],
    ]
    rows += [zero] * 5
    return jnp.stack([wide(r) for r in rows])


def small_grads(seed_sum, hsums, bsums, hbsum, isums):
    eb = jnp.stack([h[0] for h in hsums]).reshape(CH, NF, LANE).transpose(1, 0, 2).reshape(FF)
    hb = jnp.concatenate([hbsum[0, :D], hbsum[0, 2 * D :]])
    return small_rows(isums[0], isums[1], hb, bsums[2], bsums[0], bsums[1], eb, seed_sum[0])


def chain(counts, ids, patches, upstream, table, hooks):
    n = patches.shape[0]
    start, xhat, seed, seed_sum = start_call(counts, table, ids.reshape(n, 1, SLOTS), patches, upstream)
    xhat = hooks.opened(xhat)
    hw, par = hooks.heads()
    xhat = hooks.at("attend", xhat)
    first, qkv, probs, mixed, whole_w = attend_call(counts, hw, xhat, par, 0, n, PER)
    mixed = hooks.at("middle", mixed)
    ow = hooks.out()
    hsums, res, dsec = [], None, None
    for j in range(CH):
        if j:
            second = hooks.at("m%d" % j, second)
            values, weights = (second, seed, res, dsec), [hooks.mlp(j)]
        else:
            values, weights = (mixed, start, seed), [hooks.mlp(0), ow]
        done = mlp_call(j, weights, hooks.order("m%d" % j), values, par)
        if j == 0:
            middle, second, *done = done
        res, dsec, hs, *pieces = done
        hsums.append(hs)
        hooks.last = hs
        hooks.grads("m%d" % j, pieces)
    dsec = hooks.at("branch", dsec)
    dmid, dmixed, bsums, *pieces = branch_call(ow, hooks.order("o"), middle, dsec, seed, mixed, par)
    hooks.grads("o", pieces)
    dprojs, tsums = [], []
    for t in range(THIRDS):
        dmixed = hooks.at("h%d" % t, dmixed)
        dproj, tsum, *pieces = attend_back_call(t, hooks.order("h%d" % t), qkv, probs, dmixed, first)
        dprojs.append(dproj)
        tsums.append(tsum)
        hooks.grads("h%d" % t, pieces)
    dmid = hooks.at("input", dmid)
    pgrad, isums = input_call(whole_w, dprojs, start, dmid, par)
    grads = hooks.finish(seed_sum, *hsums, bsums, *tsums, isums)
    return res.reshape(n, SLOTS, D), pgrad.reshape(n, SLOTS, D), grads


class Plain:
    def __init__(self, args):
        self.full = {k: lax.all_gather(v, "fsdp", axis=0, tiled=True) for k, v in args.items()}
        self.idx = jnp.arange(4 * NF, dtype=jnp.int32)
        self.got = {}

    def order(self, name):
        return self.idx, NF

    def pieces(self, a, quarter):
        plan = tuple((q, 0, 0, quarter) for q in range(4))
        return self.idx, [a[:, q * quarter : (q + 1) * quarter] for q in range(4)], plan

    def at(self, name, value):
        return value

    def opened(self, xhat):
        return xhat

    def heads(self):
        f = self.full
        sm = small_rows(*(f[k] for k, _ in SMALL))
        w = jax.vmap(block_major)(f["hw"].reshape(NF, RB, 3 * D))
        return self.pieces(w, QH), par_of(sm)

    def out(self):
        return self.pieces(jax.vmap(block_major)(self.full["ow"].reshape(NF, RB, D)), QO)

    def mlp(self, j):
        e = self.full["ew"].reshape(NF, RB, NF, CH, LANE)[:, :, :, j].transpose(0, 2, 1, 3)
        r = self.full["rw"].reshape(NF, CH, LANE, OB, LANE)[:, j].transpose(0, 2, 1, 3)
        w = jnp.concatenate([e.reshape(NF, -1, LANE), r.reshape(NF, -1, LANE)], axis=1)
        return self.pieces(w, QM)

    def grads(self, name, pieces):
        self.got[name] = jnp.concatenate(pieces, axis=1)

    def finish(self, seed_sum, h0, h1, h2, bsums, t0, t1, t2, isums):
        hbsum = jnp.concatenate([t[:, p * WT : (p + 1) * WT] for p in range(3) for t in (t0, t1, t2)], axis=1)
        smalls = small_grads(seed_sum, (h0, h1, h2), bsums, hbsum, isums)
        g = self.got
        hs = jnp.stack([g["h%d" % t].reshape(NF, 3, PT, RB, LANE) for t in range(THIRDS)])
        hw = hs.transpose(1, 4, 2, 0, 3, 5).reshape(D, 3 * D)
        ow = jax.vmap(lambda a: from_block_major(a, RB))(g["o"]).reshape(D, D)
        e = jnp.stack([g["m%d" % j][:, : EB * RB].reshape(NF, NF, RB, LANE) for j in range(CH)])
        ew = e.transpose(1, 3, 2, 0, 4).reshape(D, FF)
        r = jnp.stack([g["m%d" % j][:, EB * RB :].reshape(NF, OB, LANE, LANE) for j in range(CH)])
        rw = r.transpose(1, 0, 3, 2, 4).reshape(FF, D)
        s = {k: v.reshape(-1) for k, v in split_small(smalls).items()}
        s.update(hw=hw, ow=ow, ew=ew, rw=rw)

        def total(v):
            part = lax.psum_scatter(v.astype(bf16), "fsdp", scatter_dimension=0, tiled=True)
            return lax.psum(part, "rep").astype(f32)

        return {k: total(v) for k, v in s.items()}


NR = 4


def moves(dy, dc, dz, dx):
    pairs = []
    for rep in range(NR):
        for f in range(NF):
            to = (rep // 2 ^ dy) * 2 + (rep % 2 ^ dc)
            at = (f // 2 ^ dz) * 2 + (f % 2 ^ dx)
            pairs.append((rep * NF + f, to * NF + at))
    return pairs


def send(a, dy=0, dc=0, dz=0, dx=0):
    return lax.ppermute(a, ("rep", "fsdp"), moves(dy, dc, dz, dx))


def to_core(a):
    return send(a, dc=1)


def together(*values):
    return lax.optimization_barrier(values)


HS = (QH + SM) // 2
NS = QO + 112


def gathered(a):
    return lax.all_gather(a[None], "fsdp", axis=0, tiled=True)


class Fast:
    def __init__(self, args):
        rep, f = lax.axis_index("rep"), lax.axis_index("fsdp")
        self.y, self.c, self.z, self.x = rep // 2, rep % 2, f // 2, f % 2
        q = 2 * self.c + self.y
        self.g, self.moves = {}, {}
        self.quarters = jnp.stack([q, q ^ 1, q ^ 2, q ^ 3]).astype(jnp.int32)
        me = q.astype(jnp.int32).reshape(1)
        hw = prepare_heads_call(
            me, args["hw"], *(args[k].reshape(1, -1) for k in SEGMENTS), args["hb"], args["eb"]
        )
        hw, ow = together(hw, args["ow"])
        near, far = prepare_call(me, args["ew"], args["rw"], ow)
        self.near, self.far = gathered(near), gathered(far)
        self.hz = [hw] + [send(hw, dz=k) for k in (1, 2, 3)]

    def halves(self, pieces, row):
        return jnp.stack([v[:row] for v in pieces]), jnp.stack([v[row:] for v in pieces])

    def round_one(self, a, b):
        return jnp.concatenate([a, send(a, dx=1)], axis=0), jnp.concatenate([b, send(b, dy=1)], axis=0)

    def round_two(self, a, b):
        return send(a, dy=1), send(b, dx=1)

    def opened(self, xhat):
        xhat, *hz = together(xhat, *self.hz)
        a, b = self.round_one(*self.halves(hz, HS))
        a2, b2 = self.round_two(a, b)
        self.h = [a, a2, b, b2] + [to_core(v) for v in (a, a2, b, b2)]
        return xhat

    def places(self, order):
        place = []
        for dc in range(2):
            for i in range(2):
                for j in range(2):
                    d = dict(zip(order, (i, j)))
                    for dz in range(4):
                        q = 2 * (self.c ^ dc) + (self.y ^ d["y"])
                        place.append(q * NF + (self.z ^ dz) * 2 + (self.x ^ d["x"]))
        return jnp.stack(place).astype(jnp.int32)

    def heads(self):
        a, b, n = self.places("yx"), self.places("xy"), 2 * NF
        idx = jnp.concatenate([a[:n], b[:n], a[n:], b[n:]])
        one, two = (0, 0, HS), (0, HS, QH - HS)
        plan = tuple((n,) + (one if n % 4 < 2 else two) for n in range(8))
        at = jnp.concatenate([b[:4], b[8:12]]) % NF
        par = par_call(at, self.h[2], self.h[3], QH - HS)
        return (idx, self.h, plan), par

    def at(self, name, value):
        g = self.g
        if name == "middle":
            value, near = together(value, self.near)
            self.near = [near, to_core(near)]
            self.c1 = send(near[:, 2 * (QO + QM) :], dy=1)
        if name == "m1":
            self.last, c1 = together(self.last, self.c1)
            self.c1 = [c1, to_core(c1)]
        if name == "m2":
            self.last, far = together(self.last, self.far)
            self.far = [far, to_core(far)]
            value = self.hold(value, self.added("m0"))
            self.y0 = send(g["m0"][1], dy=1)
        if name == "branch":
            parts = [g["m0"][0] + self.y0, *self.added("m1", keep=True), *self.added("m2", keep=True)]
            value, parts = together(value, jnp.concatenate(parts, axis=1))
            self.m = lax.psum_scatter(parts, "fsdp", scatter_dimension=0, tiled=True)[0]
        if name == "h2":
            g["near"] = merge_call([g["o"], g["h0"]], 2)
            value = self.hold(value, "near")
            self.xn = send(g["near"][1], dx=1)
        if name == "input":
            far = merge_call([g["h1"], g["h2"]], 4)
            near = g["near"][0]
            near = [near[:4] + self.xn[:4], near[4:] + self.xn[4:]]
            value, *both = together(value, *near, *far)
            self.near = [both[0], send(both[1], dy=1)]
            self.far = self.across_back(both[2:])
        return value

    def hold(self, value, *names):
        flat = [v for name in names for v in self.g[name]]
        value, *flat = together(value, *flat)
        for name in names:
            n = len(self.g[name])
            self.g[name], flat = flat[:n], flat[n:]
        return value

    def across_back(self, a):
        return [a[0], send(a[1], dx=1), send(a[2], dy=1), send(a[3], dx=1, dy=1)]

    def spread_z(self, c):
        return [c[0]] + [send(c[k], dz=k) for k in (1, 2, 3)]

    def added(self, name, keep=False):
        a, b = self.g[name]
        n = a.shape[0] // 2
        parts = [a[:n] + b[:n], a[n:] + b[n:]]
        if keep:
            return parts
        self.g[name] = parts
        return name

    def even_places(self):
        q = 2 * (self.c ^ jnp.arange(2)[:, None, None]) + jnp.arange(2)[:, None]
        return (q * NF + jnp.arange(NF)).reshape(-1).astype(jnp.int32)

    def plan(self, rows, row, n):
        return self.even_places(), tuple((dc, y * rows + row, 0, n) for dc in range(2) for y in range(2))

    def out(self):
        idx, plan = self.plan(QO + QM, 0, QO)
        self.w = self.near
        return idx, self.w, plan

    def mlp(self, j):
        if j == 2:
            idx, plan = self.plan(QM, 0, QM)
            return idx, self.far, plan
        if j == 0:
            idx, plan = self.plan(QO + QM, QO, QM)
            return idx, self.w, plan
        side, row = jnp.arange(2)[:, None, None], 2 * (QO + QM)
        q = 2 * (self.c ^ side) + (self.y ^ side.reshape(2, 1))
        idx = (q * NF + jnp.arange(NF)).reshape(-1).astype(jnp.int32)
        return idx, [self.w[0], self.c1[0], self.w[1], self.c1[1]], ((0, row, 0, QM), (1, 0, 0, QM), (2, row, 0, QM), (3, 0, 0, QM))

    def order(self, name):
        if name[0] == "m":
            side = jnp.arange(2)[:, None]
            q = 2 * (self.c ^ jnp.arange(2)[:, None, None]) + (self.y ^ side if name == "m0" else side)
            return (q * NF + jnp.arange(NF)).reshape(-1).astype(jnp.int32), 2 * NF
        return self.places("xy" if name in ("o", "h0") else "yx"), 2 * NF

    def grads(self, name, pieces):
        keep, go = pieces
        if name == "m2":
            go, self.y0 = together(go, self.y0)
        if name == "h2":
            go, self.xn = together(go, self.xn)
        self.g[name] = [keep, to_core(go)]

    def whole_shard(self, own):
        across = send(own, dy=1)
        return [own, across, to_core(own), to_core(across)]

    def finish(self, *sums):
        sums = list(sums)
        *self.far, self.near[1], sums[-1] = together(*self.far, self.near[1], sums[-1])
        s = small_grad_call(self.places("yx")[:8] % NF, *sums)
        s = merge_call([[s, to_core(s)]], 2)
        s = self.across_back([s[0], s[1], s[0], s[1]])
        last = self.spread_z(merge_call([self.near, self.far, s], 4))
        m, last[0] = together(self.m, last[0])
        across = send(m, dy=1)
        last, m, across = together(merge_call([last], 1)[0][0], m, across)
        ew, rw = finish_mlp_call(self.quarters, [m, across, to_core(m), to_core(across)])
        over = send(last, dy=1)
        last = [last, over, to_core(last), to_core(over)]
        hw, ow, g1, b1, ob, g2, b2, rb, hb, eb = finish_heads_call(self.quarters, last)
        out = dict(hw=hw, ow=ow, ew=ew, rw=rw)
        out.update(g1=g1, b1=b1, hb=hb, ob=ob, g2=g2, b2=b2, eb=eb, rb=rb)
        return {k: v if k[1] == "w" else v.reshape(-1) for k, v in out.items()}


NAMES = ("g1", "b1", "hw", "hb", "ow", "ob", "g2", "b2", "ew", "eb", "rw", "rb")


def body(fast, patches, visible_count, patch_index, *rest):
    args = dict(zip(NAMES, rest[:12]))
    upstream = rest[12]
    hooks = (Fast if fast else Plain)(args)
    out, pgrad, g = chain(visible_count, patch_index, patches, upstream, frequency_table(), hooks)
    return (out, pgrad) + tuple(g[k] for k in NAMES)


def solution(mesh):
    rows = P(("rep", "fsdp"), None, None)
    mat, vec = P("fsdp", None), P("fsdp")
    weights = tuple(mat if k[1] == "w" else vec for k in NAMES)
    fast = mesh.shape["fsdp"] == NF and mesh.shape["rep"] == 4
    return jax.shard_map(
        functools.partial(body, fast),
        mesh=mesh,
        in_specs=(rows, P(("rep", "fsdp")), P(("rep", "fsdp"), None)) + weights + (rows,),
        out_specs=(rows, rows) + weights,
        check_vma=False,
    )
```
